128 devices in a mesh: gx: 8 (over y, core), gy: 16 (over x, z).
Axes of the slice: x: 4, y: 4, z: 4, core: 2. Of those that a mesh axis runs over, the one named last changes fastest.
Arguments:
- rhs: float32 [8, 2, 1024, 2048], P(None, None, 'gy', 'gx'), may hold values from -16.5 to 16.5
- metric: float32 [1024], replicated, may hold values from 0.5 to 2
- wavenumber: float32 [8], replicated, may hold values from 2e-05 to 0.002
Outputs:
- pressure: float32 [8, 2, 1024, 2048], P(None, None, 'gy', 'gx')
The draws below stay inside these ranges and needn't reach their ends.
All inputs are finite; a program needn't handle non-finite values.
Results may differ from the reference program's by a relative error of at most 0.0009.
Values sent between devices are 32-bit elements; how exact they have to be, the bound alone decides.
No kernel may reach another device: no remote copies, remote signals or barrier semaphores. Data moves between devices by JAX's collectives and lax.ppermute only.
A program may use at most 64 MiB of HBM per device.

```python
import math
import jax
import jax.numpy as jnp
from jax import lax

NX = 2048
NY = 1024
MODES = 8


def second_differences(field):
    padded = jnp.pad(field, ((0, 0), (0, 0), (1, 1), (0, 0)))
    across = padded[:, :, 2:] + padded[:, :, :-2] - 2.0 * field
    along = jnp.roll(field, 1, 3) + jnp.roll(field, -1, 3) - 2.0 * field
    return -across - 0.02 * along


def draw_rhs(key, part):
    key = jax.random.fold_in(key, 7)
    shape = (MODES, 2, NY, NX)
    field_key, noise_key = jax.random.split(key, 2)
    field = jax.random.truncated_normal(field_key, -4.0, 4.0, shape, jnp.float32)
    noise = jax.random.truncated_normal(noise_key, -4.0, 4.0, shape, jnp.float32)
    values = second_differences(field) + 0.01 * noise
    return values.astype(jnp.float32)


def setup_inputs(seed: int = 0) -> dict:
    arg_keys = jax.random.split(jax.random.key(seed), 4)
    rhs = draw_rhs(jax.random.fold_in(arg_keys[3], 71), 0)
    metric = jnp.clip(jnp.exp(jax.random.uniform(arg_keys[1], (NY,), jnp.float32, math.log(0.5), math.log(2.0))), 0.5, 2.0)
    wavenumber = jnp.clip(jnp.exp(jax.random.uniform(arg_keys[2], (MODES,), jnp.float32, math.log(1.9999999494757503e-05), math.log(0.002))), 1.9999999494757503e-05, 0.002)
    return dict(rhs=rhs, metric=metric, wavenumber=wavenumber)


def reference(rhs, metric, wavenumber):
    field = rhs[:, 0] + 1j * rhs[:, 1]
    spectrum = jnp.fft.fft(field, axis=-1)
    wave_index = jnp.arange(NX, dtype=jnp.int32).astype(jnp.float32)
    along = 0.02 * (2.0 * jnp.sin(jnp.pi * wave_index / NX)) ** 2
    shift = wavenumber[:, None] + along[None, :]

    def solve_mode(pair):
        spec_real, spec_imag, shift_row = pair
        lower = jnp.broadcast_to(-metric[None, :], (NX, NY))
        lower = lower.at[:, 0].set(0.0)
        upper = jnp.broadcast_to(-metric[None, :], (NX, NY))
        upper = upper.at[:, NY - 1].set(0.0)
        center = 2.0 * metric[None, :] + shift_row[:, None]
        columns = jnp.stack([spec_real.T, spec_imag.T], -1)
        solved = lax.linalg.tridiagonal_solve(lower, center, upper, columns)
        return (solved[..., 0].T, solved[..., 1].T)
    solved_real, solved_imag = lax.map(solve_mode, (spectrum.real, spectrum.imag, shift))
    physical = jnp.fft.ifft(solved_real + 1j * solved_imag, axis=-1)
    return jnp.stack([physical.real, physical.imag], 1).astype(jnp.float32)
```

```python
import functools
import math

import jax
import jax.numpy as jnp
import numpy as np
from jax import lax
from jax.experimental import pallas as pl
from jax.experimental.pallas import tpu as pltpu
from jax.sharding import PartitionSpec as P


ASPECT = 0.02
STRIPS = 8
COLS = 256
ROWS = 64
BANDS = 16
NX = STRIPS * COLS
VMEM_LIMIT = 48 * 1024 * 1024
F32 = jnp.float32


def f32(values):
    return np.asarray(values, np.float32)


def sine_table():
    ramp = np.arange(COLS)
    table = np.sin(np.pi * (np.outer(ramp, ramp) % (2 * COLS)) / COLS) * math.sqrt(2.0 / COLS)
    table[0, :] = 0.0
    table[:, 0] = 0.0
    table[0, 0] = 1.0
    return f32(table)


def edge_table():
    ramp = np.arange(COLS)
    left = np.sin(np.pi * ramp / COLS) * math.sqrt(2.0 / COLS)
    right = left * np.where(ramp % 2 == 1, 1.0, -1.0)
    left[0] = right[0] = 0.0
    along = 4.0 * np.sin(np.pi * ramp / (2 * COLS)) ** 2
    rows = [ASPECT * left, ASPECT * right, ASPECT * along]
    return f32(np.stack([np.broadcast_to(r, (8, COLS)) for r in rows]))


def dft_table():
    ramp = np.arange(COLS)
    angle = 2.0 * np.pi * (np.outer(ramp, ramp) % COLS) / COLS
    return f32(np.concatenate([np.cos(angle), np.sin(angle)], 1))


def wave_table():
    kappa = np.arange(STRIPS)[:, None]
    j = np.arange(COLS)[None, :]
    angle = 2.0 * np.pi * j * kappa / NX
    along = ASPECT * (2.0 * np.sin(np.pi * (STRIPS * j + kappa) / NX)) ** 2
    return f32(np.stack([np.cos(angle), np.sin(angle), along]))


def octet_forward():
    ramp = np.arange(STRIPS)
    angle = 2.0 * np.pi * np.outer(ramp, ramp) / STRIPS
    c, s = np.cos(angle), np.sin(angle)
    return f32(np.block([[c, s], [-s, c]]))


def octet_inverse():
    ramp = np.arange(STRIPS)
    parts = []
    for offset in (0, 1):
        angle = 2.0 * np.pi * np.outer(ramp + offset, ramp) / STRIPS
        c, s = np.cos(angle), np.sin(angle)
        parts.append(np.block([[c, -s], [s, c]]))
    return f32(np.concatenate(parts, 0) / NX)


def dot(a, b):
    return jnp.dot(a, b, precision=lax.Precision.HIGHEST, preferred_element_type=F32)


def lane_ids():
    return lax.broadcasted_iota(jnp.int32, (8, 128), 1)


def wide(column):
    return jnp.broadcast_to(column, (8, 128))


def row_sum(values):
    return wide(jnp.sum(values[:, :128] + values[:, 128:], axis=1, keepdims=True))


def splat_inverse(metric_ref, index):
    return 1.0 / jnp.full((8, COLS), metric_ref[index], F32)


def local_kernel(rhs_ref, metric_ref, wave_ref, sine_ref, edge_ref, solved_ref, ratio_ref, send_ref, z_ref, f_lo, f_hi):
    first = lax.axis_index("gy") * ROWS
    sine = sine_ref[...]
    lanes = lane_ids()
    sub = lax.broadcasted_iota(jnp.int32, (8, COLS), 0)
    shift = edge_ref[2]
    for mode in range(8):
        shift = shift + jnp.where(sub == mode, wave_ref[mode], 0.0)
    height = jnp.ones((8, COLS), F32)
    slope = jnp.ones((8, COLS), F32)
    state = [jnp.zeros((8, COLS), F32)] * 2
    for mode in range(8):
        block = slice(mode * 2 * ROWS, (mode + 1) * 2 * ROWS)
        lines = dot(rhs_ref[block, :], sine)
        f_lo[block, :] = lines[:, :128]
        f_hi[block, :] = lines[:, 128:]
    for y in range(1, ROWS):
        inverse = splat_inverse(metric_ref, first + y)
        slope = slope + shift * inverse * height
        taller = height + slope
        ratio = height / taller
        height = taller
        ratio_ref[y] = ratio
        for c in range(2):
            rows = pl.ds(c * ROWS + y, 8, stride=2 * ROWS)
            line = jnp.concatenate([f_lo[rows, :], f_hi[rows, :]], 1)
            state[c] = (line * inverse + state[c]) * ratio
            z_ref[y, c] = state[c]
    left = edge_ref[0]
    right = edge_ref[1]
    columns = [[jnp.zeros((8, 128), F32)] * 2 for _ in range(2)]
    upper = [jnp.zeros((8, COLS), F32)] * 2
    for y in range(ROWS - 1, 0, -1):
        ratio = ratio_ref[y]
        inverse = splat_inverse(metric_ref, first + y)
        for c in range(2):
            upper[c] = z_ref[y, c] + ratio * upper[c]
            solved_ref[y, c] = upper[c]
            scaled = upper[c] * inverse
            a = scaled * left
            a = a[:, :128] + a[:, 128:] + jnp.where(
                lanes == 0, f_lo[pl.ds(c * ROWS + y, 8, stride=2 * ROWS), :] * inverse[:, :128], 0.0
            )
            b = scaled * right
            b = b[:, :128] + b[:, 128:]
            columns[0][c] = jnp.where(lanes == y, wide(jnp.sum(a, axis=1, keepdims=True)), columns[0][c])
            columns[1][c] = jnp.where(lanes == y + ROWS, wide(jnp.sum(b, axis=1, keepdims=True)), columns[1][c])
    edges = jnp.concatenate([solved_ref[y, c] for y in (1, ROWS - 1) for c in range(2)], 0)
    edges = dot(edges, sine)
    zero_lane = lax.broadcasted_iota(jnp.int32, (8, COLS), 1) == 0
    inverse = splat_inverse(metric_ref, first)
    for c in range(2):
        near = jnp.where(zero_lane, 0.0, edges[c * 8 : c * 8 + 8])
        row = [rhs_ref[(mode * 2 + c) * ROWS : (mode * 2 + c) * ROWS + 1, :] for mode in range(8)]
        near = near + jnp.concatenate(row, 0) * inverse
        far = jnp.where(zero_lane, 0.0, edges[16 + c * 8 : 24 + c * 8])
        for half in range(2):
            part = slice(half * 128, half * 128 + 128)
            send_ref[pl.ds(c * 2 + half, 8, stride=16), :] = near[:, part]
            send_ref[pl.ds(4 + c * 2 + half, 8, stride=16), :] = far[:, part]
        send_ref[pl.ds(8 + c, 8, stride=16), :] = jnp.where(lanes < ROWS, columns[0][c], columns[1][c])
        for pad in range(3):
            send_ref[pl.ds(10 + c * 3 + pad, 8, stride=16), :] = jnp.zeros((8, 128), F32)


def factor_kernel(metric_ref, inverse_ref, wave_ref, table_ref, alpha_ref, beta_ref, ratio_ref, pivot_ref, carry_ref):
    mine = lax.axis_index("gy")
    shift = table_ref[2] + wave_ref[lax.axis_index("gx")]

    def excess(row):
        double = 2.0 * metric_ref[row]
        return ((double + shift) - double) * inverse_ref[row]

    one = jnp.ones((8, COLS), F32)
    zero = jnp.zeros((8, COLS), F32)
    together = 4

    def bands(outer, carry):
        gamma_below, excess_below, flow = carry
        state = [(one, zero, zero, zero)] * together

        def rows(y, state):
            out = []
            for i in range(together):
                height, slope, rest, rise = state[i]
                t = excess((outer * together + i) * ROWS + y)
                slope = slope + t * height
                height = height + (slope + 1.0)
                rise = rise + t * (rest + 1.0)
                rest = rest + rise
                out.append((height, slope, rest, rise))
            return tuple(out)

        state = lax.fori_loop(1, ROWS, rows, tuple(state), unroll=7)
        for i in range(together):
            height, slope, rest, _ = state[i]
            band = outer * together + i
            gamma = 1.0 / height
            x = excess(band * ROWS) + rest * gamma + excess_below + flow
            pivot = 1.0 / (gamma + x)
            forward = gamma * pivot
            pivot_ref[band] = pivot
            carry_ref[band] = forward
            excess_below = slope * gamma
            flow = forward * x
            gamma_below = gamma
        return gamma_below, excess_below, flow

    lax.fori_loop(0, BANDS // together, bands, (one, zero, one))

    height, slope = one, one
    for y in range(1, ROWS):
        beta_ref[y] = height
        slope = slope + excess(mine * ROWS + y) * height
        taller = height + slope
        ratio_ref[y] = height / taller
        height = taller
    gamma = 1.0 / height
    height, slope = one, one
    for y in range(ROWS - 1, 0, -1):
        alpha_ref[y] = height * gamma
        beta_ref[y] = beta_ref[y] * gamma
        slope = slope + excess(mine * ROWS + y) * height
        height = height + slope


def spectrum_kernel(recv_ref, alpha_ref, beta_ref, dft_ref, table_ref, octet_ref, send_ref, column_ref):
    def take(i):
        return recv_ref[pl.ds(i, 8, stride=16), :]

    pieces = [[], []]
    for c in range(2):
        for i in range(2):
            pieces[c].append(take(c * 2 + i))
        for i in range(2):
            pieces[c].append(take(4 + c * 2 + i))
        column = take(8 + c)
        pieces[c].append(column + pltpu.roll(pltpu.roll(column, 1, 0), ROWS, 1))
    stacked = jnp.concatenate([jnp.concatenate(pieces[0], 1), jnp.concatenate(pieces[1], 1)], 0)
    mixed = dot(octet_ref[...], stacked)
    cos, sin = table_ref[0], table_ref[1]
    turned = [[], []]
    for line in range(2):
        re = mixed[:8, line * COLS : line * COLS + COLS]
        im = mixed[8:, line * COLS : line * COLS + COLS]
        turned[0].append(re * cos + im * sin)
        turned[1].append(im * cos - re * sin)
    both = dot(jnp.concatenate(turned[0] + turned[1], 0), dft_ref[...])
    columns = [mixed[c * 8 : c * 8 + 8, 2 * COLS :] for c in range(2)]
    near = [jnp.zeros((8, COLS), F32)] * 2
    far = [jnp.zeros((8, COLS), F32)] * 2
    for y in range(1, ROWS):
        alpha, beta = alpha_ref[y], beta_ref[y]
        for c in range(2):
            source = wide(columns[c][:, y : y + 1])
            source = jnp.concatenate([source, source], 1)
            near[c] = near[c] + alpha * source
            far[c] = far[c] + beta * source
    for line, extra in enumerate((near, far)):
        re_cos = both[line * 8 : line * 8 + 8, :COLS]
        re_sin = both[line * 8 : line * 8 + 8, COLS:]
        im_cos = both[16 + line * 8 : 24 + line * 8, :COLS]
        im_sin = both[16 + line * 8 : 24 + line * 8, COLS:]
        send_ref[line * 2] = re_cos + im_sin + extra[0]
        send_ref[line * 2 + 1] = im_cos - re_sin + extra[1]
    for c in range(2):
        column_ref[c] = columns[c]


def column_kernel(column_ref, ratio_ref, sum_ref, z_ref):
    lanes = lane_ids()
    columns = [column_ref[c] for c in range(2)]
    state = [jnp.zeros((8, COLS), F32)] * 2
    for y in range(1, ROWS):
        ratio = ratio_ref[y]
        for c in range(2):
            source = wide(columns[c][:, y : y + 1])
            state[c] = (jnp.concatenate([source, source], 1) + state[c]) * ratio
            z_ref[y, c] = state[c]
    upper = [jnp.zeros((8, COLS), F32)] * 2
    total = [jnp.zeros((8, 128), F32)] * 2
    for y in range(ROWS - 1, 0, -1):
        ratio = ratio_ref[y]
        for c in range(2):
            upper[c] = z_ref[y, c] + ratio * upper[c]
            total[c] = jnp.where(lanes == y, row_sum(upper[c]), total[c])
    for c in range(2):
        sum_ref[c] = total[c]


def separator_kernel(
    q0, q1, q2, q3, alpha_ref, beta_ref, pivot_ref, carry_ref, sum_ref, dft_ref, table_ref, octet_ref, send_ref, b_ref, v_ref
):
    mine = lax.axis_index("gy")
    px, pz = mine // 4, mine % 4
    for sx, q in enumerate((q0, q1, q2, q3)):
        for sz in range(4):
            b_ref[((px + 4 - sx) % 4) * 4 + (pz + 4 - sz) % 4] = q[sz]
    state = [jnp.zeros((8, COLS), F32)] * 2
    for band in range(BANDS):
        for c in range(2):
            value = b_ref[band, c]
            if band:
                value = value + b_ref[band - 1, 2 + c] + carry_ref[band - 1] * state[c]
            state[c] = value
            v_ref[band, c] = value * pivot_ref[band]
    value = [jnp.zeros((8, COLS), F32)] * 2
    for c in range(2):
        v_ref[BANDS, c] = value[c]
    for band in range(BANDS - 1, -1, -1):
        for c in range(2):
            value[c] = v_ref[band, c] + carry_ref[band] * value[c]
            v_ref[band, c] = value[c]
    near = [v_ref[mine, c] for c in range(2)]
    far = [v_ref[mine + 1, c] for c in range(2)]
    lanes = lane_ids()
    both = dot(jnp.concatenate([near[0], far[0], near[1], far[1]], 0), dft_ref[...])
    total = [sum_ref[c] for c in range(2)]
    for y in range(1, ROWS):
        alpha, beta = alpha_ref[y], beta_ref[y]
        for c in range(2):
            extra = row_sum(alpha * near[c] + beta * far[c])
            total[c] = total[c] + jnp.where(lanes == y, extra, 0.0)
    cos, sin = table_ref[0], table_ref[1]
    turned = [[], []]
    for line in range(2):
        re_cos = both[line * 8 : line * 8 + 8, :COLS]
        re_sin = both[line * 8 : line * 8 + 8, COLS:]
        im_cos = both[16 + line * 8 : 24 + line * 8, :COLS]
        im_sin = both[16 + line * 8 : 24 + line * 8, COLS:]
        re = re_cos - im_sin
        im = re_sin + im_cos
        turned[0].append(re * cos - im * sin)
        turned[1].append(re * sin + im * cos)
    stacked = [jnp.concatenate(turned[c] + [total[c]], 1) for c in range(2)]
    out = dot(octet_ref[...], jnp.concatenate(stacked, 0))
    for c in range(2):
        for i in range(4):
            row = (i // 2) * 4 + c * 2 + i % 2
            send_ref[pl.ds(row, 8, stride=16), :] = out[c * 8 : c * 8 + 8, i * 128 : i * 128 + 128]
        here = out[c * 8 : c * 8 + 8, 2 * COLS :]
        there = out[16 + c * 8 : 24 + c * 8, 2 * COLS :]
        send_ref[pl.ds(8 + c, 8, stride=16), :] = jnp.where(lanes < ROWS, here, pltpu.roll(there, ROWS, 1))
        for pad in range(3):
            send_ref[pl.ds(10 + c * 3 + pad, 8, stride=16), :] = jnp.zeros((8, 128), F32)


def finish_kernel(recv_ref, solved_ref, ratio_ref, metric_ref, sine_ref, edge_ref, out_ref, z_ref, u_lo, u_hi):
    first = lax.axis_index("gy") * ROWS

    def take(i):
        return recv_ref[pl.ds(i, 8, stride=16), :]

    sine = sine_ref[...]
    near = [jnp.concatenate([take(c * 2), take(c * 2 + 1)], 1) for c in range(2)]
    far = [jnp.concatenate([take(4 + c * 2), take(5 + c * 2)], 1) for c in range(2)]
    columns = [take(8 + c) for c in range(2)]
    edges = dot(jnp.concatenate(near + far, 0), sine)
    left, right = edge_ref[0], edge_ref[1]
    zero_lane = lax.broadcasted_iota(jnp.int32, (8, COLS), 1) == 0
    state = [edges[c * 8 : c * 8 + 8] for c in range(2)]
    for y in range(1, ROWS):
        ratio = ratio_ref[y]
        inverse = splat_inverse(metric_ref, first + y)
        a, b = left * inverse, right * inverse
        for c in range(2):
            here = wide(columns[c][:, y : y + 1])
            there = wide(columns[c][:, ROWS + y : ROWS + y + 1])
            here = jnp.concatenate([here, here], 1)
            there = jnp.concatenate([there, there], 1)
            state[c] = (state[c] + a * here + b * there) * ratio
            z_ref[y, c] = state[c]
    upper = [edges[16 + c * 8 : 24 + c * 8] for c in range(2)]
    for y in range(ROWS - 1, -1, -1):
        for c in range(2):
            if y:
                upper[c] = z_ref[y, c] + ratio_ref[y] * upper[c]
                here = wide(columns[c][:, y : y + 1])
                here = jnp.concatenate([here, here], 1)
                line = jnp.where(zero_lane, here, upper[c] + solved_ref[y, c])
            else:
                line = edges[c * 8 : c * 8 + 8]
            rows = pl.ds(c * ROWS + y, 8, stride=2 * ROWS)
            u_lo[rows, :] = line[:, :128]
            u_hi[rows, :] = line[:, 128:]
    for mode in range(8):
        block = slice(mode * 2 * ROWS, (mode + 1) * 2 * ROWS)
        out_ref[block, :] = dot(jnp.concatenate([u_lo[block, :], u_hi[block, :]], 1), sine)


def call(kernel, outs, scratch, *operands, scalars=()):
    vmem = pl.BlockSpec(memory_space=pltpu.VMEM)
    smem = pl.BlockSpec(memory_space=pltpu.SMEM)
    shapes = [jax.ShapeDtypeStruct(s, F32) for s in outs]
    return pl.pallas_call(
        kernel,
        out_shape=shapes,
        in_specs=[smem if i in scalars else vmem for i in range(len(operands))],
        out_specs=[vmem] * len(shapes),
        scratch_shapes=[pltpu.VMEM(s, F32) for s in scratch],
        compiler_params=pltpu.CompilerParams(vmem_limit_bytes=VMEM_LIMIT),
    )(*operands)


def gather_bands(piece):
    def along(values, near):
        return [values] + [
            lax.ppermute(values, "gy", [(a, near(a, s)) for a in range(BANDS)]) for s in range(1, 4)
        ]

    line = jnp.stack(along(piece, lambda a, s: a // 4 * 4 + (a + s) % 4))
    return along(line, lambda a, s: (a + 4 * s) % BANDS)


def per_device(rhs, metric, wavenumber):
    sine, edge = jnp.asarray(sine_table()), jnp.asarray(edge_table())
    dft, table = jnp.asarray(dft_table()), jnp.asarray(wave_table())
    full = (ROWS, 8, COLS)
    solved, local_ratio, send = call(
        local_kernel,
        [(ROWS, 2, 8, COLS), full, (128, 128)],
        [(ROWS, 2, 8, COLS), (1024, 128), (1024, 128)],
        rhs.reshape(1024, COLS), metric, wavenumber, sine, edge,
        scalars=(1, 2),
    )
    recv = lax.all_to_all(send.reshape(8, 16, 128), "gx", 0, 0, tiled=True)
    alpha, beta, ratio, pivot, carry = call(
        factor_kernel,
        [full, full, full, (BANDS, 8, COLS), (BANDS, 8, COLS)],
        [],
        metric, 1.0 / metric, wavenumber, table,
        scalars=(0, 1, 2),
    )
    piece, column = call(
        spectrum_kernel,
        [(4, 8, COLS), (2, 8, 128)],
        [],
        recv.reshape(128, 128), alpha, beta, dft, table, jnp.asarray(octet_forward()),
    )
    pieces = gather_bands(piece)
    (total,) = call(column_kernel, [(2, 8, 128)], [(ROWS, 2, 8, COLS)], column, ratio)
    (send,) = call(
        separator_kernel,
        [(128, 128)],
        [(BANDS, 4, 8, COLS), (BANDS + 1, 2, 8, COLS)],
        *pieces, alpha, beta, pivot, carry, total, dft, table, jnp.asarray(octet_inverse()),
    )
    recv = lax.all_to_all(send.reshape(8, 16, 128), "gx", 0, 0, tiled=True)
    (out,) = call(
        finish_kernel,
        [(1024, COLS)],
        [(ROWS, 2, 8, COLS), (1024, 128), (1024, 128)],
        recv.reshape(128, 128), solved, local_ratio, metric, sine, edge,
        scalars=(3,),
    )
    return out.reshape(8, 2, ROWS, COLS)


def solution(mesh):
    placed = (P(None, None, "gy", "gx"), P(), P())
    return jax.shard_map(
        per_device, mesh=mesh, in_specs=placed, out_specs=P(None, None, "gy", "gx"), check_vma=False
    )
```

```python
import functools
import math

import jax
import jax.numpy as jnp
import numpy as np
from jax import lax
from jax.experimental import pallas as pl
from jax.experimental.pallas import tpu as pltpu
from jax.sharding import PartitionSpec as P


ASPECT = 0.02
STRIPS = 8
COLS = 256
ROWS = 64
BANDS = 16
NX = STRIPS * COLS
VMEM_LIMIT = 16 * 1024 * 1024
F32 = jnp.float32


def f32(values):
    return np.asarray(values, np.float32)


def sine_table():
    ramp = np.arange(COLS)
    table = np.sin(np.pi * (np.outer(ramp, ramp) % (2 * COLS)) / COLS) * math.sqrt(2.0 / COLS)
    table[0, :] = 0.0
    table[:, 0] = 0.0
    table[0, 0] = 1.0
    return f32(table)


def edge_table():
    ramp = np.arange(COLS)
    left = np.sin(np.pi * ramp / COLS) * math.sqrt(2.0 / COLS)
    right = left * np.where(ramp % 2 == 1, 1.0, -1.0)
    left[0] = right[0] = 0.0
    along = 4.0 * np.sin(np.pi * ramp / (2 * COLS)) ** 2
    rows = [ASPECT * left, ASPECT * right, ASPECT * along]
    return f32(np.stack([np.broadcast_to(r, (8, COLS)) for r in rows]))


def dft_table():
    ramp = np.arange(COLS)
    angle = 2.0 * np.pi * (np.outer(ramp, ramp) % COLS) / COLS
    return f32(np.concatenate([np.cos(angle), np.sin(angle)], 1))


def wave_table():
    kappa = np.arange(STRIPS)[:, None]
    j = np.arange(COLS)[None, :]
    angle = 2.0 * np.pi * j * kappa / NX
    along = ASPECT * (2.0 * np.sin(np.pi * (STRIPS * j + kappa) / NX)) ** 2
    return f32(np.stack([np.cos(angle), np.sin(angle), along]))


def octet_forward():
    ramp = np.arange(STRIPS)
    angle = 2.0 * np.pi * np.outer(ramp, ramp) / STRIPS
    c, s = np.cos(angle), np.sin(angle)
    return f32(np.block([[c, s], [-s, c]]))


def octet_inverse():
    ramp = np.arange(STRIPS)
    parts = []
    for offset in (0, 1):
        angle = 2.0 * np.pi * np.outer(ramp + offset, ramp) / STRIPS
        c, s = np.cos(angle), np.sin(angle)
        parts.append(np.block([[c, -s], [s, c]]))
    return f32(np.concatenate(parts, 0) / NX)


def dot(a, b):
    return jnp.dot(a, b, precision=lax.Precision.HIGHEST, preferred_element_type=F32)


def lane_ids():
    return lax.broadcasted_iota(jnp.int32, (8, 128), 1)


def wide(column):
    return jnp.broadcast_to(column, (8, 128))


def row_sum(values):
    return wide(jnp.sum(values[:, :128] + values[:, 128:], axis=1, keepdims=True))


def splat_inverse(metric_ref, index):
    return 1.0 / jnp.full((8, COLS), metric_ref[index], F32)


def local_shift(wave_ref, edge_ref):
    sub = lax.broadcasted_iota(jnp.int32, (8, COLS), 0)
    shift = edge_ref[2]
    for mode in range(8):
        shift = shift + jnp.where(sub == mode, wave_ref[mode], 0.0)
    return shift


def local_kernel(
    rhs_hbm, metric_hbm, wave_hbm, sine_hbm, edge_hbm, solved_hbm, send_ref,
    ratio_ref, z_ref, f_lo, f_hi, rhs_ref, sine_ref, edge_ref, metric_ref, wave_ref, rhs_sem, sems, out_sem,
):
    first = lax.axis_index("gy") * ROWS
    small = [
        pltpu.make_async_copy(a, b, sems.at[i])
        for i, (a, b) in enumerate(
            ((sine_hbm, sine_ref), (metric_hbm, metric_ref), (wave_hbm, wave_ref), (edge_hbm, edge_ref))
        )
    ]
    blocks = [pl.ds(mode * 2 * ROWS, 2 * ROWS) for mode in range(8)]
    large = [pltpu.make_async_copy(rhs_hbm.at[b], rhs_ref.at[b], rhs_sem.at[i]) for i, b in enumerate(blocks)]
    small[0].start()
    for copy in large[:2] + small[1:] + large[2:]:
        copy.start()
    small[0].wait()
    sine = sine_ref[...]
    for mode in range(8):
        large[mode].wait()
        lines = dot(rhs_ref[blocks[mode], :], sine)
        f_lo[blocks[mode], :] = lines[:, :128]
        f_hi[blocks[mode], :] = lines[:, 128:]
    for copy in small[1:]:
        copy.wait()
    lanes = lane_ids()
    shift = local_shift(wave_ref, edge_ref)
    height = jnp.ones((8, COLS), F32)
    slope = jnp.ones((8, COLS), F32)
    state = [jnp.zeros((8, COLS), F32)] * 2
    for y in range(1, ROWS):
        inverse = splat_inverse(metric_ref, first + y)
        slope = slope + shift * inverse * height
        taller = height + slope
        ratio = height / taller
        height = taller
        ratio_ref[y] = ratio
        for c in range(2):
            rows = pl.ds(c * ROWS + y, 8, stride=2 * ROWS)
            line = jnp.concatenate([f_lo[rows, :], f_hi[rows, :]], 1)
            state[c] = (line * inverse + state[c]) * ratio
            z_ref[y, c] = state[c]
    left = edge_ref[0]
    right = edge_ref[1]
    columns = [[jnp.zeros((8, 128), F32)] * 2 for _ in range(2)]
    upper = [jnp.zeros((8, COLS), F32)] * 2
    done = []
    for y in range(ROWS - 1, 0, -1):
        ratio = ratio_ref[y]
        inverse = splat_inverse(metric_ref, first + y)
        for c in range(2):
            upper[c] = z_ref[y, c] + ratio * upper[c]
            z_ref[y, c] = upper[c]
            scaled = upper[c] * inverse
            a = scaled * left
            a = a[:, :128] + a[:, 128:] + jnp.where(
                lanes == 0, f_lo[pl.ds(c * ROWS + y, 8, stride=2 * ROWS), :] * inverse[:, :128], 0.0
            )
            b = scaled * right
            b = b[:, :128] + b[:, 128:]
            columns[0][c] = jnp.where(lanes == y, wide(jnp.sum(a, axis=1, keepdims=True)), columns[0][c])
            columns[1][c] = jnp.where(lanes == y + ROWS, wide(jnp.sum(b, axis=1, keepdims=True)), columns[1][c])
        if y % 16 == 0:
            done.append(pltpu.make_async_copy(z_ref.at[pl.ds(y, 16)], solved_hbm.at[pl.ds(y, 16)], out_sem.at[y // 16]))
            done[-1].start()
    z_ref[0] = jnp.zeros((2, 8, COLS), F32)
    done.append(pltpu.make_async_copy(z_ref.at[pl.ds(0, 16)], solved_hbm.at[pl.ds(0, 16)], out_sem.at[0]))
    done[-1].start()
    edges = jnp.concatenate([z_ref[y, c] for y in (1, ROWS - 1) for c in range(2)], 0)
    edges = dot(edges, sine)
    zero_lane = lax.broadcasted_iota(jnp.int32, (8, COLS), 1) == 0
    inverse = splat_inverse(metric_ref, first)
    for c in range(2):
        near = jnp.where(zero_lane, 0.0, edges[c * 8 : c * 8 + 8])
        row = [rhs_ref[(mode * 2 + c) * ROWS : (mode * 2 + c) * ROWS + 1, :] for mode in range(8)]
        near = near + jnp.concatenate(row, 0) * inverse
        far = jnp.where(zero_lane, 0.0, edges[16 + c * 8 : 24 + c * 8])
        for half in range(2):
            part = slice(half * 128, half * 128 + 128)
            send_ref[pl.ds(c * 2 + half, 8, stride=16), :] = near[:, part]
            send_ref[pl.ds(4 + c * 2 + half, 8, stride=16), :] = far[:, part]
        send_ref[pl.ds(8 + c, 8, stride=16), :] = jnp.where(lanes < ROWS, columns[0][c], columns[1][c])
        for pad in range(3):
            send_ref[pl.ds(10 + c * 3 + pad, 8, stride=16), :] = jnp.zeros((8, 128), F32)
    for copy in done:
        copy.wait()


def factors(ref):
    sizes = (ROWS, ROWS, ROWS, BANDS, BANDS, 3)
    starts = np.cumsum((0,) + sizes)
    return [ref.at[pl.ds(int(a), n)] for a, n in zip(starts, sizes)]


def factor_kernel(
    metric_ref, inverse_ref, wave_ref, table_ref, factor_ref, gamma_ref, base_ref, x_ref
):
    alpha_ref, beta_ref, ratio_ref, up_ref, down_ref, final_ref = factors(factor_ref)
    mine = lax.axis_index("gy")
    shift = table_ref[2] + wave_ref[lax.axis_index("gx")]

    def excess(row):
        double = 2.0 * metric_ref[row]
        return ((double + shift) - double) * inverse_ref[row]

    one = jnp.ones((8, COLS), F32)
    zero = jnp.zeros((8, COLS), F32)
    together = 4

    def bands(outer, carry):
        excess_below, flow = carry
        state = [(one, zero, zero, zero)] * together

        def rows(y, state):
            out = []
            for i in range(together):
                height, slope, rest, rise = state[i]
                t = excess((outer * together + i) * ROWS + y)
                slope = slope + t * height
                height = height + (slope + 1.0)
                rise = rise + t * (rest + 1.0)
                rest = rest + rise
                out.append((height, slope, rest, rise))
            return tuple(out)

        state = lax.fori_loop(1, ROWS, rows, tuple(state), unroll=7)
        for i in range(together):
            height, slope, rest, _ = state[i]
            band = outer * together + i
            gamma = 1.0 / height
            base = excess(band * ROWS) + rest * gamma + excess_below
            x = base + flow
            up = gamma / (gamma + x)
            gamma_ref[band] = gamma
            base_ref[band] = base
            x_ref[band] = x
            up_ref[band] = up
            excess_below = slope * gamma
            flow = up * x
        return excess_below, flow

    lax.fori_loop(0, BANDS // together, bands, (zero, one))

    above, down, inverse = one, zero, zero
    for band in range(BANDS - 1, -1, -1):
        gamma = gamma_ref[band]
        down_ref[band] = down

        @pl.when(band == mine)
        def _(above=above, down=down, inverse=inverse, gamma=gamma):
            final_ref[0] = down
            final_ref[1] = inverse
            final_ref[2] = 1.0 / (x_ref[mine] + gamma * above)

        if band:
            x = base_ref[band] + gamma * above
            below = gamma_ref[band - 1]
            inverse = 1.0 / (below + x)
            down = below * inverse
            above = x * inverse

    height, slope = one, one
    for y in range(1, ROWS):
        beta_ref[y] = height
        slope = slope + excess(mine * ROWS + y) * height
        taller = height + slope
        ratio_ref[y] = height / taller
        height = taller
    gamma = 1.0 / height
    height, slope = one, one
    for y in range(ROWS - 1, 0, -1):
        alpha_ref[y] = height * gamma
        beta_ref[y] = beta_ref[y] * gamma
        slope = slope + excess(mine * ROWS + y) * height
        height = height + slope


def spectrum_kernel(
    recv_ref, factor_ref, dft_ref, table_ref, octet_ref, send_hbm, own_ref, column_ref, send_ref, sem
):
    alpha_ref, beta_ref, _, up_ref, down_ref, _ = factors(factor_ref)
    mine = lax.axis_index("gy")

    def take(i):
        return recv_ref[pl.ds(i, 8, stride=16), :]

    pieces = [[], []]
    for c in range(2):
        for i in range(2):
            pieces[c].append(take(c * 2 + i))
        for i in range(2):
            pieces[c].append(take(4 + c * 2 + i))
        column = take(8 + c)
        pieces[c].append(column + pltpu.roll(pltpu.roll(column, 1, 0), ROWS, 1))
    stacked = jnp.concatenate([jnp.concatenate(pieces[0], 1), jnp.concatenate(pieces[1], 1)], 0)
    mixed = dot(octet_ref[...], stacked)
    cos, sin = table_ref[0], table_ref[1]
    turned = [[], []]
    for line in range(2):
        re = mixed[:8, line * COLS : line * COLS + COLS]
        im = mixed[8:, line * COLS : line * COLS + COLS]
        turned[0].append(re * cos + im * sin)
        turned[1].append(im * cos - re * sin)
    both = dot(jnp.concatenate(turned[0] + turned[1], 0), dft_ref[...])
    columns = [mixed[c * 8 : c * 8 + 8, 2 * COLS :] for c in range(2)]
    near = [jnp.zeros((8, COLS), F32)] * 2
    far = [jnp.zeros((8, COLS), F32)] * 2
    for y in range(1, ROWS):
        alpha, beta = alpha_ref[y], beta_ref[y]
        for c in range(2):
            source = wide(columns[c][:, y : y + 1])
            source = jnp.concatenate([source, source], 1)
            near[c] = near[c] + alpha * source
            far[c] = far[c] + beta * source
    sides = []
    for line, extra in enumerate((near, far)):
        re_cos = both[line * 8 : line * 8 + 8, :COLS]
        re_sin = both[line * 8 : line * 8 + 8, COLS:]
        im_cos = both[16 + line * 8 : 24 + line * 8, :COLS]
        im_sin = both[16 + line * 8 : 24 + line * 8, COLS:]
        sides.append((re_cos + im_sin + extra[0], im_cos - re_sin + extra[1]))
    for c in range(2):
        own_ref[c], own_ref[2 + c] = sides[0][c], sides[1][c]
        column_ref[c] = columns[c]
        send_ref[mine, c] = jnp.zeros((8, COLS), F32)

    def copy(band):
        return pltpu.make_async_copy(send_ref.at[band], send_hbm.at[band], sem.at[band])

    copy(mine).start()
    up, down = up_ref[mine], down_ref[mine]

    def above(band, carry):
        factor = up_ref[band]
        for c in range(2):
            send_ref[band, c] = carry[c]
        copy(band).start()
        return tuple(value * factor for value in carry)

    def below(step, carry):
        band = mine - 1 - step
        factor = down_ref[band]
        for c in range(2):
            send_ref[band, c] = carry[c]
        copy(band).start()
        return tuple(value * factor for value in carry)

    lax.fori_loop(mine + 1, BANDS, above, tuple(sides[1][c] + up * sides[0][c] for c in range(2)))
    lax.fori_loop(0, mine, below, tuple(sides[0][c] + down * sides[1][c] for c in range(2)))
    for band in range(BANDS):
        copy(band).wait()


def column_kernel(column_ref, factor_ref, metric_ref, wave_ref, edge_ref, sum_ref, local_ref, z_ref):
    ratio_ref = factors(factor_ref)[2]
    first = lax.axis_index("gy") * ROWS
    shift = local_shift(wave_ref, edge_ref)
    height = jnp.ones((8, COLS), F32)
    slope = jnp.ones((8, COLS), F32)
    for y in range(1, ROWS):
        slope = slope + shift * splat_inverse(metric_ref, first + y) * height
        taller = height + slope
        local_ref[y] = height / taller
        height = taller
    lanes = lane_ids()
    columns = [column_ref[c] for c in range(2)]
    state = [jnp.zeros((8, COLS), F32)] * 2
    for y in range(1, ROWS):
        ratio = ratio_ref[y]
        for c in range(2):
            source = wide(columns[c][:, y : y + 1])
            state[c] = (jnp.concatenate([source, source], 1) + state[c]) * ratio
            z_ref[y, c] = state[c]
    upper = [jnp.zeros((8, COLS), F32)] * 2
    total = [jnp.zeros((8, 128), F32)] * 2
    for y in range(ROWS - 1, 0, -1):
        ratio = ratio_ref[y]
        for c in range(2):
            upper[c] = z_ref[y, c] + ratio * upper[c]
            total[c] = jnp.where(lanes == y, row_sum(upper[c]), total[c])
    for c in range(2):
        sum_ref[c] = total[c]


def separator_kernel(
    recv_ref, own_ref, factor_ref, sum_ref, dft_ref, table_ref, octet_ref, send_ref
):
    alpha_ref, beta_ref, _, _, _, final_ref = factors(factor_ref)
    mine = lax.axis_index("gy")
    from_below = [own_ref[c] for c in range(2)]
    from_above = [own_ref[2 + c] for c in range(2)]
    for band in range(BANDS):
        for c in range(2):
            value = recv_ref[band, c]
            from_below[c] = from_below[c] + jnp.where(band < mine, value, 0.0)
            from_above[c] = from_above[c] + jnp.where(band > mine, value, 0.0)
    down, inverse, pivot = final_ref[0], final_ref[1], final_ref[2]
    near = [(from_below[c] + down * from_above[c]) * pivot for c in range(2)]
    far = [from_above[c] * inverse + down * near[c] for c in range(2)]
    lanes = lane_ids()
    both = dot(jnp.concatenate([near[0], far[0], near[1], far[1]], 0), dft_ref[...])
    total = [sum_ref[c] for c in range(2)]
    for y in range(1, ROWS):
        alpha, beta = alpha_ref[y], beta_ref[y]
        for c in range(2):
            extra = row_sum(alpha * near[c] + beta * far[c])
            total[c] = total[c] + jnp.where(lanes == y, extra, 0.0)
    cos, sin = table_ref[0], table_ref[1]
    turned = [[], []]
    for line in range(2):
        re_cos = both[line * 8 : line * 8 + 8, :COLS]
        re_sin = both[line * 8 : line * 8 + 8, COLS:]
        im_cos = both[16 + line * 8 : 24 + line * 8, :COLS]
        im_sin = both[16 + line * 8 : 24 + line * 8, COLS:]
        re = re_cos - im_sin
        im = re_sin + im_cos
        turned[0].append(re * cos - im * sin)
        turned[1].append(re * sin + im * cos)
    stacked = [jnp.concatenate(turned[c] + [total[c]], 1) for c in range(2)]
    out = dot(octet_ref[...], jnp.concatenate(stacked, 0))
    for c in range(2):
        for i in range(4):
            row = (i // 2) * 4 + c * 2 + i % 2
            send_ref[pl.ds(row, 8, stride=16), :] = out[c * 8 : c * 8 + 8, i * 128 : i * 128 + 128]
        here = out[c * 8 : c * 8 + 8, 2 * COLS :]
        there = out[16 + c * 8 : 24 + c * 8, 2 * COLS :]
        send_ref[pl.ds(8 + c, 8, stride=16), :] = jnp.where(lanes < ROWS, here, pltpu.roll(there, ROWS, 1))
        for pad in range(3):
            send_ref[pl.ds(10 + c * 3 + pad, 8, stride=16), :] = jnp.zeros((8, 128), F32)


def finish_kernel(recv_ref, solved_ref, ratio_ref, metric_ref, sine_ref, edge_ref, out_ref, z_ref, u_lo, u_hi):
    first = lax.axis_index("gy") * ROWS

    def take(i):
        return recv_ref[pl.ds(i, 8, stride=16), :]

    sine = sine_ref[...]
    near = [jnp.concatenate([take(c * 2), take(c * 2 + 1)], 1) for c in range(2)]
    far = [jnp.concatenate([take(4 + c * 2), take(5 + c * 2)], 1) for c in range(2)]
    columns = [take(8 + c) for c in range(2)]
    edges = dot(jnp.concatenate(near + far, 0), sine)
    left, right = edge_ref[0], edge_ref[1]
    zero_lane = lax.broadcasted_iota(jnp.int32, (8, COLS), 1) == 0
    state = [edges[c * 8 : c * 8 + 8] for c in range(2)]
    for y in range(1, ROWS):
        ratio = ratio_ref[y]
        inverse = splat_inverse(metric_ref, first + y)
        a, b = left * inverse, right * inverse
        for c in range(2):
            here = wide(columns[c][:, y : y + 1])
            there = wide(columns[c][:, ROWS + y : ROWS + y + 1])
            here = jnp.concatenate([here, here], 1)
            there = jnp.concatenate([there, there], 1)
            state[c] = (state[c] + a * here + b * there) * ratio
            z_ref[y, c] = state[c]
    upper = [edges[16 + c * 8 : 24 + c * 8] for c in range(2)]
    for y in range(ROWS - 1, -1, -1):
        for c in range(2):
            if y:
                upper[c] = z_ref[y, c] + ratio_ref[y] * upper[c]
                here = wide(columns[c][:, y : y + 1])
                here = jnp.concatenate([here, here], 1)
                line = jnp.where(zero_lane, here, upper[c] + solved_ref[y, c])
            else:
                line = edges[c * 8 : c * 8 + 8]
            rows = pl.ds(c * ROWS + y, 8, stride=2 * ROWS)
            u_lo[rows, :] = line[:, :128]
            u_hi[rows, :] = line[:, 128:]
    for mode in range(8):
        block = slice(mode * 2 * ROWS, (mode + 1) * 2 * ROWS)
        out_ref[block, :] = dot(jnp.concatenate([u_lo[block, :], u_hi[block, :]], 1), sine)


def call(kernel, outs, scratch, *operands, scalars=(), far=(), manual=(), space=pltpu.VMEM):
    smem = pl.BlockSpec(memory_space=pltpu.SMEM)
    specs = [smem if i in scalars else pl.BlockSpec(memory_space=space) for i in range(len(operands))]
    if space == pltpu.HBM:
        operands = [pltpu.with_memory_space_constraint(a, space) for a in operands]
    return pl.pallas_call(
        kernel,
        out_shape=[(pltpu.HBM if i in far else pltpu.VMEM)(s, F32) for i, s in enumerate(outs)],
        in_specs=specs,
        out_specs=[pl.BlockSpec(memory_space=pltpu.HBM if i in manual else pltpu.VMEM) for i in range(len(outs))],
        scratch_shapes=[pltpu.VMEM(s, F32) if isinstance(s, tuple) else s for s in scratch],
        compiler_params=pltpu.CompilerParams(vmem_limit_bytes=VMEM_LIMIT),
    )(*operands)


def per_device(rhs, metric, wavenumber):
    sine, edge = jnp.asarray(sine_table()), jnp.asarray(edge_table())
    dft, table = jnp.asarray(dft_table()), jnp.asarray(wave_table())
    full, lines, half = (ROWS, 8, COLS), (ROWS, 2, 8, COLS), (1024, 128)
    solved, send = call(
        local_kernel,
        [lines, (128, 128)],
        [
            full, lines, half, half, (1024, COLS), (COLS, COLS), (3, 8, COLS),
            pltpu.SMEM((1024,), F32), pltpu.SMEM((8,), F32),
            pltpu.SemaphoreType.DMA((8,)), pltpu.SemaphoreType.DMA((4,)), pltpu.SemaphoreType.DMA((4,)),
        ],
        rhs.reshape(1024, COLS), metric, wavenumber, sine, edge,
        space=pltpu.HBM, far=(0, 1), manual=(0,),
    )
    recv = lax.all_to_all(send.reshape(8, 16, 128), "gx", 0, 0, tiled=True)
    bands = (BANDS, 8, COLS)
    (factor,) = call(
        factor_kernel,
        [(3 * ROWS + 2 * BANDS + 3, 8, COLS)],
        [bands, bands, bands],
        metric, 1.0 / metric, wavenumber, table,
        scalars=(0, 1, 2),
    )
    send, own, column = call(
        spectrum_kernel,
        [(BANDS, 2, 8, COLS), (4, 8, COLS), (2, 8, 128)],
        [(BANDS, 2, 8, COLS), pltpu.SemaphoreType.DMA((BANDS,))],
        recv.reshape(128, 128), factor, dft, table, jnp.asarray(octet_forward()),
        far=(0,), manual=(0,),
    )
    recv = lax.all_to_all(send, "gy", 0, 0, tiled=True)
    total, local_ratio = call(
        column_kernel,
        [(2, 8, 128), full],
        [lines],
        column, factor, metric, wavenumber, edge,
        scalars=(2, 3),
    )
    (send,) = call(
        separator_kernel,
        [(128, 128)],
        [],
        recv, own, factor, total, dft, table, jnp.asarray(octet_inverse()),
        far=(0,),
    )
    recv = lax.all_to_all(send.reshape(8, 16, 128), "gx", 0, 0, tiled=True)
    (out,) = call(
        finish_kernel,
        [(1024, COLS)],
        [lines, half, half],
        recv.reshape(128, 128), solved, local_ratio, metric, sine, edge,
        scalars=(3,), far=(0,),
    )
    return out.reshape(8, 2, ROWS, COLS)


def solution(mesh):
    placed = (P(None, None, "gy", "gx"), P(), P())
    return jax.shard_map(
        per_device, mesh=mesh, in_specs=placed, out_specs=P(None, None, "gy", "gx"), check_vma=False
    )
```

```python
import functools
import math

import jax
import jax.numpy as jnp
import numpy as np
from jax import lax
from jax.experimental import pallas as pl
from jax.experimental.pallas import tpu as pltpu
from jax.sharding import PartitionSpec as P


ASPECT = 0.02
STRIPS = 8
COLS = 256
ROWS = 64
BANDS = 16
NX = STRIPS * COLS
VMEM_LIMIT = 16 * 1024 * 1024
F32 = jnp.float32


def f32(values):
    return np.asarray(values, np.float32)


def sine_table():
    ramp = np.arange(COLS)
    table = np.sin(np.pi * (np.outer(ramp, ramp) % (2 * COLS)) / COLS) * math.sqrt(2.0 / COLS)
    table[0, :] = 0.0
    table[:, 0] = 0.0
    table[0, 0] = 1.0
    return f32(table)


def edge_table():
    ramp = np.arange(COLS)
    left = np.sin(np.pi * ramp / COLS) * math.sqrt(2.0 / COLS)
    right = left * np.where(ramp % 2 == 1, 1.0, -1.0)
    left[0] = right[0] = 0.0
    along = 4.0 * np.sin(np.pi * ramp / (2 * COLS)) ** 2
    rows = [ASPECT * left, ASPECT * right, ASPECT * along]
    kappa = np.arange(STRIPS)[:, None]
    whole = ASPECT * (2.0 * np.sin(np.pi * (STRIPS * ramp[None, :] + kappa) / NX)) ** 2
    return f32(np.stack([np.broadcast_to(r, (8, COLS)) for r in rows] + [whole]))


def dft_table():
    ramp = np.arange(COLS)
    angle = 2.0 * np.pi * (np.outer(ramp, ramp) % COLS) / COLS
    return f32(np.concatenate([np.cos(angle), np.sin(angle)], 1))


def wave_table():
    kappa = np.arange(STRIPS)[:, None]
    j = np.arange(COLS)[None, :]
    angle = 2.0 * np.pi * j * kappa / NX
    return f32(np.stack([np.cos(angle), np.sin(angle)]))


def octet_forward():
    ramp = np.arange(STRIPS)
    angle = 2.0 * np.pi * np.outer(ramp, ramp) / STRIPS
    c, s = np.cos(angle), np.sin(angle)
    return f32(np.block([[c, s], [-s, c]]))


def octet_inverse():
    ramp = np.arange(STRIPS)
    parts = []
    for offset in (0, 1):
        angle = 2.0 * np.pi * np.outer(ramp + offset, ramp) / STRIPS
        c, s = np.cos(angle), np.sin(angle)
        parts.append(np.block([[c, -s], [s, c]]))
    return f32(np.concatenate(parts, 0) / NX)


def dot(a, b):
    return jnp.dot(a, b, precision=lax.Precision.HIGHEST, preferred_element_type=F32)


def lane_ids():
    return lax.broadcasted_iota(jnp.int32, (8, 128), 1)


def wide(column):
    return jnp.broadcast_to(column, (8, 128))


def row_sum(values):
    return wide(jnp.sum(values[:, :128] + values[:, 128:], axis=1, keepdims=True))


def entry(ref, row):
    return ref[row // 128, row % 128]


def splat_inverse(metric_ref, row):
    return 1.0 / jnp.full((8, COLS), entry(metric_ref, row), F32)


def local_shift(wave_ref, edge_ref):
    sub = lax.broadcasted_iota(jnp.int32, (8, COLS), 0)
    shift = edge_ref[2]
    for mode in range(8):
        shift = shift + jnp.where(sub == mode, wave_ref[mode], 0.0)
    return shift


def local_kernel(
    rhs_hbm, metric_hbm, wave_hbm, sine_hbm, edge_hbm, solved_hbm, send_ref, metrics_ref, shift_ref,
    ratio_ref, z_ref, r_lo, r_hi, sine_ref, edge_ref, metric_vec, metric_ref, wave_ref, rhs_sem, sems, out_sem,
):
    first = lax.axis_index("gy") * ROWS
    pairs = (
        (metric_hbm, metric_ref), (wave_hbm, wave_ref), (edge_hbm, edge_ref), (metric_hbm, metric_vec), (sine_hbm, sine_ref)
    )
    small = [pltpu.make_async_copy(a, b, sems.at[i]) for i, (a, b) in enumerate(pairs)]
    half = ROWS // 2
    large = [
        pltpu.make_async_copy(
            rhs_hbm.at[:, pl.ds(part * half, half), pl.ds(side * 128, 128)],
            ref.at[:, pl.ds(part * half, half), :],
            rhs_sem.at[part * 2 + side],
        )
        for part in range(2)
        for side, ref in enumerate((r_lo, r_hi))
    ]
    for copy in small + large:
        copy.start()
    for copy in small[:4]:
        copy.wait()
    metrics_ref[:8, :] = metric_vec[...]
    metrics_ref[8:, :] = 1.0 / metric_vec[...]
    shift_ref[...] = edge_ref[3] + wave_ref[lax.axis_index("gx")]
    lanes = lane_ids()
    shift = local_shift(wave_ref, edge_ref)
    height = jnp.ones((8, COLS), F32)
    slope = jnp.ones((8, COLS), F32)
    for y in range(1, ROWS):
        slope = slope + shift * splat_inverse(metric_ref, first + y) * height
        taller = height + slope
        ratio_ref[y] = height / taller
        height = taller
    small[4].wait()
    sine = sine_ref[...]
    flat = [ref.reshape(16 * ROWS, 128) for ref in (r_lo, r_hi)]

    def line(y, c):
        rows = pl.ds(c * ROWS + y, 8, stride=2 * ROWS)
        return jnp.concatenate([ref[rows, :] for ref in flat], 1)

    state = [jnp.zeros((8, COLS), F32)] * 2
    group = 8
    for base in range(0, ROWS, group):
        if base % half == 0:
            for copy in large[base // half * 2 : base // half * 2 + 2]:
                copy.wait()
        lines = dot(jnp.concatenate([line(y, c) for y in range(base, base + group) for c in range(2)], 0), sine)
        for y in range(max(base, 1), base + group):
            ratio = ratio_ref[y]
            inverse = splat_inverse(metric_ref, first + y)
            for c in range(2):
                at = ((y - base) * 2 + c) * 8
                state[c] = (lines[at : at + 8] * inverse + state[c]) * ratio
                z_ref[y, c] = state[c]
    left = edge_ref[0]
    right = edge_ref[1]
    columns = [[jnp.zeros((8, 128), F32)] * 2 for _ in range(2)]
    upper = [jnp.zeros((8, COLS), F32)] * 2
    done = []
    for y in range(ROWS - 1, 0, -1):
        ratio = ratio_ref[y]
        inverse = splat_inverse(metric_ref, first + y)
        for c in range(2):
            upper[c] = z_ref[y, c] + ratio * upper[c]
            z_ref[y, c] = upper[c]
            a = upper[c] * left
            source = flat[0][pl.ds(c * ROWS + y, 8, stride=2 * ROWS), :]
            a = (a[:, :128] + a[:, 128:] + jnp.where(lanes == 0, source, 0.0)) * inverse[:, :128]
            b = upper[c] * right
            b = (b[:, :128] + b[:, 128:]) * inverse[:, :128]
            columns[0][c] = jnp.where(lanes == y, wide(jnp.sum(a, axis=1, keepdims=True)), columns[0][c])
            columns[1][c] = jnp.where(lanes == y + ROWS, wide(jnp.sum(b, axis=1, keepdims=True)), columns[1][c])
        if y % 16 == 0:
            done.append(pltpu.make_async_copy(z_ref.at[pl.ds(y, 16)], solved_hbm.at[pl.ds(y, 16)], out_sem.at[y // 16]))
            done[-1].start()
    z_ref[0] = jnp.zeros((2, 8, COLS), F32)
    done.append(pltpu.make_async_copy(z_ref.at[pl.ds(0, 16)], solved_hbm.at[pl.ds(0, 16)], out_sem.at[0]))
    done[-1].start()
    edges = jnp.concatenate([z_ref[y, c] for y in (1, ROWS - 1) for c in range(2)], 0)
    edges = dot(edges, sine)
    zero_lane = lax.broadcasted_iota(jnp.int32, (8, COLS), 1) == 0
    inverse = splat_inverse(metric_ref, first)
    for c in range(2):
        near = jnp.where(zero_lane, 0.0, edges[c * 8 : c * 8 + 8]) + line(0, c) * inverse
        far = jnp.where(zero_lane, 0.0, edges[16 + c * 8 : 24 + c * 8])
        for i in range(2):
            part = slice(i * 128, i * 128 + 128)
            send_ref[pl.ds(c * 2 + i, 8, stride=16), :] = near[:, part]
            send_ref[pl.ds(4 + c * 2 + i, 8, stride=16), :] = far[:, part]
        send_ref[pl.ds(8 + c, 8, stride=16), :] = jnp.where(lanes < ROWS, columns[0][c], columns[1][c])
        for pad in range(3):
            send_ref[pl.ds(10 + c * 3 + pad, 8, stride=16), :] = jnp.zeros((8, 128), F32)
    for copy in done:
        copy.wait()


def factors(ref):
    sizes = (ROWS, ROWS, ROWS, BANDS, BANDS, 3)
    starts = np.cumsum((0,) + sizes)
    return [ref.at[pl.ds(int(a), n)] for a, n in zip(starts, sizes)]


def factor_kernel(
    metrics_ref, shift_ref, factor_ref, gamma_ref, base_ref, x_ref
):
    alpha_ref, beta_ref, ratio_ref, up_ref, down_ref, final_ref = factors(factor_ref)
    mine = lax.axis_index("gy")
    shift = shift_ref[...]

    def excess(row):
        double = 2.0 * entry(metrics_ref, row)
        return ((double + shift) - double) * entry(metrics_ref, 1024 + row)

    one = jnp.ones((8, COLS), F32)
    zero = jnp.zeros((8, COLS), F32)
    together = 4

    def bands(outer, carry):
        excess_below, flow = carry
        state = [(one, one, zero, zero)] * together

        def rows(y, state):
            out = []
            for i in range(together):
                height, slope, rest, rise = state[i]
                t = excess((outer * together + i) * ROWS + y)
                slope = slope + t * height
                height = height + slope
                rise = rise + t * (rest + 1.0)
                rest = rest + rise
                out.append((height, slope, rest, rise))
            return tuple(out)

        state = lax.fori_loop(1, ROWS, rows, tuple(state), unroll=21)
        for i in range(together):
            height, slope, rest, _ = state[i]
            band = outer * together + i
            gamma = 1.0 / height
            base = excess(band * ROWS) + rest * gamma + excess_below
            x = base + flow
            up = gamma / (gamma + x)
            gamma_ref[band] = gamma
            base_ref[band] = base
            x_ref[band] = x
            up_ref[band] = up
            excess_below = (slope - 1.0) * gamma
            flow = up * x
        return excess_below, flow

    lax.fori_loop(0, BANDS // together, bands, (zero, one))

    above, down, inverse = one, zero, zero
    for band in range(BANDS - 1, -1, -1):
        gamma = gamma_ref[band]
        down_ref[band] = down

        @pl.when(band == mine)
        def _(above=above, down=down, inverse=inverse, gamma=gamma):
            final_ref[0] = down
            final_ref[1] = inverse
            final_ref[2] = 1.0 / (x_ref[mine] + gamma * above)

        if band:
            x = base_ref[band] + gamma * above
            below = gamma_ref[band - 1]
            inverse = 1.0 / (below + x)
            down = below * inverse
            above = x * inverse

    height, slope = one, one
    for y in range(1, ROWS):
        beta_ref[y] = height
        slope = slope + excess(mine * ROWS + y) * height
        taller = height + slope
        ratio_ref[y] = height / taller
        height = taller
    gamma = 1.0 / height
    height, slope = one, one
    for y in range(ROWS - 1, 0, -1):
        alpha_ref[y] = height * gamma
        beta_ref[y] = beta_ref[y] * gamma
        slope = slope + excess(mine * ROWS + y) * height
        height = height + slope


def spectrum_kernel(
    recv_ref, factor_ref, dft_ref, table_ref, octet_ref, send_ref, own_ref, column_ref
):
    alpha_ref, beta_ref, _, up_ref, down_ref, _ = factors(factor_ref)
    mine = lax.axis_index("gy")

    def take(i):
        return recv_ref[pl.ds(i, 8, stride=16), :]

    pieces = [[], []]
    for c in range(2):
        for i in range(2):
            pieces[c].append(take(c * 2 + i))
        for i in range(2):
            pieces[c].append(take(4 + c * 2 + i))
        column = take(8 + c)
        pieces[c].append(column + pltpu.roll(pltpu.roll(column, 1, 0), ROWS, 1))
    stacked = jnp.concatenate([jnp.concatenate(pieces[0], 1), jnp.concatenate(pieces[1], 1)], 0)
    mixed = dot(octet_ref[...], stacked)
    cos, sin = table_ref[0], table_ref[1]
    turned = [[], []]
    for line in range(2):
        re = mixed[:8, line * COLS : line * COLS + COLS]
        im = mixed[8:, line * COLS : line * COLS + COLS]
        turned[0].append(re * cos + im * sin)
        turned[1].append(im * cos - re * sin)
    both = dot(jnp.concatenate(turned[0] + turned[1], 0), dft_ref[...])
    columns = [mixed[c * 8 : c * 8 + 8, 2 * COLS :] for c in range(2)]
    near = [jnp.zeros((8, COLS), F32)] * 2
    far = [jnp.zeros((8, COLS), F32)] * 2
    for y in range(1, ROWS):
        alpha, beta = alpha_ref[y], beta_ref[y]
        for c in range(2):
            source = wide(columns[c][:, y : y + 1])
            source = jnp.concatenate([source, source], 1)
            near[c] = near[c] + alpha * source
            far[c] = far[c] + beta * source
    sides = []
    for line, extra in enumerate((near, far)):
        re_cos = both[line * 8 : line * 8 + 8, :COLS]
        re_sin = both[line * 8 : line * 8 + 8, COLS:]
        im_cos = both[16 + line * 8 : 24 + line * 8, :COLS]
        im_sin = both[16 + line * 8 : 24 + line * 8, COLS:]
        sides.append((re_cos + im_sin + extra[0], im_cos - re_sin + extra[1]))
    for c in range(2):
        own_ref[c], own_ref[2 + c] = sides[0][c], sides[1][c]
        column_ref[c] = columns[c]
        send_ref[mine, c] = jnp.zeros((8, COLS), F32)
    up, down = up_ref[mine], down_ref[mine]

    def above(band, carry):
        factor = up_ref[band]
        for c in range(2):
            send_ref[band, c] = carry[c]
        return tuple(value * factor for value in carry)

    def below(step, carry):
        band = mine - 1 - step
        factor = down_ref[band]
        for c in range(2):
            send_ref[band, c] = carry[c]
        return tuple(value * factor for value in carry)

    lax.fori_loop(mine + 1, BANDS, above, tuple(sides[1][c] + up * sides[0][c] for c in range(2)))
    lax.fori_loop(0, mine, below, tuple(sides[0][c] + down * sides[1][c] for c in range(2)))


def column_kernel(column_ref, factor_ref, metric_ref, wave_ref, edge_ref, sum_ref, local_ref, z_ref):
    ratio_ref = factors(factor_ref)[2]
    first = lax.axis_index("gy") * ROWS
    shift = local_shift(wave_ref, edge_ref)
    height = jnp.ones((8, COLS), F32)
    slope = jnp.ones((8, COLS), F32)
    for y in range(1, ROWS):
        slope = slope + shift * splat_inverse(metric_ref, first + y) * height
        taller = height + slope
        local_ref[y] = height / taller
        height = taller
    lanes = lane_ids()
    columns = [column_ref[c] for c in range(2)]
    state = [jnp.zeros((8, COLS), F32)] * 2
    for y in range(1, ROWS):
        ratio = ratio_ref[y]
        for c in range(2):
            source = wide(columns[c][:, y : y + 1])
            state[c] = (jnp.concatenate([source, source], 1) + state[c]) * ratio
            z_ref[y, c] = state[c]
    upper = [jnp.zeros((8, COLS), F32)] * 2
    total = [jnp.zeros((8, 128), F32)] * 2
    for y in range(ROWS - 1, 0, -1):
        ratio = ratio_ref[y]
        for c in range(2):
            upper[c] = z_ref[y, c] + ratio * upper[c]
            total[c] = jnp.where(lanes == y, row_sum(upper[c]), total[c])
    for c in range(2):
        sum_ref[c] = total[c]


def separator_kernel(
    recv_ref, own_ref, factor_ref, sum_ref, dft_ref, table_ref, octet_ref, send_ref
):
    alpha_ref, beta_ref, _, _, _, final_ref = factors(factor_ref)
    mine = lax.axis_index("gy")
    from_below = [own_ref[c] for c in range(2)]
    from_above = [own_ref[2 + c] for c in range(2)]
    for band in range(BANDS):
        for c in range(2):
            value = recv_ref[band, c]
            from_below[c] = from_below[c] + jnp.where(band < mine, value, 0.0)
            from_above[c] = from_above[c] + jnp.where(band > mine, value, 0.0)
    down, inverse, pivot = final_ref[0], final_ref[1], final_ref[2]
    near = [(from_below[c] + down * from_above[c]) * pivot for c in range(2)]
    far = [from_above[c] * inverse + down * near[c] for c in range(2)]
    lanes = lane_ids()
    both = dot(jnp.concatenate([near[0], far[0], near[1], far[1]], 0), dft_ref[...])
    total = [sum_ref[c] for c in range(2)]
    for y in range(1, ROWS):
        alpha, beta = alpha_ref[y], beta_ref[y]
        for c in range(2):
            extra = row_sum(alpha * near[c] + beta * far[c])
            total[c] = total[c] + jnp.where(lanes == y, extra, 0.0)
    cos, sin = table_ref[0], table_ref[1]
    turned = [[], []]
    for line in range(2):
        re_cos = both[line * 8 : line * 8 + 8, :COLS]
        re_sin = both[line * 8 : line * 8 + 8, COLS:]
        im_cos = both[16 + line * 8 : 24 + line * 8, :COLS]
        im_sin = both[16 + line * 8 : 24 + line * 8, COLS:]
        re = re_cos - im_sin
        im = re_sin + im_cos
        turned[0].append(re * cos - im * sin)
        turned[1].append(re * sin + im * cos)
    stacked = [jnp.concatenate(turned[c] + [total[c]], 1) for c in range(2)]
    out = dot(octet_ref[...], jnp.concatenate(stacked, 0))
    for c in range(2):
        for i in range(4):
            row = (i // 2) * 4 + c * 2 + i % 2
            send_ref[pl.ds(row, 8, stride=16), :] = out[c * 8 : c * 8 + 8, i * 128 : i * 128 + 128]
        here = out[c * 8 : c * 8 + 8, 2 * COLS :]
        there = out[16 + c * 8 : 24 + c * 8, 2 * COLS :]
        send_ref[pl.ds(8 + c, 8, stride=16), :] = jnp.where(lanes < ROWS, here, pltpu.roll(there, ROWS, 1))
        for pad in range(3):
            send_ref[pl.ds(10 + c * 3 + pad, 8, stride=16), :] = jnp.zeros((8, 128), F32)


def finish_kernel(recv_ref, solved_ref, ratio_ref, metric_ref, sine_ref, edge_ref, out_hbm, z_ref, o_lo, o_hi, sems):
    first = lax.axis_index("gy") * ROWS

    def take(i):
        return recv_ref[pl.ds(i, 8, stride=16), :]

    sine = sine_ref[...]
    near = [jnp.concatenate([take(c * 2), take(c * 2 + 1)], 1) for c in range(2)]
    far = [jnp.concatenate([take(4 + c * 2), take(5 + c * 2)], 1) for c in range(2)]
    columns = [take(8 + c) for c in range(2)]
    edges = dot(jnp.concatenate(near + far, 0), sine)
    left, right = edge_ref[0], edge_ref[1]
    zero_lane = lax.broadcasted_iota(jnp.int32, (8, COLS), 1) == 0
    state = [edges[c * 8 : c * 8 + 8] for c in range(2)]
    for y in range(1, ROWS):
        ratio = ratio_ref[y]
        inverse = splat_inverse(metric_ref, first + y)
        a, b = left * inverse, right * inverse
        for c in range(2):
            here = wide(columns[c][:, y : y + 1])
            there = wide(columns[c][:, ROWS + y : ROWS + y + 1])
            here = jnp.concatenate([here, here], 1)
            there = jnp.concatenate([there, there], 1)
            state[c] = (state[c] + (a * here + b * there)) * ratio
            z_ref[y, c] = state[c]
    upper = [edges[16 + c * 8 : 24 + c * 8] for c in range(2)]
    flat = [ref.reshape(16 * ROWS, 128) for ref in (o_lo, o_hi)]
    group, half = 8, ROWS // 2
    copies = []
    for base in range(ROWS - group, -1, -group):
        lines = []
        for y in range(base + group - 1, base - 1, -1):
            for c in range(2):
                if y:
                    upper[c] = z_ref[y, c] + ratio_ref[y] * upper[c]
                    here = wide(columns[c][:, y : y + 1])
                    here = jnp.concatenate([here, here], 1)
                    lines.append(jnp.where(zero_lane, here, upper[c] + solved_ref[y, c]))
                else:
                    lines.append(edges[c * 8 : c * 8 + 8])
        product = dot(jnp.concatenate(lines, 0), sine)
        for i in range(2 * group):
            rows = pl.ds(i % 2 * ROWS + base + group - 1 - i // 2, 8, stride=2 * ROWS)
            flat[0][rows, :] = product[i * 8 : i * 8 + 8, :128]
            flat[1][rows, :] = product[i * 8 : i * 8 + 8, 128:]
        if base % half == 0:
            for side, ref in enumerate((o_lo, o_hi)):
                copies.append(
                    pltpu.make_async_copy(
                        ref.at[:, pl.ds(base, half), :],
                        out_hbm.at[:, pl.ds(base, half), pl.ds(side * 128, 128)],
                        sems.at[len(copies)],
                    )
                )
                copies[-1].start()
    for copy in copies:
        copy.wait()


def call(kernel, outs, scratch, *operands, scalars=(), far=(), manual=(), space=pltpu.VMEM):
    smem = pl.BlockSpec(memory_space=pltpu.SMEM)
    specs = [smem if i in scalars else pl.BlockSpec(memory_space=space) for i in range(len(operands))]
    if space == pltpu.HBM:
        operands = [pltpu.with_memory_space_constraint(a, space) for a in operands]
    return pl.pallas_call(
        kernel,
        out_shape=[(pltpu.HBM if i in far else pltpu.VMEM)(s, F32) for i, s in enumerate(outs)],
        in_specs=specs,
        out_specs=[pl.BlockSpec(memory_space=pltpu.HBM if i in manual else pltpu.VMEM) for i in range(len(outs))],
        scratch_shapes=[pltpu.VMEM(s, F32) if isinstance(s, tuple) else s for s in scratch],
        compiler_params=pltpu.CompilerParams(vmem_limit_bytes=VMEM_LIMIT),
    )(*operands)


def per_device(rhs, metric, wavenumber):
    sine, edge = jnp.asarray(sine_table()), jnp.asarray(edge_table())
    dft, table = jnp.asarray(dft_table()), jnp.asarray(wave_table())
    metric = metric.reshape(8, 128)
    full, lines, side, bands = (ROWS, 8, COLS), (ROWS, 2, 8, COLS), (16, ROWS, 128), (BANDS, 8, COLS)
    solved, send, metrics, shift = call(
        local_kernel,
        [lines, (128, 128), (16, 128), (8, COLS)],
        [
            full, lines, side, side, (COLS, COLS), (4, 8, COLS), (8, 128),
            pltpu.SMEM((8, 128), F32), pltpu.SMEM((8,), F32),
            pltpu.SemaphoreType.DMA((4,)), pltpu.SemaphoreType.DMA((5,)), pltpu.SemaphoreType.DMA((4,)),
        ],
        rhs.reshape(16, ROWS, COLS), metric, wavenumber, sine, edge,
        space=pltpu.HBM, far=(0, 1), manual=(0,),
    )
    recv = lax.all_to_all(send.reshape(8, 16, 128), "gx", 0, 0, tiled=True)
    (factor,) = call(
        factor_kernel,
        [(3 * ROWS + 2 * BANDS + 3, 8, COLS)],
        [bands, bands, bands],
        metrics, shift,
        scalars=(0,),
    )
    send, own, column = call(
        spectrum_kernel,
        [(BANDS, 2, 8, COLS), (4, 8, COLS), (2, 8, 128)],
        [],
        recv.reshape(128, 128), factor, dft, table, jnp.asarray(octet_forward()),
        far=(0,),
    )
    recv = lax.all_to_all(send, "gy", 0, 0, tiled=True)
    total, local_ratio = call(
        column_kernel,
        [(2, 8, 128), full],
        [lines],
        column, factor, metric, wavenumber, edge,
        scalars=(2, 3),
    )
    (send,) = call(
        separator_kernel,
        [(128, 128)],
        [],
        recv, own, factor, total, dft, table, jnp.asarray(octet_inverse()),
    )
    recv = lax.all_to_all(send.reshape(8, 16, 128), "gx", 0, 0, tiled=True)
    (out,) = call(
        finish_kernel,
        [(16, ROWS, COLS)],
        [lines, side, side, pltpu.SemaphoreType.DMA((4,))],
        recv.reshape(128, 128), solved, local_ratio, metric, sine, edge,
        scalars=(3,), far=(0,), manual=(0,),
    )
    return out.reshape(8, 2, ROWS, COLS)


def solution(mesh):
    placed = (P(None, None, "gy", "gx"), P(), P())
    return jax.shard_map(
        per_device, mesh=mesh, in_specs=placed, out_specs=P(None, None, "gy", "gx"), check_vma=False
    )
```

```python
import functools
import math

import jax
import jax.numpy as jnp
import numpy as np
from jax import lax
from jax.experimental import pallas as pl
from jax.experimental.pallas import tpu as pltpu
from jax.sharding import PartitionSpec as P


ASPECT = 0.02
STRIPS = 8
COLS = 256
ROWS = 64
BANDS = 16
PITCH = ROWS + 8
NX = STRIPS * COLS
VMEM_LIMIT = 16 * 1024 * 1024
F32 = jnp.float32


def f32(values):
    return np.asarray(values, np.float32)


def sine_table():
    ramp = np.arange(COLS)
    table = np.sin(np.pi * (np.outer(ramp, ramp) % (2 * COLS)) / COLS) * math.sqrt(2.0 / COLS)
    table[0, :] = 0.0
    table[:, 0] = 0.0
    table[0, 0] = 1.0
    return f32(table)


def edge_table():
    ramp = np.arange(COLS)
    left = np.sin(np.pi * ramp / COLS) * math.sqrt(2.0 / COLS)
    left[0] = 0.0
    along = 4.0 * np.sin(np.pi * ramp / (2 * COLS)) ** 2
    flip = np.where(ramp % 2 == 1, 1.0, -1.0)
    rows = [ASPECT * left, ASPECT * left * flip, ASPECT * along]
    kappa = np.arange(STRIPS)[:, None]
    whole = ASPECT * (2.0 * np.sin(np.pi * (STRIPS * ramp[None, :] + kappa) / NX)) ** 2
    return f32(np.stack([np.broadcast_to(r, (8, COLS)) for r in rows] + [whole, np.broadcast_to(flip, (8, COLS))]))


def dft_table():
    ramp = np.arange(COLS)
    angle = 2.0 * np.pi * (np.outer(ramp, ramp) % COLS) / COLS
    return f32(np.concatenate([np.cos(angle), np.sin(angle)], 1))


def wave_table():
    kappa = np.arange(STRIPS)[:, None]
    j = np.arange(COLS)[None, :]
    angle = 2.0 * np.pi * j * kappa / NX
    return f32(np.stack([np.cos(angle), np.sin(angle)]))


def octet_forward():
    ramp = np.arange(STRIPS)
    angle = 2.0 * np.pi * np.outer(ramp, ramp) / STRIPS
    c, s = np.cos(angle), np.sin(angle)
    return f32(np.block([[c, s], [-s, c]]))


def octet_inverse():
    ramp = np.arange(STRIPS)
    parts = []
    for offset in (0, 1):
        angle = 2.0 * np.pi * np.outer(ramp + offset, ramp) / STRIPS
        c, s = np.cos(angle), np.sin(angle)
        parts.append(np.block([[c, -s], [s, c]]))
    return f32(np.concatenate(parts, 0) / NX)


def dot(a, b):
    return jnp.dot(a, b, precision=lax.Precision.HIGHEST, preferred_element_type=F32)


def lane_ids():
    return lax.broadcasted_iota(jnp.int32, (8, 128), 1)


def wide(column):
    return jnp.broadcast_to(column, (8, 128))


def row_sum(values):
    return wide(jnp.sum(values[:, :128] + values[:, 128:], axis=1, keepdims=True))


def splat_inverse(metric_ref, row):
    return 1.0 / jnp.full((8, COLS), metric_ref[row], F32)


def local_shift(wave_ref, edge_ref):
    sub = lax.broadcasted_iota(jnp.int32, (8, COLS), 0)
    shift = edge_ref[2]
    for mode in range(8):
        shift = shift + jnp.where(sub == mode, wave_ref[mode], 0.0)
    return shift


def local_kernel(
    rhs_hbm, metric_hbm, tiled_hbm, wave_hbm, sine_hbm, edge_hbm, solved_hbm, send_ref, metrics_ref, shift_ref,
    ratio_ref, z_ref, r_lo, r_hi, sine_ref, edge_ref, metric_vec, metric_ref, wave_ref, rhs_sem, sems, out_sem,
):
    first = lax.axis_index("gy") * ROWS
    pairs = (
        (metric_hbm, metric_ref), (wave_hbm, wave_ref), (edge_hbm, edge_ref), (tiled_hbm, metric_vec), (sine_hbm, sine_ref)
    )
    small = [pltpu.make_async_copy(a, b, sems.at[i]) for i, (a, b) in enumerate(pairs)]
    half = ROWS // 2
    large = [
        pltpu.make_async_copy(
            rhs_hbm.at[:, pl.ds(part * half, half), pl.ds(side * 128, 128)],
            ref.at[:, pl.ds(part * half, half), :],
            rhs_sem.at[part * 2 + side],
        )
        for part in range(2)
        for side, ref in enumerate((r_lo, r_hi))
    ]
    for copy in small + large:
        copy.start()
    for copy in small[:4]:
        copy.wait()
    metrics_ref[:8, :] = metric_vec[...]
    metrics_ref[8:, :] = 1.0 / metric_vec[...]
    shift_ref[...] = edge_ref[3] + wave_ref[lax.axis_index("gx")]
    lanes = lane_ids()
    shift = local_shift(wave_ref, edge_ref)
    height = jnp.ones((8, COLS), F32)
    slope = jnp.ones((8, COLS), F32)
    for y in range(1, ROWS):
        slope = slope + shift * splat_inverse(metric_ref, first + y) * height
        taller = height + slope
        ratio_ref[y] = height / taller
        height = taller
    small[4].wait()
    sine = sine_ref[...]
    flat = [ref.reshape(16 * PITCH, 128) for ref in (r_lo, r_hi)]

    def line(y, c):
        rows = pl.ds(c * PITCH + y, 8, stride=2 * PITCH)
        return jnp.concatenate([ref[rows, :] for ref in flat], 1)

    state = [jnp.zeros((8, COLS), F32)] * 2
    group = 8
    for base in range(0, ROWS, group):
        if base % half == 0:
            for copy in large[base // half * 2 : base // half * 2 + 2]:
                copy.wait()
        lines = dot(jnp.concatenate([line(y, c) for y in range(base, base + group) for c in range(2)], 0), sine)
        for y in range(max(base, 1), base + group):
            ratio = ratio_ref[y]
            inverse = splat_inverse(metric_ref, first + y)
            for c in range(2):
                at = ((y - base) * 2 + c) * 8
                state[c] = (lines[at : at + 8] * inverse + state[c]) * ratio
                z_ref[y, c] = state[c]
    left = edge_ref[0]
    right = edge_ref[1]
    columns = [[jnp.zeros((8, 128), F32)] * 2 for _ in range(2)]
    upper = [jnp.zeros((8, COLS), F32)] * 2
    done = []
    for y in range(ROWS - 1, 0, -1):
        ratio = ratio_ref[y]
        inverse = splat_inverse(metric_ref, first + y)
        for c in range(2):
            upper[c] = z_ref[y, c] + ratio * upper[c]
            z_ref[y, c] = upper[c]
            a = upper[c] * left
            source = flat[0][pl.ds(c * PITCH + y, 8, stride=2 * PITCH), :]
            a = (a[:, :128] + a[:, 128:] + jnp.where(lanes == 0, source, 0.0)) * inverse[:, :128]
            b = upper[c] * right
            b = (b[:, :128] + b[:, 128:]) * inverse[:, :128]
            columns[0][c] = jnp.where(lanes == y, wide(jnp.sum(a, axis=1, keepdims=True)), columns[0][c])
            columns[1][c] = jnp.where(lanes == y + ROWS, wide(jnp.sum(b, axis=1, keepdims=True)), columns[1][c])
        if y % 16 == 0:
            done.append(pltpu.make_async_copy(z_ref.at[pl.ds(y, 16)], solved_hbm.at[pl.ds(y, 16)], out_sem.at[y // 16]))
            done[-1].start()
    z_ref[0] = jnp.zeros((2, 8, COLS), F32)
    done.append(pltpu.make_async_copy(z_ref.at[pl.ds(0, 16)], solved_hbm.at[pl.ds(0, 16)], out_sem.at[0]))
    done[-1].start()
    edges = jnp.concatenate([z_ref[y, c] for y in (1, ROWS - 1) for c in range(2)], 0)
    edges = dot(edges, sine)
    zero_lane = lax.broadcasted_iota(jnp.int32, (8, COLS), 1) == 0
    inverse = splat_inverse(metric_ref, first)
    for c in range(2):
        near = jnp.where(zero_lane, 0.0, edges[c * 8 : c * 8 + 8]) + line(0, c) * inverse
        far = jnp.where(zero_lane, 0.0, edges[16 + c * 8 : 24 + c * 8])
        for i in range(2):
            part = slice(i * 128, i * 128 + 128)
            send_ref[pl.ds(c * 2 + i, 8, stride=16), :] = near[:, part]
            send_ref[pl.ds(4 + c * 2 + i, 8, stride=16), :] = far[:, part]
        send_ref[pl.ds(8 + c, 8, stride=16), :] = jnp.where(lanes < ROWS, columns[0][c], columns[1][c])
        for pad in range(3):
            send_ref[pl.ds(10 + c * 3 + pad, 8, stride=16), :] = jnp.zeros((8, 128), F32)
    for copy in done:
        copy.wait()


def factors(ref):
    sizes = (ROWS, ROWS, ROWS, BANDS, BANDS, 3)
    starts = np.cumsum((0,) + sizes)
    return [ref.at[pl.ds(int(a), n)] for a, n in zip(starts, sizes)]


def factor_kernel(
    metrics_ref, shift_ref, factor_ref, gamma_ref, base_ref, x_ref
):
    alpha_ref, beta_ref, ratio_ref, up_ref, down_ref, final_ref = factors(factor_ref)
    mine = lax.axis_index("gy")
    shift = shift_ref[...]

    def excess(row):
        double = 2.0 * metrics_ref[row]
        return ((double + shift) - double) * metrics_ref[1024 + row]

    one = jnp.ones((8, COLS), F32)
    zero = jnp.zeros((8, COLS), F32)
    together = 4

    def bands(outer, carry):
        excess_below, flow = carry
        state = [(one, one, zero, zero)] * together

        def rows(y, state):
            out = []
            for i in range(together):
                height, slope, rest, rise = state[i]
                t = excess((outer * together + i) * ROWS + y)
                slope = slope + t * height
                height = height + slope
                rise = rise + t * (rest + 1.0)
                rest = rest + rise
                out.append((height, slope, rest, rise))
            return tuple(out)

        state = lax.fori_loop(1, ROWS, rows, tuple(state), unroll=21)
        for i in range(together):
            height, slope, rest, _ = state[i]
            band = outer * together + i
            gamma = 1.0 / height
            base = excess(band * ROWS) + rest * gamma + excess_below
            x = base + flow
            up = gamma / (gamma + x)
            gamma_ref[band] = gamma
            base_ref[band] = base
            x_ref[band] = x
            up_ref[band] = up
            excess_below = (slope - 1.0) * gamma
            flow = up * x
        return excess_below, flow

    lax.fori_loop(0, BANDS // together, bands, (zero, one))

    above, down, inverse = one, zero, zero
    for band in range(BANDS - 1, -1, -1):
        gamma = gamma_ref[band]
        down_ref[band] = down

        @pl.when(band == mine)
        def _(above=above, down=down, inverse=inverse, gamma=gamma):
            final_ref[0] = down
            final_ref[1] = inverse
            final_ref[2] = 1.0 / (x_ref[mine] + gamma * above)

        if band:
            x = base_ref[band] + gamma * above
            below = gamma_ref[band - 1]
            inverse = 1.0 / (below + x)
            down = below * inverse
            above = x * inverse

    height, slope = one, one
    for y in range(1, ROWS):
        beta_ref[y] = height
        slope = slope + excess(mine * ROWS + y) * height
        taller = height + slope
        ratio_ref[y] = height / taller
        height = taller
    gamma = 1.0 / height
    height, slope = one, one
    for y in range(ROWS - 1, 0, -1):
        alpha_ref[y] = height * gamma
        beta_ref[y] = beta_ref[y] * gamma
        slope = slope + excess(mine * ROWS + y) * height
        height = height + slope


def spectrum_kernel(
    recv_ref, factor_ref, dft_ref, table_ref, octet_ref, send_ref, own_ref, column_ref
):
    alpha_ref, beta_ref, _, up_ref, down_ref, _ = factors(factor_ref)
    mine = lax.axis_index("gy")

    def take(i):
        return recv_ref[pl.ds(i, 8, stride=16), :]

    pieces = [[], []]
    for c in range(2):
        for i in range(2):
            pieces[c].append(take(c * 2 + i))
        for i in range(2):
            pieces[c].append(take(4 + c * 2 + i))
        column = take(8 + c)
        pieces[c].append(column + pltpu.roll(pltpu.roll(column, 1, 0), ROWS, 1))
    stacked = jnp.concatenate([jnp.concatenate(pieces[0], 1), jnp.concatenate(pieces[1], 1)], 0)
    mixed = dot(octet_ref[...], stacked)
    cos, sin = table_ref[0], table_ref[1]
    turned = [[], []]
    for line in range(2):
        re = mixed[:8, line * COLS : line * COLS + COLS]
        im = mixed[8:, line * COLS : line * COLS + COLS]
        turned[0].append(re * cos + im * sin)
        turned[1].append(im * cos - re * sin)
    both = dot(jnp.concatenate(turned[0] + turned[1], 0), dft_ref[...])
    columns = [mixed[c * 8 : c * 8 + 8, 2 * COLS :] for c in range(2)]
    near = [jnp.zeros((8, COLS), F32)] * 2
    far = [jnp.zeros((8, COLS), F32)] * 2
    for y in range(1, ROWS):
        alpha, beta = alpha_ref[y], beta_ref[y]
        for c in range(2):
            source = wide(columns[c][:, y : y + 1])
            source = jnp.concatenate([source, source], 1)
            near[c] = near[c] + alpha * source
            far[c] = far[c] + beta * source
    sides = []
    for line, extra in enumerate((near, far)):
        re_cos = both[line * 8 : line * 8 + 8, :COLS]
        re_sin = both[line * 8 : line * 8 + 8, COLS:]
        im_cos = both[16 + line * 8 : 24 + line * 8, :COLS]
        im_sin = both[16 + line * 8 : 24 + line * 8, COLS:]
        sides.append((re_cos + im_sin + extra[0], im_cos - re_sin + extra[1]))
    for c in range(2):
        own_ref[c], own_ref[2 + c] = sides[0][c], sides[1][c]
        column_ref[c] = columns[c]
        send_ref[mine, c] = jnp.zeros((8, COLS), F32)
    up, down = up_ref[mine], down_ref[mine]

    def above(band, carry):
        factor = up_ref[band]
        for c in range(2):
            send_ref[band, c] = carry[c]
        return tuple(value * factor for value in carry)

    def below(step, carry):
        band = mine - 1 - step
        factor = down_ref[band]
        for c in range(2):
            send_ref[band, c] = carry[c]
        return tuple(value * factor for value in carry)

    lax.fori_loop(mine + 1, BANDS, above, tuple(sides[1][c] + up * sides[0][c] for c in range(2)))
    lax.fori_loop(0, mine, below, tuple(sides[0][c] + down * sides[1][c] for c in range(2)))


def column_kernel(column_ref, factor_ref, metric_ref, wave_ref, edge_ref, sum_ref, local_ref, coupling_ref, z_ref):
    ratio_ref = factors(factor_ref)[2]
    first = lax.axis_index("gy") * ROWS
    shift = local_shift(wave_ref, edge_ref)
    height = jnp.ones((8, COLS), F32)
    slope = jnp.ones((8, COLS), F32)
    for y in range(1, ROWS):
        inverse = splat_inverse(metric_ref, first + y)
        coupling_ref[y] = edge_ref[0] * inverse
        slope = slope + shift * inverse * height
        taller = height + slope
        local_ref[y] = height / taller
        height = taller
    lanes = lane_ids()
    columns = [column_ref[c] for c in range(2)]
    state = [jnp.zeros((8, COLS), F32)] * 2
    for y in range(1, ROWS):
        ratio = ratio_ref[y]
        for c in range(2):
            source = wide(columns[c][:, y : y + 1])
            state[c] = (jnp.concatenate([source, source], 1) + state[c]) * ratio
            z_ref[y, c] = state[c]
    upper = [jnp.zeros((8, COLS), F32)] * 2
    total = [jnp.zeros((8, 128), F32)] * 2
    for y in range(ROWS - 1, 0, -1):
        ratio = ratio_ref[y]
        for c in range(2):
            upper[c] = z_ref[y, c] + ratio * upper[c]
            total[c] = jnp.where(lanes == y, row_sum(upper[c]), total[c])
    for c in range(2):
        sum_ref[c] = total[c]


def separator_kernel(
    recv_ref, own_ref, factor_ref, sum_ref, dft_ref, table_ref, octet_ref, send_ref
):
    alpha_ref, beta_ref, _, _, _, final_ref = factors(factor_ref)
    mine = lax.axis_index("gy")
    from_below = [own_ref[c] for c in range(2)]
    from_above = [own_ref[2 + c] for c in range(2)]
    for band in range(BANDS):
        for c in range(2):
            value = recv_ref[band, c]
            from_below[c] = from_below[c] + jnp.where(band < mine, value, 0.0)
            from_above[c] = from_above[c] + jnp.where(band > mine, value, 0.0)
    down, inverse, pivot = final_ref[0], final_ref[1], final_ref[2]
    near = [(from_below[c] + down * from_above[c]) * pivot for c in range(2)]
    far = [from_above[c] * inverse + down * near[c] for c in range(2)]
    lanes = lane_ids()
    both = dot(jnp.concatenate([near[0], far[0], near[1], far[1]], 0), dft_ref[...])
    total = [sum_ref[c] for c in range(2)]
    for y in range(1, ROWS):
        alpha, beta = alpha_ref[y], beta_ref[y]
        for c in range(2):
            extra = row_sum(alpha * near[c] + beta * far[c])
            total[c] = total[c] + jnp.where(lanes == y, extra, 0.0)
    cos, sin = table_ref[0], table_ref[1]
    turned = [[], []]
    for line in range(2):
        re_cos = both[line * 8 : line * 8 + 8, :COLS]
        re_sin = both[line * 8 : line * 8 + 8, COLS:]
        im_cos = both[16 + line * 8 : 24 + line * 8, :COLS]
        im_sin = both[16 + line * 8 : 24 + line * 8, COLS:]
        re = re_cos - im_sin
        im = re_sin + im_cos
        turned[0].append(re * cos - im * sin)
        turned[1].append(re * sin + im * cos)
    stacked = [jnp.concatenate(turned[c] + [total[c]], 1) for c in range(2)]
    out = dot(octet_ref[...], jnp.concatenate(stacked, 0))
    for c in range(2):
        for i in range(4):
            row = (i // 2) * 4 + c * 2 + i % 2
            send_ref[pl.ds(row, 8, stride=16), :] = out[c * 8 : c * 8 + 8, i * 128 : i * 128 + 128]
        here = out[c * 8 : c * 8 + 8, 2 * COLS :]
        there = out[16 + c * 8 : 24 + c * 8, 2 * COLS :]
        send_ref[pl.ds(8 + c, 8, stride=16), :] = jnp.where(lanes < ROWS, here, pltpu.roll(there, ROWS, 1))
        for pad in range(3):
            send_ref[pl.ds(10 + c * 3 + pad, 8, stride=16), :] = jnp.zeros((8, 128), F32)


def finish_kernel(recv_ref, solved_ref, ratio_ref, coupling_ref, sine_ref, edge_ref, out_hbm, z_ref, o_lo, o_hi, sems):
    def take(i):
        return recv_ref[pl.ds(i, 8, stride=16), :]

    sine = sine_ref[...]
    near = [jnp.concatenate([take(c * 2), take(c * 2 + 1)], 1) for c in range(2)]
    far = [jnp.concatenate([take(4 + c * 2), take(5 + c * 2)], 1) for c in range(2)]
    columns = [take(8 + c) for c in range(2)]
    edges = dot(jnp.concatenate(near + far, 0), sine)
    flip = edge_ref[4]
    zero_lane = lax.broadcasted_iota(jnp.int32, (8, COLS), 1) == 0
    state = [edges[c * 8 : c * 8 + 8] for c in range(2)]
    for y in range(1, ROWS):
        ratio = ratio_ref[y]
        coupling = coupling_ref[y]
        for c in range(2):
            here = wide(columns[c][:, y : y + 1])
            there = wide(columns[c][:, ROWS + y : ROWS + y + 1])
            here = jnp.concatenate([here, here], 1)
            there = jnp.concatenate([there, there], 1)
            state[c] = (state[c] + coupling * (here + flip * there)) * ratio
            z_ref[y, c] = state[c]
    upper = [edges[16 + c * 8 : 24 + c * 8] for c in range(2)]
    flat = [ref.reshape(16 * PITCH, 128) for ref in (o_lo, o_hi)]
    group, half = 8, ROWS // 2
    copies = []
    for base in range(ROWS - group, -1, -group):
        lines = []
        for y in range(base + group - 1, base - 1, -1):
            for c in range(2):
                if y:
                    upper[c] = z_ref[y, c] + ratio_ref[y] * upper[c]
                    here = wide(columns[c][:, y : y + 1])
                    here = jnp.concatenate([here, here], 1)
                    lines.append(jnp.where(zero_lane, here, upper[c] + solved_ref[y, c]))
                else:
                    lines.append(edges[c * 8 : c * 8 + 8])
        product = dot(jnp.concatenate(lines, 0), sine)
        for i in range(2 * group):
            rows = pl.ds(i % 2 * PITCH + base + group - 1 - i // 2, 8, stride=2 * PITCH)
            flat[0][rows, :] = product[i * 8 : i * 8 + 8, :128]
            flat[1][rows, :] = product[i * 8 : i * 8 + 8, 128:]
        if base % half == 0:
            for side, ref in enumerate((o_lo, o_hi)):
                copies.append(
                    pltpu.make_async_copy(
                        ref.at[:, pl.ds(base, half), :],
                        out_hbm.at[:, pl.ds(base, half), pl.ds(side * 128, 128)],
                        sems.at[len(copies)],
                    )
                )
                copies[-1].start()
    for copy in copies:
        copy.wait()


def call(kernel, outs, scratch, *operands, scalars=(), far=(), manual=(), space=pltpu.VMEM):
    smem = pl.BlockSpec(memory_space=pltpu.SMEM)
    specs = [smem if i in scalars else pl.BlockSpec(memory_space=space) for i in range(len(operands))]
    if space == pltpu.HBM:
        operands = [pltpu.with_memory_space_constraint(a, space) for a in operands]
    return pl.pallas_call(
        kernel,
        out_shape=[(pltpu.HBM if i in far else pltpu.VMEM)(s, F32) for i, s in enumerate(outs)],
        in_specs=specs,
        out_specs=[pl.BlockSpec(memory_space=pltpu.HBM if i in manual else pltpu.VMEM) for i in range(len(outs))],
        scratch_shapes=[pltpu.VMEM(s, F32) if isinstance(s, tuple) else s for s in scratch],
        compiler_params=pltpu.CompilerParams(vmem_limit_bytes=VMEM_LIMIT),
    )(*operands)


def per_device(rhs, metric, wavenumber):
    sine, edge = jnp.asarray(sine_table()), jnp.asarray(edge_table())
    dft, table = jnp.asarray(dft_table()), jnp.asarray(wave_table())
    full, lines, side, bands = (ROWS, 8, COLS), (ROWS, 2, 8, COLS), (16, PITCH, 128), (BANDS, 8, COLS)
    solved, send, metrics, shift = call(
        local_kernel,
        [lines, (128, 128), (16, 128), (8, COLS)],
        [
            full, lines, side, side, (COLS, COLS), (5, 8, COLS), (8, 128),
            pltpu.SMEM((1024,), F32), pltpu.SMEM((8,), F32),
            pltpu.SemaphoreType.DMA((4,)), pltpu.SemaphoreType.DMA((5,)), pltpu.SemaphoreType.DMA((4,)),
        ],
        rhs.reshape(16, ROWS, COLS), metric, metric.reshape(8, 128), wavenumber, sine, edge,
        space=pltpu.HBM, far=(0, 1), manual=(0,),
    )
    recv = lax.all_to_all(send.reshape(8, 16, 128), "gx", 0, 0, tiled=True)
    (factor,) = call(
        factor_kernel,
        [(3 * ROWS + 2 * BANDS + 3, 8, COLS)],
        [bands, bands, bands],
        metrics.reshape(2048), shift,
        scalars=(0,),
    )
    send, own, column = call(
        spectrum_kernel,
        [(BANDS, 2, 8, COLS), (4, 8, COLS), (2, 8, 128)],
        [],
        recv.reshape(128, 128), factor, dft, table, jnp.asarray(octet_forward()),
        far=(0,),
    )
    recv = lax.all_to_all(send, "gy", 0, 0, tiled=True)
    total, local_ratio, coupling = call(
        column_kernel,
        [(2, 8, 128), full, full],
        [lines],
        column, factor, metric, wavenumber, edge,
        scalars=(2, 3),
    )
    (send,) = call(
        separator_kernel,
        [(128, 128)],
        [],
        recv, own, factor, total, dft, table, jnp.asarray(octet_inverse()),
    )
    recv = lax.all_to_all(send.reshape(8, 16, 128), "gx", 0, 0, tiled=True)
    (out,) = call(
        finish_kernel,
        [(16, ROWS, COLS)],
        [lines, side, side, pltpu.SemaphoreType.DMA((4,))],
        recv.reshape(128, 128), solved, local_ratio, coupling, sine, edge,
        far=(0,), manual=(0,),
    )
    return out.reshape(8, 2, ROWS, COLS)


def solution(mesh):
    placed = (P(None, None, "gy", "gx"), P(), P())
    return jax.shard_map(
        per_device, mesh=mesh, in_specs=placed, out_specs=P(None, None, "gy", "gx"), check_vma=False
    )
```

```python
import functools
import math

import jax
import jax.numpy as jnp
import numpy as np
from jax import lax
from jax.experimental import pallas as pl
from jax.experimental.pallas import tpu as pltpu
from jax.sharding import PartitionSpec as P


ASPECT = 0.02
STRIPS = 8
COLS = 256
ROWS = 64
BANDS = 16
PITCH = ROWS + 8
NX = STRIPS * COLS
VMEM_LIMIT = 16 * 1024 * 1024
F32 = jnp.float32


def f32(values):
    return np.asarray(values, np.float32)


def sine_table():
    ramp = np.arange(COLS)
    table = np.sin(np.pi * (np.outer(ramp, ramp) % (2 * COLS)) / COLS) * math.sqrt(2.0 / COLS)
    table[0, :] = 0.0
    table[:, 0] = 0.0
    table[0, 0] = 1.0
    return f32(table)


def edge_table():
    ramp = np.arange(COLS)
    left = np.sin(np.pi * ramp / COLS) * math.sqrt(2.0 / COLS)
    left[0] = 0.0
    along = 4.0 * np.sin(np.pi * ramp / (2 * COLS)) ** 2
    flip = np.where(ramp % 2 == 1, 1.0, -1.0)
    rows = [ASPECT * left, ASPECT * left * flip, ASPECT * along]
    kappa = np.arange(STRIPS)[:, None]
    whole = ASPECT * (2.0 * np.sin(np.pi * (STRIPS * ramp[None, :] + kappa) / NX)) ** 2
    return f32(np.stack([np.broadcast_to(r, (8, COLS)) for r in rows] + [whole, np.broadcast_to(flip, (8, COLS))]))


def dft_table():
    ramp = np.arange(COLS)
    angle = 2.0 * np.pi * (np.outer(ramp, ramp) % COLS) / COLS
    return f32(np.concatenate([np.cos(angle), np.sin(angle)], 1))


def wave_table():
    kappa = np.arange(STRIPS)[:, None]
    j = np.arange(COLS)[None, :]
    angle = 2.0 * np.pi * j * kappa / NX
    return f32(np.stack([np.cos(angle), np.sin(angle)]))


def octet_forward():
    ramp = np.arange(STRIPS)
    angle = 2.0 * np.pi * np.outer(ramp, ramp) / STRIPS
    c, s = np.cos(angle), np.sin(angle)
    return f32(np.block([[c, s], [-s, c]]))


def octet_inverse():
    ramp = np.arange(STRIPS)
    parts = []
    for offset in (0, 1):
        angle = 2.0 * np.pi * np.outer(ramp + offset, ramp) / STRIPS
        c, s = np.cos(angle), np.sin(angle)
        parts.append(np.block([[c, -s], [s, c]]))
    return f32(np.concatenate(parts, 0) / NX)


def dot(a, b):
    return jnp.dot(a, b, precision=lax.Precision.HIGHEST, preferred_element_type=F32)


def lane_ids():
    return lax.broadcasted_iota(jnp.int32, (8, 128), 1)


def wide(column):
    return jnp.broadcast_to(column, (8, 128))


def row_sum(values):
    return wide(jnp.sum(values[:, :128] + values[:, 128:], axis=1, keepdims=True))


def splat_inverse(metric_ref, row):
    return 1.0 / jnp.full((8, COLS), metric_ref[row], F32)


def local_shift(wave_ref, edge_ref):
    sub = lax.broadcasted_iota(jnp.int32, (8, COLS), 0)
    shift = edge_ref[2]
    for mode in range(8):
        shift = shift + jnp.where(sub == mode, wave_ref[mode], 0.0)
    return shift


def local_kernel(
    rhs_hbm, metric_hbm, tiled_hbm, wave_hbm, sine_hbm, edge_hbm, solved_hbm, send_ref, metrics_ref, shift_ref,
    ratio_ref, z_ref, r_lo, r_hi, sine_ref, edge_ref, metric_vec, metric_ref, wave_ref, rhs_sem, sems, out_sem,
):
    first = lax.axis_index("gy") * ROWS
    pairs = (
        (metric_hbm, metric_ref), (wave_hbm, wave_ref), (edge_hbm, edge_ref), (tiled_hbm, metric_vec), (sine_hbm, sine_ref)
    )
    small = [pltpu.make_async_copy(a, b, sems.at[i]) for i, (a, b) in enumerate(pairs)]
    half = ROWS // 2
    large = [
        pltpu.make_async_copy(
            rhs_hbm.at[:, pl.ds(part * half, half), pl.ds(side * 128, 128)],
            ref.at[:, pl.ds(part * half, half), :],
            rhs_sem.at[part * 2 + side],
        )
        for part in range(2)
        for side, ref in enumerate((r_lo, r_hi))
    ]
    for copy in small + large:
        copy.start()
    for copy in small[:4]:
        copy.wait()
    metrics_ref[:8, :] = metric_vec[...]
    metrics_ref[8:, :] = 1.0 / metric_vec[...]
    shift_ref[...] = edge_ref[3] + wave_ref[lax.axis_index("gx")]
    lanes = lane_ids()
    shift = local_shift(wave_ref, edge_ref)
    height = jnp.ones((8, COLS), F32)
    slope = jnp.ones((8, COLS), F32)
    for y in range(1, ROWS):
        slope = slope + shift * splat_inverse(metric_ref, first + y) * height
        taller = height + slope
        ratio_ref[y] = height / taller
        height = taller
    small[4].wait()
    sine = sine_ref[...]
    flat = [ref.reshape(16 * PITCH, 128) for ref in (r_lo, r_hi)]

    def line(y, c):
        rows = pl.ds(c * PITCH + y, 8, stride=2 * PITCH)
        return jnp.concatenate([ref[rows, :] for ref in flat], 1)

    state = [jnp.zeros((8, COLS), F32)] * 2
    group = 8
    for base in range(0, ROWS, group):
        if base % half == 0:
            for copy in large[base // half * 2 : base // half * 2 + 2]:
                copy.wait()
        lines = dot(jnp.concatenate([line(y, c) for y in range(base, base + group) for c in range(2)], 0), sine)
        for y in range(max(base, 1), base + group):
            ratio = ratio_ref[y]
            inverse = splat_inverse(metric_ref, first + y)
            for c in range(2):
                at = ((y - base) * 2 + c) * 8
                state[c] = (lines[at : at + 8] * inverse + state[c]) * ratio
                z_ref[y, c] = state[c]
    left = edge_ref[0]
    right = edge_ref[1]
    columns = [[jnp.zeros((8, 128), F32)] * 2 for _ in range(2)]
    upper = [jnp.zeros((8, COLS), F32)] * 2
    done = []
    for y in range(ROWS - 1, 0, -1):
        ratio = ratio_ref[y]
        inverse = splat_inverse(metric_ref, first + y)
        for c in range(2):
            upper[c] = z_ref[y, c] + ratio * upper[c]
            z_ref[y, c] = upper[c]
            a = upper[c] * left
            source = flat[0][pl.ds(c * PITCH + y, 8, stride=2 * PITCH), :]
            a = (a[:, :128] + a[:, 128:] + jnp.where(lanes == 0, source, 0.0)) * inverse[:, :128]
            b = upper[c] * right
            b = (b[:, :128] + b[:, 128:]) * inverse[:, :128]
            columns[0][c] = jnp.where(lanes == y, wide(jnp.sum(a, axis=1, keepdims=True)), columns[0][c])
            columns[1][c] = jnp.where(lanes == y + ROWS, wide(jnp.sum(b, axis=1, keepdims=True)), columns[1][c])
        if y % 16 == 0:
            done.append(pltpu.make_async_copy(z_ref.at[pl.ds(y, 16)], solved_hbm.at[pl.ds(y, 16)], out_sem.at[y // 16]))
            done[-1].start()
    z_ref[0] = jnp.zeros((2, 8, COLS), F32)
    done.append(pltpu.make_async_copy(z_ref.at[pl.ds(0, 16)], solved_hbm.at[pl.ds(0, 16)], out_sem.at[0]))
    done[-1].start()
    edges = jnp.concatenate([z_ref[y, c] for y in (1, ROWS - 1) for c in range(2)], 0)
    edges = dot(edges, sine)
    zero_lane = lax.broadcasted_iota(jnp.int32, (8, COLS), 1) == 0
    inverse = splat_inverse(metric_ref, first)
    for c in range(2):
        near = jnp.where(zero_lane, 0.0, edges[c * 8 : c * 8 + 8]) + line(0, c) * inverse
        far = jnp.where(zero_lane, 0.0, edges[16 + c * 8 : 24 + c * 8])
        for i in range(2):
            part = slice(i * 128, i * 128 + 128)
            send_ref[pl.ds(c * 2 + i, 8, stride=16), :] = near[:, part]
            send_ref[pl.ds(4 + c * 2 + i, 8, stride=16), :] = far[:, part]
        send_ref[pl.ds(8 + c, 8, stride=16), :] = jnp.where(lanes < ROWS, columns[0][c], columns[1][c])
        for pad in range(3):
            send_ref[pl.ds(10 + c * 3 + pad, 8, stride=16), :] = jnp.zeros((8, 128), F32)
    for copy in done:
        copy.wait()


def factors(ref):
    sizes = (ROWS, ROWS, BANDS, BANDS, 4)
    starts = np.cumsum((0,) + sizes)
    return [ref.at[pl.ds(int(a), n)] for a, n in zip(starts, sizes)]


def factor_kernel(metrics_ref, shift_ref, factor_ref, gamma_ref, base_ref, edge_ref, x_ref, above_ref, inverse_ref):
    over_ref, under_ref, up_ref, down_ref, final_ref = factors(factor_ref)
    mine = lax.axis_index("gy")
    shift = shift_ref[...]

    def excess(row):
        double = 2.0 * metrics_ref[row]
        return ((double + shift) - double) * metrics_ref[1024 + row]

    one = jnp.ones((8, COLS), F32)
    zero = jnp.zeros((8, COLS), F32)
    together = 4

    def bands(outer, _):
        state = [(one, one, zero, zero)] * together

        def rows(y, state):
            out = []
            for i in range(together):
                height, slope, rest, rise = state[i]
                t = excess((outer * together + i) * ROWS + y)
                slope = slope + t * height
                height = height + slope
                rise = rise + t * (rest + 1.0)
                rest = rest + rise
                out.append((height, slope, rest, rise))
            return tuple(out)

        state = lax.fori_loop(1, ROWS, rows, tuple(state), unroll=21)
        for i in range(together):
            height, slope, rest, _ = state[i]
            band = outer * together + i
            gamma = 1.0 / height
            gamma_ref[band] = gamma
            base_ref[band] = excess(band * ROWS) + rest * gamma
            edge_ref[band] = (slope - 1.0) * gamma
        return 0

    lax.fori_loop(0, BANDS // together, bands, 0)

    flow = one
    above, down, inverse = one, zero, zero
    height, slope = one, one
    rest, rise = one, one
    for y in range(1, ROWS + 1):
        if y < ROWS:
            under_ref[y] = height
            slope = slope + excess(mine * ROWS + y) * height
            height = height + slope
            over_ref[ROWS - y] = rest
            rise = rise + excess(mine * ROWS + ROWS - y) * rest
            rest = rest + rise
        if y % 4 == 0:
            band = y // 4 - 1
            x = base_ref[band] + flow
            if band:
                x = x + edge_ref[band - 1]
            x_ref[band] = x
            gamma = gamma_ref[band]
            up = gamma / (gamma + x)
            up_ref[band] = up
            flow = up * x
            band = BANDS - 1 - band
            above_ref[band], down_ref[band], inverse_ref[band] = above, down, inverse
            if band:
                x = base_ref[band] + edge_ref[band - 1] + gamma_ref[band] * above
                below = gamma_ref[band - 1]
                inverse = 1.0 / (below + x)
                down = below * inverse
                above = x * inverse
    gamma = gamma_ref[mine]
    final_ref[0] = down_ref[mine]
    final_ref[1] = inverse_ref[mine]
    final_ref[2] = 1.0 / (x_ref[mine] + gamma * above_ref[mine])
    final_ref[3] = gamma
    under_ref[0] = height


def spectrum_kernel(
    recv_ref, factor_ref, dft_ref, table_ref, octet_ref, send_ref, own_ref, column_ref
):
    over_ref, under_ref, up_ref, down_ref, final_ref = factors(factor_ref)
    mine = lax.axis_index("gy")

    def take(i):
        return recv_ref[pl.ds(i, 8, stride=16), :]

    pieces = [[], []]
    for c in range(2):
        for i in range(2):
            pieces[c].append(take(c * 2 + i))
        for i in range(2):
            pieces[c].append(take(4 + c * 2 + i))
        column = take(8 + c)
        pieces[c].append(column + pltpu.roll(pltpu.roll(column, 1, 0), ROWS, 1))
    stacked = jnp.concatenate([jnp.concatenate(pieces[0], 1), jnp.concatenate(pieces[1], 1)], 0)
    mixed = dot(octet_ref[...], stacked)
    cos, sin = table_ref[0], table_ref[1]
    turned = [[], []]
    for line in range(2):
        re = mixed[:8, line * COLS : line * COLS + COLS]
        im = mixed[8:, line * COLS : line * COLS + COLS]
        turned[0].append(re * cos + im * sin)
        turned[1].append(im * cos - re * sin)
    both = dot(jnp.concatenate(turned[0] + turned[1], 0), dft_ref[...])
    columns = [mixed[c * 8 : c * 8 + 8, 2 * COLS :] for c in range(2)]
    near = [jnp.zeros((8, COLS), F32)] * 2
    far = [jnp.zeros((8, COLS), F32)] * 2
    for y in range(1, ROWS):
        over, under = over_ref[y], under_ref[y]
        for c in range(2):
            source = wide(columns[c][:, y : y + 1])
            source = jnp.concatenate([source, source], 1)
            near[c] = near[c] + over * source
            far[c] = far[c] + under * source
    gamma = final_ref[3]
    sides = []
    for line, extra in enumerate((near, far)):
        re_cos = both[line * 8 : line * 8 + 8, :COLS]
        re_sin = both[line * 8 : line * 8 + 8, COLS:]
        im_cos = both[16 + line * 8 : 24 + line * 8, :COLS]
        im_sin = both[16 + line * 8 : 24 + line * 8, COLS:]
        sides.append((re_cos + im_sin + extra[0] * gamma, im_cos - re_sin + extra[1] * gamma))
    for c in range(2):
        own_ref[c], own_ref[2 + c] = sides[0][c], sides[1][c]
        column_ref[c] = columns[c]
        send_ref[mine, c] = jnp.zeros((8, COLS), F32)
    up, down = up_ref[mine], down_ref[mine]

    def above(band, carry):
        factor = up_ref[band]
        for c in range(2):
            send_ref[band, c] = carry[c]
        return tuple(value * factor for value in carry)

    def below(step, carry):
        band = mine - 1 - step
        factor = down_ref[band]
        for c in range(2):
            send_ref[band, c] = carry[c]
        return tuple(value * factor for value in carry)

    lax.fori_loop(mine + 1, BANDS, above, tuple(sides[1][c] + up * sides[0][c] for c in range(2)))
    lax.fori_loop(0, mine, below, tuple(sides[0][c] + down * sides[1][c] for c in range(2)))


def column_kernel(column_ref, factor_ref, metric_ref, wave_ref, edge_ref, out_ref, z_ref, ratio_ref):
    under_ref = factors(factor_ref)[1]
    first = lax.axis_index("gy") * ROWS
    shift = local_shift(wave_ref, edge_ref)
    height = jnp.ones((8, COLS), F32)
    slope = jnp.ones((8, COLS), F32)
    for y in range(1, ROWS):
        inverse = splat_inverse(metric_ref, first + y)
        out_ref[ROWS + y] = edge_ref[0] * inverse
        slope = slope + shift * inverse * height
        taller = height + slope
        out_ref[y] = height / taller
        height = taller
    lanes = lane_ids()
    columns = [column_ref[c] for c in range(2)]
    state = [jnp.zeros((8, COLS), F32)] * 2
    for y in range(1, ROWS):
        ratio = under_ref[y] / under_ref[(y + 1) % ROWS]
        ratio_ref[y] = ratio
        for c in range(2):
            source = wide(columns[c][:, y : y + 1])
            state[c] = (jnp.concatenate([source, source], 1) + state[c]) * ratio
            z_ref[y, c] = state[c]
    upper = [jnp.zeros((8, COLS), F32)] * 2
    total = [jnp.zeros((8, 128), F32)] * 2
    for y in range(ROWS - 1, 0, -1):
        ratio = ratio_ref[y]
        for c in range(2):
            upper[c] = z_ref[y, c] + ratio * upper[c]
            total[c] = jnp.where(lanes == y, row_sum(upper[c]), total[c])
    out_ref[0] = jnp.concatenate(total, 1)


def separator_kernel(
    recv_ref, own_ref, factor_ref, local_ref, dft_ref, table_ref, octet_ref, send_ref
):
    over_ref, under_ref, _, _, final_ref = factors(factor_ref)
    mine = lax.axis_index("gy")
    from_below = [own_ref[c] for c in range(2)]
    from_above = [own_ref[2 + c] for c in range(2)]
    for band in range(BANDS):
        for c in range(2):
            value = recv_ref[band, c]
            from_below[c] = from_below[c] + jnp.where(band < mine, value, 0.0)
            from_above[c] = from_above[c] + jnp.where(band > mine, value, 0.0)
    down, inverse, pivot = final_ref[0], final_ref[1], final_ref[2]
    near = [(from_below[c] + down * from_above[c]) * pivot for c in range(2)]
    far = [from_above[c] * inverse + down * near[c] for c in range(2)]
    lanes = lane_ids()
    both = dot(jnp.concatenate([near[0], far[0], near[1], far[1]], 0), dft_ref[...])
    total = [local_ref[0, :, c * 128 : c * 128 + 128] for c in range(2)]
    gamma = final_ref[3]
    near = [value * gamma for value in near]
    far = [value * gamma for value in far]
    for y in range(1, ROWS):
        over, under = over_ref[y], under_ref[y]
        for c in range(2):
            extra = row_sum(over * near[c] + under * far[c])
            total[c] = total[c] + jnp.where(lanes == y, extra, 0.0)
    cos, sin = table_ref[0], table_ref[1]
    turned = [[], []]
    for line in range(2):
        re_cos = both[line * 8 : line * 8 + 8, :COLS]
        re_sin = both[line * 8 : line * 8 + 8, COLS:]
        im_cos = both[16 + line * 8 : 24 + line * 8, :COLS]
        im_sin = both[16 + line * 8 : 24 + line * 8, COLS:]
        re = re_cos - im_sin
        im = re_sin + im_cos
        turned[0].append(re * cos - im * sin)
        turned[1].append(re * sin + im * cos)
    stacked = [jnp.concatenate(turned[c] + [total[c]], 1) for c in range(2)]
    out = dot(octet_ref[...], jnp.concatenate(stacked, 0))
    for c in range(2):
        for i in range(4):
            row = (i // 2) * 4 + c * 2 + i % 2
            send_ref[pl.ds(row, 8, stride=16), :] = out[c * 8 : c * 8 + 8, i * 128 : i * 128 + 128]
        here = out[c * 8 : c * 8 + 8, 2 * COLS :]
        there = out[16 + c * 8 : 24 + c * 8, 2 * COLS :]
        send_ref[pl.ds(8 + c, 8, stride=16), :] = jnp.where(lanes < ROWS, here, pltpu.roll(there, ROWS, 1))
        for pad in range(3):
            send_ref[pl.ds(10 + c * 3 + pad, 8, stride=16), :] = jnp.zeros((8, 128), F32)


def finish_kernel(recv_ref, solved_ref, local_ref, sine_ref, edge_ref, out_hbm, z_ref, o_lo, o_hi, sems):
    def take(i):
        return recv_ref[pl.ds(i, 8, stride=16), :]

    sine = sine_ref[...]
    near = [jnp.concatenate([take(c * 2), take(c * 2 + 1)], 1) for c in range(2)]
    far = [jnp.concatenate([take(4 + c * 2), take(5 + c * 2)], 1) for c in range(2)]
    columns = [take(8 + c) for c in range(2)]
    edges = dot(jnp.concatenate(near + far, 0), sine)
    flip = edge_ref[4]
    zero_lane = lax.broadcasted_iota(jnp.int32, (8, COLS), 1) == 0
    state = [edges[c * 8 : c * 8 + 8] for c in range(2)]
    for y in range(1, ROWS):
        ratio = local_ref[y]
        coupling = local_ref[ROWS + y]
        for c in range(2):
            here = wide(columns[c][:, y : y + 1])
            there = wide(columns[c][:, ROWS + y : ROWS + y + 1])
            here = jnp.concatenate([here, here], 1)
            there = jnp.concatenate([there, there], 1)
            state[c] = (state[c] + coupling * (here + flip * there)) * ratio
            z_ref[y, c] = state[c]
    upper = [edges[16 + c * 8 : 24 + c * 8] for c in range(2)]
    flat = [ref.reshape(16 * PITCH, 128) for ref in (o_lo, o_hi)]
    group, half = 8, ROWS // 2
    copies = []
    for base in range(ROWS - group, -1, -group):
        lines = []
        for y in range(base + group - 1, base - 1, -1):
            for c in range(2):
                if y:
                    upper[c] = z_ref[y, c] + local_ref[y] * upper[c]
                    here = wide(columns[c][:, y : y + 1])
                    here = jnp.concatenate([here, here], 1)
                    lines.append(jnp.where(zero_lane, here, upper[c] + solved_ref[y, c]))
                else:
                    lines.append(edges[c * 8 : c * 8 + 8])
        product = dot(jnp.concatenate(lines, 0), sine)
        for i in range(2 * group):
            rows = pl.ds(i % 2 * PITCH + base + group - 1 - i // 2, 8, stride=2 * PITCH)
            flat[0][rows, :] = product[i * 8 : i * 8 + 8, :128]
            flat[1][rows, :] = product[i * 8 : i * 8 + 8, 128:]
        if base % half == 0:
            for side, ref in enumerate((o_lo, o_hi)):
                copies.append(
                    pltpu.make_async_copy(
                        ref.at[:, pl.ds(base, half), :],
                        out_hbm.at[:, pl.ds(base, half), pl.ds(side * 128, 128)],
                        sems.at[len(copies)],
                    )
                )
                copies[-1].start()
    for copy in copies:
        copy.wait()


def call(kernel, outs, scratch, *operands, scalars=(), far=(), manual=(), space=pltpu.VMEM):
    places = [pltpu.SMEM if i in scalars else space for i in range(len(operands))]
    if space == pltpu.HBM:
        operands = [pltpu.with_memory_space_constraint(a, space) for a in operands]
    return pl.pallas_call(
        kernel,
        out_shape=[(pltpu.HBM if i in far else pltpu.VMEM)(s, F32) for i, s in enumerate(outs)],
        in_specs=[pl.BlockSpec(memory_space=place) for place in places],
        out_specs=[pl.BlockSpec(memory_space=pltpu.HBM if i in manual else pltpu.VMEM) for i in range(len(outs))],
        scratch_shapes=[pltpu.VMEM(s, F32) if isinstance(s, tuple) else s for s in scratch],
        compiler_params=pltpu.CompilerParams(vmem_limit_bytes=VMEM_LIMIT),
    )(*operands)


def per_device(rhs, metric, wavenumber):
    sine, edge = jnp.asarray(sine_table()), jnp.asarray(edge_table())
    dft, table = jnp.asarray(dft_table()), jnp.asarray(wave_table())
    full, lines, side, bands = (ROWS, 8, COLS), (ROWS, 2, 8, COLS), (16, PITCH, 128), (BANDS, 8, COLS)
    solved, send, metrics, shift = call(
        local_kernel,
        [lines, (128, 128), (16, 128), (8, COLS)],
        [
            full, lines, side, side, (COLS, COLS), (5, 8, COLS), (8, 128),
            pltpu.SMEM((1024,), F32), pltpu.SMEM((8,), F32),
            pltpu.SemaphoreType.DMA((4,)), pltpu.SemaphoreType.DMA((5,)), pltpu.SemaphoreType.DMA((4,)),
        ],
        rhs.reshape(16, ROWS, COLS), metric, metric.reshape(8, 128), wavenumber, sine, edge,
        space=pltpu.HBM, far=(0, 1), manual=(0,),
    )
    recv = lax.all_to_all(send.reshape(8, 16, 128), "gx", 0, 0, tiled=True)
    (factor,) = call(
        factor_kernel,
        [(2 * ROWS + 2 * BANDS + 4, 8, COLS)],
        [bands] * 6,
        metrics.reshape(2048), shift,
        scalars=(0,),
    )
    send, own, column = call(
        spectrum_kernel,
        [(BANDS, 2, 8, COLS), (4, 8, COLS), (2, 8, 128)],
        [],
        recv.reshape(128, 128), factor, dft, table, jnp.asarray(octet_forward()),
        far=(0,),
    )
    recv = lax.all_to_all(send, "gy", 0, 0, tiled=True)
    (local,) = call(
        column_kernel,
        [(2 * ROWS, 8, COLS)],
        [lines, full],
        column, factor, metric, wavenumber, edge,
        scalars=(2, 3),
    )
    (send,) = call(
        separator_kernel,
        [(128, 128)],
        [],
        recv, own, factor, local, dft, table, jnp.asarray(octet_inverse()),
    )
    recv = lax.all_to_all(send.reshape(8, 16, 128), "gx", 0, 0, tiled=True)
    (out,) = call(
        finish_kernel,
        [(16, ROWS, COLS)],
        [lines, side, side, pltpu.SemaphoreType.DMA((4,))],
        recv.reshape(128, 128), solved, local, sine, edge,
        far=(0,), manual=(0,),
    )
    return out.reshape(8, 2, ROWS, COLS)


def solution(mesh):
    placed = (P(None, None, "gy", "gx"), P(), P())
    return jax.shard_map(
        per_device, mesh=mesh, in_specs=placed, out_specs=P(None, None, "gy", "gx"), check_vma=False
    )
```

```python
import functools
import math

import jax
import jax.numpy as jnp
import numpy as np
from jax import lax
from jax.experimental import pallas as pl
from jax.experimental.pallas import tpu as pltpu
from jax.sharding import PartitionSpec as P


ASPECT = 0.02
STRIPS = 8
COLS = 256
ROWS = 64
BANDS = 16
PITCH = ROWS + 8
NX = STRIPS * COLS
VMEM_LIMIT = 16 * 1024 * 1024
F32 = jnp.float32


def f32(values):
    return np.asarray(values, np.float32)


def sine_table():
    ramp = np.arange(COLS)
    table = np.sin(np.pi * (np.outer(ramp, ramp) % (2 * COLS)) / COLS) * math.sqrt(2.0 / COLS)
    table[0, :] = 0.0
    table[:, 0] = 0.0
    table[0, 0] = 1.0
    return f32(table)


def edge_table():
    ramp = np.arange(COLS)
    left = np.sin(np.pi * ramp / COLS) * math.sqrt(2.0 / COLS)
    left[0] = 0.0
    along = 4.0 * np.sin(np.pi * ramp / (2 * COLS)) ** 2
    flip = np.where(ramp % 2 == 1, 1.0, -1.0)
    rows = [ASPECT * left, ASPECT * left * flip, ASPECT * along]
    kappa = np.arange(STRIPS)[:, None]
    whole = ASPECT * (2.0 * np.sin(np.pi * (STRIPS * ramp[None, :] + kappa) / NX)) ** 2
    return f32(np.stack([np.broadcast_to(r, (8, COLS)) for r in rows] + [whole, np.broadcast_to(flip, (8, COLS))]))


def dft_table():
    ramp = np.arange(COLS)
    angle = 2.0 * np.pi * (np.outer(ramp, ramp) % COLS) / COLS
    return f32(np.concatenate([np.cos(angle), np.sin(angle)], 1))


def wave_table():
    kappa = np.arange(STRIPS)[:, None]
    j = np.arange(COLS)[None, :]
    angle = 2.0 * np.pi * j * kappa / NX
    return f32(np.stack([np.cos(angle), np.sin(angle)]))


def octet_forward():
    ramp = np.arange(STRIPS)
    angle = 2.0 * np.pi * np.outer(ramp, ramp) / STRIPS
    c, s = np.cos(angle), np.sin(angle)
    return f32(np.block([[c, s], [-s, c]]))


def octet_inverse():
    ramp = np.arange(STRIPS)
    parts = []
    for offset in (0, 1):
        angle = 2.0 * np.pi * np.outer(ramp + offset, ramp) / STRIPS
        c, s = np.cos(angle), np.sin(angle)
        parts.append(np.block([[c, -s], [s, c]]))
    return f32(np.concatenate(parts, 0) / NX)


def dot(a, b):
    return jnp.dot(a, b, precision=lax.Precision.HIGHEST, preferred_element_type=F32)


def lane_ids():
    return lax.broadcasted_iota(jnp.int32, (8, 128), 1)


def wide(column):
    return jnp.broadcast_to(column, (8, 128))


def row_sum(values):
    return wide(jnp.sum(values[:, :128] + values[:, 128:], axis=1, keepdims=True))


def splat_inverse(metric_ref, row):
    return 1.0 / jnp.full((8, COLS), metric_ref[row], F32)


def local_shift(wave_ref, edge_ref):
    sub = lax.broadcasted_iota(jnp.int32, (8, COLS), 0)
    shift = edge_ref[2]
    for mode in range(8):
        shift = shift + jnp.where(sub == mode, wave_ref[mode], 0.0)
    return shift


def local_kernel(
    rhs_hbm, metric_hbm, tiled_hbm, wave_hbm, sine_hbm, edge_hbm, solved_hbm, send_hbm, metrics_hbm, shift_hbm,
    metrics_ref, shift_ref, send_ref, ratio_ref, z_ref, r_lo, r_hi, sine_ref, edge_ref, metric_vec, metric_ref, wave_ref, rhs_sem, sems, out_sem,
):
    first = lax.axis_index("gy") * ROWS
    pairs = (
        (metric_hbm, metric_ref), (wave_hbm, wave_ref), (edge_hbm, edge_ref), (tiled_hbm, metric_vec), (sine_hbm, sine_ref)
    )
    small = [pltpu.make_async_copy(a, b, sems.at[i]) for i, (a, b) in enumerate(pairs)]
    half = ROWS // 2
    large = [
        pltpu.make_async_copy(
            rhs_hbm.at[:, pl.ds(part * half, half), pl.ds(side * 128, 128)],
            ref.at[:, pl.ds(part * half, half), :],
            rhs_sem.at[part * 2 + side],
        )
        for part in range(2)
        for side, ref in enumerate((r_lo, r_hi))
    ]
    for copy in small + large:
        copy.start()
    for copy in small[:4]:
        copy.wait()
    metrics_ref[:8, :] = metric_vec[...]
    metrics_ref[8:, :] = 1.0 / metric_vec[...]
    shift = local_shift(wave_ref, edge_ref)
    shift_ref[0] = edge_ref[3] + wave_ref[lax.axis_index("gx")]
    shift_ref[1] = shift
    shift_ref[2] = edge_ref[0]
    done = [
        pltpu.make_async_copy(metrics_ref, metrics_hbm, sems.at[1]), pltpu.make_async_copy(shift_ref, shift_hbm, sems.at[2])
    ]
    for copy in done:
        copy.start()
    lanes = lane_ids()
    height = jnp.ones((8, COLS), F32)
    slope = jnp.ones((8, COLS), F32)
    for y in range(1, ROWS):
        slope = slope + shift * splat_inverse(metric_ref, first + y) * height
        taller = height + slope
        ratio_ref[y] = height / taller
        height = taller
    small[4].wait()
    sine = sine_ref[...]
    flat = [ref.reshape(16 * PITCH, 128) for ref in (r_lo, r_hi)]

    def line(y, c):
        rows = pl.ds(c * PITCH + y, 8, stride=2 * PITCH)
        return jnp.concatenate([ref[rows, :] for ref in flat], 1)

    state = [jnp.zeros((8, COLS), F32)] * 2
    group = 8
    for base in range(0, ROWS, group):
        if base % half == 0:
            for copy in large[base // half * 2 : base // half * 2 + 2]:
                copy.wait()
        lines = dot(jnp.concatenate([line(y, c) for y in range(base, base + group) for c in range(2)], 0), sine)
        for y in range(max(base, 1), base + group):
            ratio = ratio_ref[y]
            inverse = splat_inverse(metric_ref, first + y)
            for c in range(2):
                at = ((y - base) * 2 + c) * 8
                state[c] = (lines[at : at + 8] * inverse + state[c]) * ratio
                z_ref[y, c] = state[c]
    left = edge_ref[0]
    right = edge_ref[1]
    columns = [[jnp.zeros((8, 128), F32)] * 2 for _ in range(2)]
    upper = [jnp.zeros((8, COLS), F32)] * 2
    for y in range(ROWS - 1, 0, -1):
        ratio = ratio_ref[y]
        inverse = splat_inverse(metric_ref, first + y)
        for c in range(2):
            upper[c] = z_ref[y, c] + ratio * upper[c]
            z_ref[y, c] = upper[c]
            a = upper[c] * left
            source = flat[0][pl.ds(c * PITCH + y, 8, stride=2 * PITCH), :]
            a = (a[:, :128] + a[:, 128:] + jnp.where(lanes == 0, source, 0.0)) * inverse[:, :128]
            b = upper[c] * right
            b = (b[:, :128] + b[:, 128:]) * inverse[:, :128]
            columns[0][c] = jnp.where(lanes == y, wide(jnp.sum(a, axis=1, keepdims=True)), columns[0][c])
            columns[1][c] = jnp.where(lanes == y + ROWS, wide(jnp.sum(b, axis=1, keepdims=True)), columns[1][c])
        if y % 16 == 0:
            done.append(pltpu.make_async_copy(z_ref.at[pl.ds(y, 16)], solved_hbm.at[pl.ds(y, 16)], out_sem.at[y // 16]))
            done[-1].start()
    z_ref[0] = jnp.zeros((2, 8, COLS), F32)
    done.append(pltpu.make_async_copy(z_ref.at[pl.ds(0, 16)], solved_hbm.at[pl.ds(0, 16)], out_sem.at[0]))
    done[-1].start()
    edges = jnp.concatenate([z_ref[y, c] for y in (1, ROWS - 1) for c in range(2)], 0)
    edges = dot(edges, sine)
    zero_lane = lax.broadcasted_iota(jnp.int32, (8, COLS), 1) == 0
    inverse = splat_inverse(metric_ref, first)
    for c in range(2):
        near = jnp.where(zero_lane, 0.0, edges[c * 8 : c * 8 + 8]) + line(0, c) * inverse
        far = jnp.where(zero_lane, 0.0, edges[16 + c * 8 : 24 + c * 8])
        for i in range(2):
            part = slice(i * 128, i * 128 + 128)
            send_ref[pl.ds(c * 2 + i, 8, stride=16), :] = near[:, part]
            send_ref[pl.ds(4 + c * 2 + i, 8, stride=16), :] = far[:, part]
        send_ref[pl.ds(8 + c, 8, stride=16), :] = jnp.where(lanes < ROWS, columns[0][c], columns[1][c])
        for pad in range(3):
            send_ref[pl.ds(10 + c * 3 + pad, 8, stride=16), :] = jnp.zeros((8, 128), F32)
    done.append(pltpu.make_async_copy(send_ref, send_hbm, sems.at[0]))
    done[-1].start()
    for copy in done:
        copy.wait()


def factors(ref):
    sizes = (ROWS, ROWS, ROWS, BANDS, BANDS, 4, ROWS, ROWS)
    starts = np.cumsum((0,) + sizes)
    return [ref.at[pl.ds(int(a), n)] for a, n in zip(starts, sizes)]


def factor_kernel(
    metrics_hbm, shift_hbm, factor_ref,
    gamma_ref, base_ref, edge_ref, x_ref, above_ref, inverse_ref, metrics_ref, shift_ref, sems,
):
    copies = [
        pltpu.make_async_copy(metrics_hbm, metrics_ref, sems.at[0]), pltpu.make_async_copy(shift_hbm, shift_ref, sems.at[1])
    ]
    for copy in copies:
        copy.start()
    for copy in copies:
        copy.wait()
    over_ref, under_ref, ratio_ref, up_ref, down_ref, final_ref, local_ref, coupling_ref = factors(factor_ref)
    mine = lax.axis_index("gy")
    shift = shift_ref[0]

    def excess(row):
        double = 2.0 * metrics_ref[row]
        return ((double + shift) - double) * metrics_ref[1024 + row]

    one = jnp.ones((8, COLS), F32)
    zero = jnp.zeros((8, COLS), F32)
    together = 4

    def bands(outer, _):
        state = [(one, one, zero, zero)] * together

        def rows(y, state):
            out = []
            for i in range(together):
                height, slope, rest, rise = state[i]
                t = excess((outer * together + i) * ROWS + y)
                slope = slope + t * height
                height = height + slope
                rise = rise + t * (rest + 1.0)
                rest = rest + rise
                out.append((height, slope, rest, rise))
            return tuple(out)

        state = lax.fori_loop(1, ROWS, rows, tuple(state), unroll=21)
        for i in range(together):
            height, slope, rest, _ = state[i]
            band = outer * together + i
            gamma = 1.0 / height
            gamma_ref[band] = gamma
            base_ref[band] = excess(band * ROWS) + rest * gamma
            edge_ref[band] = (slope - 1.0) * gamma
        return 0

    lax.fori_loop(0, BANDS // together, bands, 0)

    flow = one
    above, down, inverse = one, zero, zero
    height, slope = one, one
    rest, rise = one, one
    near, near_slope = one, one
    for y in range(1, ROWS + 1):
        if y < ROWS:
            under_ref[y] = height
            slope = slope + excess(mine * ROWS + y) * height
            taller = height + slope
            ratio_ref[y] = height / taller
            height = taller
            inverse_metric = metrics_ref[1024 + mine * ROWS + y]
            coupling_ref[y] = shift_ref[2] * inverse_metric
            near_slope = near_slope + shift_ref[1] * inverse_metric * near
            taller = near + near_slope
            local_ref[y] = near / taller
            near = taller
            over_ref[ROWS - y] = rest
            rise = rise + excess(mine * ROWS + ROWS - y) * rest
            rest = rest + rise
        if y % 4 == 0:
            band = y // 4 - 1
            x = base_ref[band] + flow
            if band:
                x = x + edge_ref[band - 1]
            x_ref[band] = x
            gamma = gamma_ref[band]
            up = gamma / (gamma + x)
            up_ref[band] = up
            flow = up * x
            band = BANDS - 1 - band
            above_ref[band], down_ref[band], inverse_ref[band] = above, down, inverse
            if band:
                x = base_ref[band] + edge_ref[band - 1] + gamma_ref[band] * above
                below = gamma_ref[band - 1]
                inverse = 1.0 / (below + x)
                down = below * inverse
                above = x * inverse
    gamma = gamma_ref[mine]
    final_ref[0] = down_ref[mine]
    final_ref[1] = inverse_ref[mine]
    final_ref[2] = 1.0 / (x_ref[mine] + gamma * above_ref[mine])
    final_ref[3] = gamma


def spectrum_kernel(
    recv_ref, factor_ref, dft_ref, table_ref, octet_ref, send_ref, own_ref, z_ref
):
    _, _, ratio_ref, up_ref, down_ref, _, _, _ = factors(factor_ref)
    mine = lax.axis_index("gy")

    def take(i):
        return recv_ref[pl.ds(i, 8, stride=16), :]

    pieces = [[], []]
    for c in range(2):
        for i in range(2):
            pieces[c].append(take(c * 2 + i))
        for i in range(2):
            pieces[c].append(take(4 + c * 2 + i))
        column = take(8 + c)
        pieces[c].append(column + pltpu.roll(pltpu.roll(column, 1, 0), ROWS, 1))
    stacked = jnp.concatenate([jnp.concatenate(pieces[0], 1), jnp.concatenate(pieces[1], 1)], 0)
    mixed = dot(octet_ref[...], stacked)
    cos, sin = table_ref[0], table_ref[1]
    turned = [[], []]
    for line in range(2):
        re = mixed[:8, line * COLS : line * COLS + COLS]
        im = mixed[8:, line * COLS : line * COLS + COLS]
        turned[0].append(re * cos + im * sin)
        turned[1].append(im * cos - re * sin)
    both = dot(jnp.concatenate(turned[0] + turned[1], 0), dft_ref[...])
    columns = [mixed[c * 8 : c * 8 + 8, 2 * COLS :] for c in range(2)]
    lanes = lane_ids()
    state = [jnp.zeros((8, COLS), F32)] * 2
    for y in range(1, ROWS):
        ratio = ratio_ref[y]
        for c in range(2):
            source = wide(columns[c][:, y : y + 1])
            state[c] = (jnp.concatenate([source, source], 1) + state[c]) * ratio
            z_ref[y, c] = state[c]
    upper = [jnp.zeros((8, COLS), F32)] * 2
    total = [jnp.zeros((8, 128), F32)] * 2
    for y in range(ROWS - 1, 0, -1):
        ratio = ratio_ref[y]
        for c in range(2):
            upper[c] = z_ref[y, c] + ratio * upper[c]
            total[c] = jnp.where(lanes == y, row_sum(upper[c]), total[c])
    sides = []
    for line, extra in enumerate((upper, state)):
        re_cos = both[line * 8 : line * 8 + 8, :COLS]
        re_sin = both[line * 8 : line * 8 + 8, COLS:]
        im_cos = both[16 + line * 8 : 24 + line * 8, :COLS]
        im_sin = both[16 + line * 8 : 24 + line * 8, COLS:]
        sides.append((re_cos + im_sin + extra[0], im_cos - re_sin + extra[1]))
    for c in range(2):
        own_ref[c], own_ref[2 + c] = sides[0][c], sides[1][c]
        send_ref[mine, c] = jnp.zeros((8, COLS), F32)
    own_ref[4] = jnp.concatenate(total, 1)
    up, down = up_ref[mine], down_ref[mine]

    def above(band, carry):
        factor = up_ref[band]
        for c in range(2):
            send_ref[band, c] = carry[c]
        return tuple(value * factor for value in carry)

    def below(step, carry):
        band = mine - 1 - step
        factor = down_ref[band]
        for c in range(2):
            send_ref[band, c] = carry[c]
        return tuple(value * factor for value in carry)

    lax.fori_loop(mine + 1, BANDS, above, tuple(sides[1][c] + up * sides[0][c] for c in range(2)))
    lax.fori_loop(0, mine, below, tuple(sides[0][c] + down * sides[1][c] for c in range(2)))


def separator_kernel(
    recv_ref, own_ref, factor_ref, dft_ref, table_ref, octet_ref, send_ref
):
    over_ref, under_ref, _, _, _, final_ref, _, _ = factors(factor_ref)
    mine = lax.axis_index("gy")
    from_below = [own_ref[c] for c in range(2)]
    from_above = [own_ref[2 + c] for c in range(2)]
    for band in range(BANDS):
        for c in range(2):
            value = recv_ref[band, c]
            from_below[c] = from_below[c] + jnp.where(band < mine, value, 0.0)
            from_above[c] = from_above[c] + jnp.where(band > mine, value, 0.0)
    down, inverse, pivot = final_ref[0], final_ref[1], final_ref[2]
    near = [(from_below[c] + down * from_above[c]) * pivot for c in range(2)]
    far = [from_above[c] * inverse + down * near[c] for c in range(2)]
    lanes = lane_ids()
    both = dot(jnp.concatenate([near[0], far[0], near[1], far[1]], 0), dft_ref[...])
    total = [own_ref[4, :, c * 128 : c * 128 + 128] for c in range(2)]
    gamma = final_ref[3]
    near = [value * gamma for value in near]
    far = [value * gamma for value in far]
    for y in range(1, ROWS):
        over, under = over_ref[y], under_ref[y]
        for c in range(2):
            extra = row_sum(over * near[c] + under * far[c])
            total[c] = total[c] + jnp.where(lanes == y, extra, 0.0)
    cos, sin = table_ref[0], table_ref[1]
    turned = [[], []]
    for line in range(2):
        re_cos = both[line * 8 : line * 8 + 8, :COLS]
        re_sin = both[line * 8 : line * 8 + 8, COLS:]
        im_cos = both[16 + line * 8 : 24 + line * 8, :COLS]
        im_sin = both[16 + line * 8 : 24 + line * 8, COLS:]
        re = re_cos - im_sin
        im = re_sin + im_cos
        turned[0].append(re * cos - im * sin)
        turned[1].append(re * sin + im * cos)
    stacked = [jnp.concatenate(turned[c] + [total[c]], 1) for c in range(2)]
    out = dot(octet_ref[...], jnp.concatenate(stacked, 0))
    for c in range(2):
        for i in range(4):
            row = (i // 2) * 4 + c * 2 + i % 2
            send_ref[pl.ds(row, 8, stride=16), :] = out[c * 8 : c * 8 + 8, i * 128 : i * 128 + 128]
        here = out[c * 8 : c * 8 + 8, 2 * COLS :]
        there = out[16 + c * 8 : 24 + c * 8, 2 * COLS :]
        send_ref[pl.ds(8 + c, 8, stride=16), :] = jnp.where(lanes < ROWS, here, pltpu.roll(there, ROWS, 1))
        for pad in range(3):
            send_ref[pl.ds(10 + c * 3 + pad, 8, stride=16), :] = jnp.zeros((8, 128), F32)


def finish_kernel(recv_ref, solved_ref, factor_ref, sine_ref, edge_ref, out_hbm, z_ref, o_lo, o_hi, sems):
    local_ref, coupling_ref = factors(factor_ref)[6:]
    def take(i):
        return recv_ref[pl.ds(i, 8, stride=16), :]

    sine = sine_ref[...]
    near = [jnp.concatenate([take(c * 2), take(c * 2 + 1)], 1) for c in range(2)]
    far = [jnp.concatenate([take(4 + c * 2), take(5 + c * 2)], 1) for c in range(2)]
    columns = [take(8 + c) for c in range(2)]
    edges = dot(jnp.concatenate(near + far, 0), sine)
    flip = edge_ref[4]
    zero_lane = lax.broadcasted_iota(jnp.int32, (8, COLS), 1) == 0
    state = [edges[c * 8 : c * 8 + 8] for c in range(2)]
    for y in range(1, ROWS):
        ratio = local_ref[y]
        coupling = coupling_ref[y]
        for c in range(2):
            here = wide(columns[c][:, y : y + 1])
            there = wide(columns[c][:, ROWS + y : ROWS + y + 1])
            here = jnp.concatenate([here, here], 1)
            there = jnp.concatenate([there, there], 1)
            state[c] = (state[c] + coupling * (here + flip * there)) * ratio
            z_ref[y, c] = state[c]
    upper = [edges[16 + c * 8 : 24 + c * 8] for c in range(2)]
    flat = [ref.reshape(16 * PITCH, 128) for ref in (o_lo, o_hi)]
    group, half = 8, ROWS // 2
    copies = []
    for base in range(ROWS - group, -1, -group):
        lines = []
        for y in range(base + group - 1, base - 1, -1):
            for c in range(2):
                if y:
                    upper[c] = z_ref[y, c] + local_ref[y] * upper[c]
                    here = wide(columns[c][:, y : y + 1])
                    here = jnp.concatenate([here, here], 1)
                    lines.append(jnp.where(zero_lane, here, upper[c] + solved_ref[y, c]))
                else:
                    lines.append(edges[c * 8 : c * 8 + 8])
        product = dot(jnp.concatenate(lines, 0), sine)
        for i in range(2 * group):
            rows = pl.ds(i % 2 * PITCH + base + group - 1 - i // 2, 8, stride=2 * PITCH)
            flat[0][rows, :] = product[i * 8 : i * 8 + 8, :128]
            flat[1][rows, :] = product[i * 8 : i * 8 + 8, 128:]
        if base % half == 0:
            for side, ref in enumerate((o_lo, o_hi)):
                copies.append(
                    pltpu.make_async_copy(
                        ref.at[:, pl.ds(base, half), :],
                        out_hbm.at[:, pl.ds(base, half), pl.ds(side * 128, 128)],
                        sems.at[len(copies)],
                    )
                )
                copies[-1].start()
    for copy in copies:
        copy.wait()


def call(kernel, outs, scratch, *operands, scalars=(), far=(), manual=(), space=pltpu.VMEM):
    places = [pltpu.SMEM if i in scalars else space for i in range(len(operands))]
    if space == pltpu.HBM:
        operands = [pltpu.with_memory_space_constraint(a, space) for a in operands]
    return pl.pallas_call(
        kernel,
        out_shape=[(pltpu.HBM if i in far else pltpu.VMEM)(s, F32) for i, s in enumerate(outs)],
        in_specs=[pl.BlockSpec(memory_space=place) for place in places],
        out_specs=[pl.BlockSpec(memory_space=pltpu.HBM if i in manual else pltpu.VMEM) for i in range(len(outs))],
        scratch_shapes=[pltpu.VMEM(s, F32) if isinstance(s, tuple) else s for s in scratch],
        compiler_params=pltpu.CompilerParams(vmem_limit_bytes=VMEM_LIMIT),
    )(*operands)


def per_device(rhs, metric, wavenumber):
    sine, edge = jnp.asarray(sine_table()), jnp.asarray(edge_table())
    dft, table = jnp.asarray(dft_table()), jnp.asarray(wave_table())
    full, lines, side, bands = (ROWS, 8, COLS), (ROWS, 2, 8, COLS), (16, PITCH, 128), (BANDS, 8, COLS)
    solved, send, metrics, shift = call(
        local_kernel,
        [lines, (128, 128), (16, 128), (3, 8, COLS)],
        [
            (16, 128), (3, 8, COLS), (128, 128), full, lines, side, side, (COLS, COLS), (5, 8, COLS), (8, 128),
            pltpu.SMEM((1024,), F32), pltpu.SMEM((8,), F32),
            pltpu.SemaphoreType.DMA((4,)), pltpu.SemaphoreType.DMA((5,)), pltpu.SemaphoreType.DMA((4,)),
        ],
        rhs.reshape(16, ROWS, COLS), metric, metric.reshape(8, 128), wavenumber, sine, edge,
        space=pltpu.HBM, far=(0, 1, 2, 3), manual=(0, 1, 2, 3),
    )
    recv = lax.all_to_all(send.reshape(8, 16, 128), "gx", 0, 0, tiled=True)
    (factor,) = call(
        factor_kernel,
        [(5 * ROWS + 2 * BANDS + 4, 8, COLS)],
        [bands] * 6 + [pltpu.SMEM((2048,), F32), (3, 8, COLS), pltpu.SemaphoreType.DMA((2,))],
        metrics.reshape(2048), shift,
        space=pltpu.HBM,
    )
    send, own = call(
        spectrum_kernel,
        [(BANDS, 2, 8, COLS), (5, 8, COLS)],
        [lines],
        recv.reshape(128, 128), factor, dft, table, jnp.asarray(octet_forward()),
    )
    recv = lax.all_to_all(send, "gy", 0, 0, tiled=True)
    (send,) = call(
        separator_kernel,
        [(128, 128)],
        [],
        recv, own, factor, dft, table, jnp.asarray(octet_inverse()),
    )
    recv = lax.all_to_all(send.reshape(8, 16, 128), "gx", 0, 0, tiled=True)
    (out,) = call(
        finish_kernel,
        [(16, ROWS, COLS)],
        [lines, side, side, pltpu.SemaphoreType.DMA((4,))],
        recv.reshape(128, 128), solved, factor, sine, edge,
        far=(0,), manual=(0,),
    )
    return out.reshape(8, 2, ROWS, COLS)


def solution(mesh):
    placed = (P(None, None, "gy", "gx"), P(), P())
    return jax.shard_map(
        per_device, mesh=mesh, in_specs=placed, out_specs=P(None, None, "gy", "gx"), check_vma=False
    )
```

```python
import functools
import math

import jax
import jax.numpy as jnp
import numpy as np
from jax import lax
from jax.experimental import pallas as pl
from jax.experimental.pallas import tpu as pltpu
from jax.sharding import PartitionSpec as P


ASPECT = 0.02
STRIPS = 8
COLS = 256
ROWS = 64
BANDS = 16
PITCH = ROWS + 8
NX = STRIPS * COLS
VMEM_LIMIT = 16 * 1024 * 1024
F32 = jnp.float32


def f32(values):
    return np.asarray(values, np.float32)


def sine_table():
    ramp = np.arange(COLS)
    table = np.sin(np.pi * (np.outer(ramp, ramp) % (2 * COLS)) / COLS) * math.sqrt(2.0 / COLS)
    table[0, :] = 0.0
    table[:, 0] = 0.0
    table[0, 0] = 1.0
    return f32(table)


def edge_table():
    ramp = np.arange(COLS)
    left = np.sin(np.pi * ramp / COLS) * math.sqrt(2.0 / COLS)
    left[0] = 0.0
    along = 4.0 * np.sin(np.pi * ramp / (2 * COLS)) ** 2
    flip = np.where(ramp % 2 == 1, 1.0, -1.0)
    rows = [ASPECT * left, ASPECT * left * flip, ASPECT * along]
    kappa = np.arange(STRIPS)[:, None]
    whole = ASPECT * (2.0 * np.sin(np.pi * (STRIPS * ramp[None, :] + kappa) / NX)) ** 2
    return f32(np.stack([np.broadcast_to(r, (8, COLS)) for r in rows] + [whole, np.broadcast_to(flip, (8, COLS))]))


def dft_table():
    ramp = np.arange(COLS)
    angle = 2.0 * np.pi * (np.outer(ramp, ramp) % COLS) / COLS
    return f32(np.concatenate([np.cos(angle), np.sin(angle)], 1))


def wave_table():
    kappa = np.arange(STRIPS)[:, None]
    j = np.arange(COLS)[None, :]
    angle = 2.0 * np.pi * j * kappa / NX
    return f32(np.stack([np.cos(angle), np.sin(angle)]))


def octet_forward():
    ramp = np.arange(STRIPS)
    angle = 2.0 * np.pi * np.outer(ramp, ramp) / STRIPS
    c, s = np.cos(angle), np.sin(angle)
    return f32(np.block([[c, s], [-s, c]]))


def octet_inverse():
    ramp = np.arange(STRIPS)
    parts = []
    for offset in (0, 1):
        angle = 2.0 * np.pi * np.outer(ramp + offset, ramp) / STRIPS
        c, s = np.cos(angle), np.sin(angle)
        parts.append(np.block([[c, -s], [s, c]]))
    return f32(np.concatenate(parts, 0) / NX)


def dot(a, b):
    return jnp.dot(a, b, precision=lax.Precision.HIGHEST, preferred_element_type=F32)


def lane_ids():
    return lax.broadcasted_iota(jnp.int32, (8, 128), 1)


def wide(column):
    return jnp.broadcast_to(column, (8, 128))


def row_sum(values):
    return wide(jnp.sum(values[:, :128] + values[:, 128:], axis=1, keepdims=True))


def splat_inverse(metric_ref, row):
    return 1.0 / jnp.full((8, COLS), metric_ref[row], F32)


def local_shift(wave_ref, edge_ref):
    sub = lax.broadcasted_iota(jnp.int32, (8, COLS), 0)
    shift = edge_ref[2]
    for mode in range(8):
        shift = shift + jnp.where(sub == mode, wave_ref[mode], 0.0)
    return shift


def local_kernel(
    rhs_hbm, metric_hbm, tiled_hbm, wave_hbm, sine_hbm, edge_hbm, solved_hbm, send_hbm, metrics_hbm, shift_hbm, ratio_hbm,
    metrics_ref, shift_ref, send_ref, ratio_ref, z_ref, r_lo, r_hi, sine_ref, edge_ref, metric_vec, metric_ref, wave_ref, rhs_sem, sems, out_sem,
):
    first = lax.axis_index("gy") * ROWS
    pairs = (
        (metric_hbm, metric_ref), (wave_hbm, wave_ref), (edge_hbm, edge_ref), (tiled_hbm, metric_vec), (sine_hbm, sine_ref)
    )
    small = [pltpu.make_async_copy(a, b, sems.at[i]) for i, (a, b) in enumerate(pairs)]
    half = ROWS // 2
    large = [
        pltpu.make_async_copy(
            rhs_hbm.at[:, pl.ds(part * half, half), pl.ds(side * 128, 128)],
            ref.at[:, pl.ds(part * half, half), :],
            rhs_sem.at[part * 2 + side],
        )
        for part in range(2)
        for side, ref in enumerate((r_lo, r_hi))
    ]
    for copy in small + large:
        copy.start()
    for copy in small[:4]:
        copy.wait()
    metrics_ref[:8, :] = metric_vec[...]
    metrics_ref[8:, :] = 1.0 / metric_vec[...]
    shift = local_shift(wave_ref, edge_ref)
    shift_ref[...] = edge_ref[3] + wave_ref[lax.axis_index("gx")]
    done = [
        pltpu.make_async_copy(metrics_ref, metrics_hbm, sems.at[1]), pltpu.make_async_copy(shift_ref, shift_hbm, sems.at[2])
    ]
    for copy in done:
        copy.start()
    lanes = lane_ids()
    height = jnp.ones((8, COLS), F32)
    slope = jnp.ones((8, COLS), F32)
    for y in range(1, ROWS):
        slope = slope + shift * splat_inverse(metric_ref, first + y) * height
        taller = height + slope
        ratio_ref[y] = height / taller
        height = taller
    ratio_ref[0] = jnp.ones((8, COLS), F32)
    done.append(pltpu.make_async_copy(ratio_ref, ratio_hbm, sems.at[3]))
    done[-1].start()
    small[4].wait()
    sine = sine_ref[...]
    flat = [ref.reshape(16 * PITCH, 128) for ref in (r_lo, r_hi)]

    def line(y, c):
        rows = pl.ds(c * PITCH + y, 8, stride=2 * PITCH)
        return jnp.concatenate([ref[rows, :] for ref in flat], 1)

    state = [jnp.zeros((8, COLS), F32)] * 2
    group = 8
    for base in range(0, ROWS, group):
        if base % half == 0:
            for copy in large[base // half * 2 : base // half * 2 + 2]:
                copy.wait()
        lines = dot(jnp.concatenate([line(y, c) for y in range(base, base + group) for c in range(2)], 0), sine)
        for y in range(max(base, 1), base + group):
            ratio = ratio_ref[y]
            inverse = splat_inverse(metric_ref, first + y)
            for c in range(2):
                at = ((y - base) * 2 + c) * 8
                state[c] = (lines[at : at + 8] * inverse + state[c]) * ratio
                z_ref[y, c] = state[c]
    left = edge_ref[0]
    right = edge_ref[1]
    columns = [[jnp.zeros((8, 128), F32)] * 2 for _ in range(2)]
    upper = [jnp.zeros((8, COLS), F32)] * 2
    for y in range(ROWS - 1, 0, -1):
        ratio = ratio_ref[y]
        inverse = splat_inverse(metric_ref, first + y)
        for c in range(2):
            upper[c] = z_ref[y, c] + ratio * upper[c]
            z_ref[y, c] = upper[c]
            a = upper[c] * left
            source = flat[0][pl.ds(c * PITCH + y, 8, stride=2 * PITCH), :]
            a = (a[:, :128] + a[:, 128:] + jnp.where(lanes == 0, source, 0.0)) * inverse[:, :128]
            b = upper[c] * right
            b = (b[:, :128] + b[:, 128:]) * inverse[:, :128]
            columns[0][c] = jnp.where(lanes == y, wide(jnp.sum(a, axis=1, keepdims=True)), columns[0][c])
            columns[1][c] = jnp.where(lanes == y + ROWS, wide(jnp.sum(b, axis=1, keepdims=True)), columns[1][c])
        if y % 16 == 0:
            done.append(pltpu.make_async_copy(z_ref.at[pl.ds(y, 16)], solved_hbm.at[pl.ds(y, 16)], out_sem.at[y // 16]))
            done[-1].start()
    z_ref[0] = jnp.zeros((2, 8, COLS), F32)
    done.append(pltpu.make_async_copy(z_ref.at[pl.ds(0, 16)], solved_hbm.at[pl.ds(0, 16)], out_sem.at[0]))
    done[-1].start()
    edges = jnp.concatenate([z_ref[y, c] for y in (1, ROWS - 1) for c in range(2)], 0)
    edges = dot(edges, sine)
    zero_lane = lax.broadcasted_iota(jnp.int32, (8, COLS), 1) == 0
    inverse = splat_inverse(metric_ref, first)
    for c in range(2):
        near = jnp.where(zero_lane, 0.0, edges[c * 8 : c * 8 + 8]) + line(0, c) * inverse
        far = jnp.where(zero_lane, 0.0, edges[16 + c * 8 : 24 + c * 8])
        for i in range(2):
            part = slice(i * 128, i * 128 + 128)
            send_ref[pl.ds(c * 2 + i, 8, stride=16), :] = near[:, part]
            send_ref[pl.ds(4 + c * 2 + i, 8, stride=16), :] = far[:, part]
        send_ref[pl.ds(8 + c, 8, stride=16), :] = jnp.where(lanes < ROWS, columns[0][c], columns[1][c])
        for pad in range(3):
            send_ref[pl.ds(10 + c * 3 + pad, 8, stride=16), :] = jnp.zeros((8, 128), F32)
    done.append(pltpu.make_async_copy(send_ref, send_hbm, sems.at[0]))
    done[-1].start()
    for copy in done:
        copy.wait()


def factors(ref):
    sizes = (ROWS, ROWS, ROWS, BANDS, BANDS, 4)
    starts = np.cumsum((0,) + sizes)
    return [ref.at[pl.ds(int(a), n)] for a, n in zip(starts, sizes)]


def factor_kernel(
    metrics_hbm, shift_hbm, factor_ref,
    gamma_ref, base_ref, edge_ref, x_ref, above_ref, inverse_ref, metrics_ref, shift_ref, sems,
):
    copies = [
        pltpu.make_async_copy(metrics_hbm, metrics_ref, sems.at[0]), pltpu.make_async_copy(shift_hbm, shift_ref, sems.at[1])
    ]
    for copy in copies:
        copy.start()
    for copy in copies:
        copy.wait()
    over_ref, under_ref, ratio_ref, up_ref, down_ref, final_ref = factors(factor_ref)
    mine = lax.axis_index("gy")
    shift = shift_ref[...]

    def excess(row):
        double = 2.0 * metrics_ref[row]
        return ((double + shift) - double) * metrics_ref[1024 + row]

    one = jnp.ones((8, COLS), F32)
    zero = jnp.zeros((8, COLS), F32)
    together = 4

    def bands(outer, _):
        state = [(one, one, zero, zero)] * together

        def rows(y, state):
            out = []
            for i in range(together):
                height, slope, rest, rise = state[i]
                t = excess((outer * together + i) * ROWS + y)
                slope = slope + t * height
                height = height + slope
                rise = rise + t * (rest + 1.0)
                rest = rest + rise
                out.append((height, slope, rest, rise))
            return tuple(out)

        state = lax.fori_loop(1, ROWS, rows, tuple(state), unroll=21)
        for i in range(together):
            height, slope, rest, _ = state[i]
            band = outer * together + i
            gamma = 1.0 / height
            gamma_ref[band] = gamma
            base_ref[band] = excess(band * ROWS) + rest * gamma
            edge_ref[band] = (slope - 1.0) * gamma
        return 0

    lax.fori_loop(0, BANDS // together, bands, 0)

    flow = one
    above, down, inverse = one, zero, zero
    height, slope = one, one
    rest, rise = one, one
    for y in range(1, ROWS + 1):
        if y < ROWS:
            under_ref[y] = height
            slope = slope + excess(mine * ROWS + y) * height
            taller = height + slope
            ratio_ref[y] = height / taller
            height = taller
            over_ref[ROWS - y] = rest
            rise = rise + excess(mine * ROWS + ROWS - y) * rest
            rest = rest + rise
        if y % 4 == 0:
            band = y // 4 - 1
            x = base_ref[band] + flow
            if band:
                x = x + edge_ref[band - 1]
            x_ref[band] = x
            gamma = gamma_ref[band]
            up = gamma / (gamma + x)
            up_ref[band] = up
            flow = up * x
            band = BANDS - 1 - band
            above_ref[band], down_ref[band], inverse_ref[band] = above, down, inverse
            if band:
                x = base_ref[band] + edge_ref[band - 1] + gamma_ref[band] * above
                below = gamma_ref[band - 1]
                inverse = 1.0 / (below + x)
                down = below * inverse
                above = x * inverse
    gamma = gamma_ref[mine]
    final_ref[0] = down_ref[mine]
    final_ref[1] = inverse_ref[mine]
    final_ref[2] = 1.0 / (x_ref[mine] + gamma * above_ref[mine])
    final_ref[3] = gamma


def spectrum_kernel(
    recv_ref, factor_ref, dft_ref, table_ref, octet_ref, send_ref, own_ref, z_ref
):
    _, _, ratio_ref, up_ref, down_ref, _ = factors(factor_ref)
    mine = lax.axis_index("gy")

    def take(i):
        return recv_ref[pl.ds(i, 8, stride=16), :]

    pieces = [[], []]
    for c in range(2):
        for i in range(2):
            pieces[c].append(take(c * 2 + i))
        for i in range(2):
            pieces[c].append(take(4 + c * 2 + i))
        column = take(8 + c)
        pieces[c].append(column + pltpu.roll(pltpu.roll(column, 1, 0), ROWS, 1))
    stacked = jnp.concatenate([jnp.concatenate(pieces[0], 1), jnp.concatenate(pieces[1], 1)], 0)
    mixed = dot(octet_ref[...], stacked)
    cos, sin = table_ref[0], table_ref[1]
    turned = [[], []]
    for line in range(2):
        re = mixed[:8, line * COLS : line * COLS + COLS]
        im = mixed[8:, line * COLS : line * COLS + COLS]
        turned[0].append(re * cos + im * sin)
        turned[1].append(im * cos - re * sin)
    both = dot(jnp.concatenate(turned[0] + turned[1], 0), dft_ref[...])
    columns = [mixed[c * 8 : c * 8 + 8, 2 * COLS :] for c in range(2)]
    lanes = lane_ids()
    state = [jnp.zeros((8, COLS), F32)] * 2
    for y in range(1, ROWS):
        ratio = ratio_ref[y]
        for c in range(2):
            source = wide(columns[c][:, y : y + 1])
            state[c] = (jnp.concatenate([source, source], 1) + state[c]) * ratio
            z_ref[y, c] = state[c]
    upper = [jnp.zeros((8, COLS), F32)] * 2
    total = [jnp.zeros((8, 128), F32)] * 2
    for y in range(ROWS - 1, 0, -1):
        ratio = ratio_ref[y]
        for c in range(2):
            upper[c] = z_ref[y, c] + ratio * upper[c]
            total[c] = jnp.where(lanes == y, row_sum(upper[c]), total[c])
    sides = []
    for line, extra in enumerate((upper, state)):
        re_cos = both[line * 8 : line * 8 + 8, :COLS]
        re_sin = both[line * 8 : line * 8 + 8, COLS:]
        im_cos = both[16 + line * 8 : 24 + line * 8, :COLS]
        im_sin = both[16 + line * 8 : 24 + line * 8, COLS:]
        sides.append((re_cos + im_sin + extra[0], im_cos - re_sin + extra[1]))
    for c in range(2):
        own_ref[c], own_ref[2 + c] = sides[0][c], sides[1][c]
        send_ref[mine, c] = jnp.zeros((8, COLS), F32)
    own_ref[4] = jnp.concatenate(total, 1)
    up, down = up_ref[mine], down_ref[mine]

    def above(band, carry):
        factor = up_ref[band]
        for c in range(2):
            send_ref[band, c] = carry[c]
        return tuple(value * factor for value in carry)

    def below(step, carry):
        band = mine - 1 - step
        factor = down_ref[band]
        for c in range(2):
            send_ref[band, c] = carry[c]
        return tuple(value * factor for value in carry)

    lax.fori_loop(mine + 1, BANDS, above, tuple(sides[1][c] + up * sides[0][c] for c in range(2)))
    lax.fori_loop(0, mine, below, tuple(sides[0][c] + down * sides[1][c] for c in range(2)))


def separator_kernel(
    recv_ref, own_ref, factor_ref, dft_ref, table_ref, octet_ref, send_ref
):
    over_ref, under_ref, _, _, _, final_ref = factors(factor_ref)
    mine = lax.axis_index("gy")
    from_below = [own_ref[c] for c in range(2)]
    from_above = [own_ref[2 + c] for c in range(2)]
    for band in range(BANDS):
        for c in range(2):
            value = recv_ref[band, c]
            from_below[c] = from_below[c] + jnp.where(band < mine, value, 0.0)
            from_above[c] = from_above[c] + jnp.where(band > mine, value, 0.0)
    down, inverse, pivot = final_ref[0], final_ref[1], final_ref[2]
    near = [(from_below[c] + down * from_above[c]) * pivot for c in range(2)]
    far = [from_above[c] * inverse + down * near[c] for c in range(2)]
    lanes = lane_ids()
    both = dot(jnp.concatenate([near[0], far[0], near[1], far[1]], 0), dft_ref[...])
    total = [own_ref[4, :, c * 128 : c * 128 + 128] for c in range(2)]
    gamma = final_ref[3]
    near = [value * gamma for value in near]
    far = [value * gamma for value in far]
    for y in range(1, ROWS):
        over, under = over_ref[y], under_ref[y]
        for c in range(2):
            extra = row_sum(over * near[c] + under * far[c])
            total[c] = total[c] + jnp.where(lanes == y, extra, 0.0)
    cos, sin = table_ref[0], table_ref[1]
    turned = [[], []]
    for line in range(2):
        re_cos = both[line * 8 : line * 8 + 8, :COLS]
        re_sin = both[line * 8 : line * 8 + 8, COLS:]
        im_cos = both[16 + line * 8 : 24 + line * 8, :COLS]
        im_sin = both[16 + line * 8 : 24 + line * 8, COLS:]
        re = re_cos - im_sin
        im = re_sin + im_cos
        turned[0].append(re * cos - im * sin)
        turned[1].append(re * sin + im * cos)
    stacked = [jnp.concatenate(turned[c] + [total[c]], 1) for c in range(2)]
    out = dot(octet_ref[...], jnp.concatenate(stacked, 0))
    for c in range(2):
        for i in range(4):
            row = (i // 2) * 4 + c * 2 + i % 2
            send_ref[pl.ds(row, 8, stride=16), :] = out[c * 8 : c * 8 + 8, i * 128 : i * 128 + 128]
        here = out[c * 8 : c * 8 + 8, 2 * COLS :]
        there = out[16 + c * 8 : 24 + c * 8, 2 * COLS :]
        send_ref[pl.ds(8 + c, 8, stride=16), :] = jnp.where(lanes < ROWS, here, pltpu.roll(there, ROWS, 1))
        for pad in range(3):
            send_ref[pl.ds(10 + c * 3 + pad, 8, stride=16), :] = jnp.zeros((8, 128), F32)


def finish_kernel(recv_ref, solved_ref, local_ref, metric_ref, sine_ref, edge_ref, out_hbm, z_ref, o_lo, o_hi, sems):
    band = lax.axis_index("gy")
    lanes = lane_ids()
    metric = jnp.broadcast_to(metric_ref[pl.ds(band // 2, 1), :], (8, 128))
    swapped = pltpu.roll(metric, ROWS, 1)
    metric = jnp.where((lanes < ROWS) == (band % 2 == 0), metric, swapped)
    def take(i):
        return recv_ref[pl.ds(i, 8, stride=16), :]

    sine = sine_ref[...]
    near = [jnp.concatenate([take(c * 2), take(c * 2 + 1)], 1) for c in range(2)]
    far = [jnp.concatenate([take(4 + c * 2), take(5 + c * 2)], 1) for c in range(2)]
    columns = [take(8 + c) for c in range(2)]
    edges = dot(jnp.concatenate(near + far, 0), sine)
    scaled = [value / metric for value in columns]
    left, flip = edge_ref[0], edge_ref[4]
    zero_lane = lax.broadcasted_iota(jnp.int32, (8, COLS), 1) == 0
    state = [edges[c * 8 : c * 8 + 8] for c in range(2)]
    for y in range(1, ROWS):
        ratio = local_ref[y]
        for c in range(2):
            here = wide(scaled[c][:, y : y + 1])
            there = wide(scaled[c][:, ROWS + y : ROWS + y + 1])
            here = jnp.concatenate([here, here], 1)
            there = jnp.concatenate([there, there], 1)
            state[c] = (state[c] + left * (here + flip * there)) * ratio
            z_ref[y, c] = state[c]
    upper = [edges[16 + c * 8 : 24 + c * 8] for c in range(2)]
    flat = [ref.reshape(16 * PITCH, 128) for ref in (o_lo, o_hi)]
    group, half = 8, ROWS // 2
    copies = []
    for base in range(ROWS - group, -1, -group):
        lines = []
        for y in range(base + group - 1, base - 1, -1):
            for c in range(2):
                if y:
                    upper[c] = z_ref[y, c] + local_ref[y] * upper[c]
                    here = wide(columns[c][:, y : y + 1])
                    here = jnp.concatenate([here, here], 1)
                    lines.append(jnp.where(zero_lane, here, upper[c] + solved_ref[y, c]))
                else:
                    lines.append(edges[c * 8 : c * 8 + 8])
        product = dot(jnp.concatenate(lines, 0), sine)
        for i in range(2 * group):
            rows = pl.ds(i % 2 * PITCH + base + group - 1 - i // 2, 8, stride=2 * PITCH)
            flat[0][rows, :] = product[i * 8 : i * 8 + 8, :128]
            flat[1][rows, :] = product[i * 8 : i * 8 + 8, 128:]
        if base % half == 0:
            for side, ref in enumerate((o_lo, o_hi)):
                copies.append(
                    pltpu.make_async_copy(
                        ref.at[:, pl.ds(base, half), :],
                        out_hbm.at[:, pl.ds(base, half), pl.ds(side * 128, 128)],
                        sems.at[len(copies)],
                    )
                )
                copies[-1].start()
    for copy in copies:
        copy.wait()


def call(kernel, outs, scratch, *operands, scalars=(), far=(), manual=(), space=pltpu.VMEM):
    places = [pltpu.SMEM if i in scalars else space for i in range(len(operands))]
    if space == pltpu.HBM:
        operands = [pltpu.with_memory_space_constraint(a, space) for a in operands]
    return pl.pallas_call(
        kernel,
        out_shape=[(pltpu.HBM if i in far else pltpu.VMEM)(s, F32) for i, s in enumerate(outs)],
        in_specs=[pl.BlockSpec(memory_space=place) for place in places],
        out_specs=[pl.BlockSpec(memory_space=pltpu.HBM if i in manual else pltpu.VMEM) for i in range(len(outs))],
        scratch_shapes=[pltpu.VMEM(s, F32) if isinstance(s, tuple) else s for s in scratch],
        compiler_params=pltpu.CompilerParams(vmem_limit_bytes=VMEM_LIMIT),
    )(*operands)


def per_device(rhs, metric, wavenumber):
    sine, edge = jnp.asarray(sine_table()), jnp.asarray(edge_table())
    dft, table = jnp.asarray(dft_table()), jnp.asarray(wave_table())
    full, lines, side, bands = (ROWS, 8, COLS), (ROWS, 2, 8, COLS), (16, PITCH, 128), (BANDS, 8, COLS)
    solved, send, metrics, shift, ratio = call(
        local_kernel,
        [lines, (128, 128), (16, 128), (8, COLS), full],
        [
            (16, 128), (8, COLS), (128, 128), full, lines, side, side, (COLS, COLS), (5, 8, COLS), (8, 128),
            pltpu.SMEM((1024,), F32), pltpu.SMEM((8,), F32),
            pltpu.SemaphoreType.DMA((4,)), pltpu.SemaphoreType.DMA((5,)), pltpu.SemaphoreType.DMA((4,)),
        ],
        rhs.reshape(16, ROWS, COLS), metric, metric.reshape(8, 128), wavenumber, sine, edge,
        space=pltpu.HBM, far=range(5), manual=range(5),
    )
    recv = lax.all_to_all(send.reshape(8, 16, 128), "gx", 0, 0, tiled=True)
    (factor,) = call(
        factor_kernel,
        [(3 * ROWS + 2 * BANDS + 4, 8, COLS)],
        [bands] * 6 + [pltpu.SMEM((2048,), F32), (8, COLS), pltpu.SemaphoreType.DMA((2,))],
        metrics.reshape(2048), shift,
        space=pltpu.HBM,
    )
    send, own = call(
        spectrum_kernel,
        [(BANDS, 2, 8, COLS), (5, 8, COLS)],
        [lines],
        recv.reshape(128, 128), factor, dft, table, jnp.asarray(octet_forward()),
    )
    recv = lax.all_to_all(send, "gy", 0, 0, tiled=True)
    (send,) = call(
        separator_kernel,
        [(128, 128)],
        [],
        recv, own, factor, dft, table, jnp.asarray(octet_inverse()),
    )
    recv = lax.all_to_all(send.reshape(8, 16, 128), "gx", 0, 0, tiled=True)
    (out,) = call(
        finish_kernel,
        [(16, ROWS, COLS)],
        [lines, side, side, pltpu.SemaphoreType.DMA((4,))],
        recv.reshape(128, 128), solved, ratio, metric.reshape(8, 128), sine, edge,
        far=(0,), manual=(0,),
    )
    return out.reshape(8, 2, ROWS, COLS)


def solution(mesh):
    placed = (P(None, None, "gy", "gx"), P(), P())
    return jax.shard_map(
        per_device, mesh=mesh, in_specs=placed, out_specs=P(None, None, "gy", "gx"), check_vma=False
    )
```

```python
import functools
import math

import jax
import jax.numpy as jnp
import numpy as np
from jax import lax
from jax.experimental import pallas as pl
from jax.experimental.pallas import tpu as pltpu
from jax.sharding import PartitionSpec as P


ASPECT = 0.02
STRIPS = 8
COLS = 256
ROWS = 64
BANDS = 16
PITCH = ROWS + 8
NX = STRIPS * COLS
VMEM_LIMIT = 16 * 1024 * 1024
F32 = jnp.float32


def f32(values):
    return np.asarray(values, np.float32)


def sine_table():
    ramp = np.arange(COLS)
    table = np.sin(np.pi * (np.outer(ramp, ramp) % (2 * COLS)) / COLS) * math.sqrt(2.0 / COLS)
    table[0, :] = 0.0
    table[:, 0] = 0.0
    table[0, 0] = 1.0
    return f32(table)


def edge_table():
    ramp = np.arange(COLS)
    left = np.sin(np.pi * ramp / COLS) * math.sqrt(2.0 / COLS)
    left[0] = 0.0
    along = 4.0 * np.sin(np.pi * ramp / (2 * COLS)) ** 2
    flip = np.where(ramp % 2 == 1, 1.0, -1.0)
    rows = [ASPECT * left, ASPECT * left * flip, ASPECT * along]
    kappa = np.arange(STRIPS)[:, None]
    whole = ASPECT * (2.0 * np.sin(np.pi * (STRIPS * ramp[None, :] + kappa) / NX)) ** 2
    return f32(np.stack([np.broadcast_to(r, (8, COLS)) for r in rows] + [whole, np.broadcast_to(flip, (8, COLS))]))


def dft_table():
    ramp = np.arange(COLS)
    angle = 2.0 * np.pi * (np.outer(ramp, ramp) % COLS) / COLS
    return f32(np.concatenate([np.cos(angle), np.sin(angle)], 1))


def wave_table():
    kappa = np.arange(STRIPS)[:, None]
    j = np.arange(COLS)[None, :]
    angle = 2.0 * np.pi * j * kappa / NX
    return f32(np.stack([np.cos(angle), np.sin(angle)]))


def octet_forward():
    ramp = np.arange(STRIPS)
    angle = 2.0 * np.pi * np.outer(ramp, ramp) / STRIPS
    c, s = np.cos(angle), np.sin(angle)
    return f32(np.block([[c, s], [-s, c]]))


def octet_inverse():
    ramp = np.arange(STRIPS)
    parts = []
    for offset in (0, 1):
        angle = 2.0 * np.pi * np.outer(ramp + offset, ramp) / STRIPS
        c, s = np.cos(angle), np.sin(angle)
        parts.append(np.block([[c, -s], [s, c]]))
    return f32(np.concatenate(parts, 0) / NX)


def dot(a, b, precision=lax.Precision.HIGHEST):
    return jnp.dot(a, b, precision=precision, preferred_element_type=F32)


def short_dot(a, b):
    return dot(a, b, lax.Precision.HIGH)


def lane_ids():
    return lax.broadcasted_iota(jnp.int32, (8, 128), 1)


def wide(column):
    return jnp.broadcast_to(column, (8, 128))


def row_sum(values):
    return wide(jnp.sum(values[:, :128] + values[:, 128:], axis=1, keepdims=True))


def splat_inverse(metric_ref, row):
    return 1.0 / jnp.full((8, COLS), metric_ref[row], F32)


def local_shift(wave_ref, edge_ref):
    sub = lax.broadcasted_iota(jnp.int32, (8, COLS), 0)
    shift = edge_ref[2]
    for mode in range(8):
        shift = shift + jnp.where(sub == mode, wave_ref[mode], 0.0)
    return shift


def local_kernel(
    rhs_hbm, metric_hbm, tiled_hbm, wave_hbm, sine_hbm, edge_hbm, solved_hbm, send_hbm, metrics_hbm, shift_hbm, ratio_hbm,
    metrics_ref, shift_ref, send_ref, ratio_ref, z_ref, r_lo, r_hi, sine_ref, edge_ref, metric_vec, metric_ref, wave_ref, rhs_sem, sems, out_sem,
):
    first = lax.axis_index("gy") * ROWS
    pairs = (
        (metric_hbm, metric_ref), (wave_hbm, wave_ref), (edge_hbm, edge_ref), (tiled_hbm, metric_vec), (sine_hbm, sine_ref)
    )
    small = [pltpu.make_async_copy(a, b, sems.at[i]) for i, (a, b) in enumerate(pairs)]
    half = ROWS // 2
    large = [
        pltpu.make_async_copy(
            rhs_hbm.at[:, pl.ds(part * half, half), pl.ds(side * 128, 128)],
            ref.at[:, pl.ds(part * half, half), :],
            rhs_sem.at[part * 2 + side],
        )
        for part in range(2)
        for side, ref in enumerate((r_lo, r_hi))
    ]
    for copy in small + large:
        copy.start()
    for copy in small[:4]:
        copy.wait()
    metrics_ref[:8, :] = metric_vec[...]
    metrics_ref[8:, :] = 1.0 / metric_vec[...]
    shift = local_shift(wave_ref, edge_ref)
    shift_ref[...] = edge_ref[3] + wave_ref[lax.axis_index("gx")]
    done = [
        pltpu.make_async_copy(metrics_ref, metrics_hbm, sems.at[1]), pltpu.make_async_copy(shift_ref, shift_hbm, sems.at[2])
    ]
    for copy in done:
        copy.start()
    lanes = lane_ids()
    height = jnp.ones((8, COLS), F32)
    slope = jnp.ones((8, COLS), F32)
    for y in range(1, ROWS):
        slope = slope + shift * splat_inverse(metric_ref, first + y) * height
        taller = height + slope
        ratio_ref[y] = height / taller
        height = taller
    ratio_ref[0] = jnp.ones((8, COLS), F32)
    done.append(pltpu.make_async_copy(ratio_ref, ratio_hbm, sems.at[3]))
    done[-1].start()
    small[4].wait()
    sine = sine_ref[...]
    flat = [ref.reshape(16 * PITCH, 128) for ref in (r_lo, r_hi)]

    def line(y, c):
        rows = pl.ds(c * PITCH + y, 8, stride=2 * PITCH)
        return jnp.concatenate([ref[rows, :] for ref in flat], 1)

    state = [jnp.zeros((8, COLS), F32)] * 2
    group = 8
    for base in range(0, ROWS, group):
        if base % half == 0:
            for copy in large[base // half * 2 : base // half * 2 + 2]:
                copy.wait()
        lines = dot(jnp.concatenate([line(y, c) for y in range(base, base + group) for c in range(2)], 0), sine)
        for y in range(max(base, 1), base + group):
            ratio = ratio_ref[y]
            inverse = splat_inverse(metric_ref, first + y)
            for c in range(2):
                at = ((y - base) * 2 + c) * 8
                state[c] = (lines[at : at + 8] * inverse + state[c]) * ratio
                z_ref[y, c] = state[c]
    left = edge_ref[0]
    right = edge_ref[1]
    columns = [[jnp.zeros((8, 128), F32)] * 2 for _ in range(2)]
    upper = [jnp.zeros((8, COLS), F32)] * 2
    for y in range(ROWS - 1, 0, -1):
        ratio = ratio_ref[y]
        inverse = splat_inverse(metric_ref, first + y)
        for c in range(2):
            upper[c] = z_ref[y, c] + ratio * upper[c]
            z_ref[y, c] = upper[c]
            a = upper[c] * left
            source = flat[0][pl.ds(c * PITCH + y, 8, stride=2 * PITCH), :]
            a = (a[:, :128] + a[:, 128:] + jnp.where(lanes == 0, source, 0.0)) * inverse[:, :128]
            b = upper[c] * right
            b = (b[:, :128] + b[:, 128:]) * inverse[:, :128]
            columns[0][c] = jnp.where(lanes == y, wide(jnp.sum(a, axis=1, keepdims=True)), columns[0][c])
            columns[1][c] = jnp.where(lanes == y + ROWS, wide(jnp.sum(b, axis=1, keepdims=True)), columns[1][c])
        if y % 16 == 0:
            done.append(pltpu.make_async_copy(z_ref.at[pl.ds(y, 16)], solved_hbm.at[pl.ds(y, 16)], out_sem.at[y // 16]))
            done[-1].start()
    z_ref[0] = jnp.zeros((2, 8, COLS), F32)
    done.append(pltpu.make_async_copy(z_ref.at[pl.ds(0, 16)], solved_hbm.at[pl.ds(0, 16)], out_sem.at[0]))
    done[-1].start()
    edges = jnp.concatenate([z_ref[y, c] for y in (1, ROWS - 1) for c in range(2)], 0)
    edges = dot(edges, sine)
    zero_lane = lax.broadcasted_iota(jnp.int32, (8, COLS), 1) == 0
    inverse = splat_inverse(metric_ref, first)
    for c in range(2):
        near = jnp.where(zero_lane, 0.0, edges[c * 8 : c * 8 + 8]) + line(0, c) * inverse
        far = jnp.where(zero_lane, 0.0, edges[16 + c * 8 : 24 + c * 8])
        for i in range(2):
            part = slice(i * 128, i * 128 + 128)
            send_ref[pl.ds(c * 2 + i, 8, stride=16), :] = near[:, part]
            send_ref[pl.ds(4 + c * 2 + i, 8, stride=16), :] = far[:, part]
        send_ref[pl.ds(8 + c, 8, stride=16), :] = jnp.where(lanes < ROWS, columns[0][c], columns[1][c])
        for pad in range(3):
            send_ref[pl.ds(10 + c * 3 + pad, 8, stride=16), :] = jnp.zeros((8, 128), F32)
    done.append(pltpu.make_async_copy(send_ref, send_hbm, sems.at[0]))
    done[-1].start()
    for copy in done:
        copy.wait()


def factors(ref):
    sizes = (ROWS, ROWS, ROWS, BANDS, BANDS, 4)
    starts = np.cumsum((0,) + sizes)
    return [ref.at[pl.ds(int(a), n)] for a, n in zip(starts, sizes)]


def factor_kernel(
    metrics_hbm, shift_hbm, factor_ref,
    gamma_ref, base_ref, edge_ref, x_ref, above_ref, inverse_ref, metrics_ref, shift_ref, sems,
):
    copies = [
        pltpu.make_async_copy(metrics_hbm, metrics_ref, sems.at[0]), pltpu.make_async_copy(shift_hbm, shift_ref, sems.at[1])
    ]
    for copy in copies:
        copy.start()
    for copy in copies:
        copy.wait()
    over_ref, under_ref, ratio_ref, up_ref, down_ref, final_ref = factors(factor_ref)
    mine = lax.axis_index("gy")
    shift = shift_ref[...]

    def excess(row):
        double = 2.0 * metrics_ref[row]
        return ((double + shift) - double) * metrics_ref[1024 + row]

    one = jnp.ones((8, COLS), F32)
    zero = jnp.zeros((8, COLS), F32)
    together = 4

    def bands(outer, _):
        state = [(one, one, zero, zero)] * together

        def rows(y, state):
            out = []
            for i in range(together):
                height, slope, rest, rise = state[i]
                t = excess((outer * together + i) * ROWS + y)
                slope = slope + t * height
                height = height + slope
                rise = rise + t * (rest + 1.0)
                rest = rest + rise
                out.append((height, slope, rest, rise))
            return tuple(out)

        state = lax.fori_loop(1, ROWS, rows, tuple(state), unroll=21)
        for i in range(together):
            height, slope, rest, _ = state[i]
            band = outer * together + i
            gamma = 1.0 / height
            gamma_ref[band] = gamma
            base_ref[band] = excess(band * ROWS) + rest * gamma
            edge_ref[band] = (slope - 1.0) * gamma
        return 0

    lax.fori_loop(0, BANDS // together, bands, 0)

    flow = one
    above, down, inverse = one, zero, zero
    height, slope = one, one
    rest, rise = one, one
    for y in range(1, ROWS + 1):
        if y < ROWS:
            under_ref[y] = height
            slope = slope + excess(mine * ROWS + y) * height
            taller = height + slope
            ratio_ref[y] = height / taller
            height = taller
            over_ref[ROWS - y] = rest
            rise = rise + excess(mine * ROWS + ROWS - y) * rest
            rest = rest + rise
        if y % 4 == 0:
            band = y // 4 - 1
            x = base_ref[band] + flow
            if band:
                x = x + edge_ref[band - 1]
            x_ref[band] = x
            gamma = gamma_ref[band]
            up = gamma / (gamma + x)
            up_ref[band] = up
            flow = up * x
            band = BANDS - 1 - band
            above_ref[band], down_ref[band], inverse_ref[band] = above, down, inverse
            if band:
                x = base_ref[band] + edge_ref[band - 1] + gamma_ref[band] * above
                below = gamma_ref[band - 1]
                inverse = 1.0 / (below + x)
                down = below * inverse
                above = x * inverse
    gamma = gamma_ref[mine]
    final_ref[0] = down_ref[mine]
    final_ref[1] = inverse_ref[mine]
    final_ref[2] = 1.0 / (x_ref[mine] + gamma * above_ref[mine])
    final_ref[3] = gamma


def spectrum_kernel(
    recv_ref, factor_ref, dft_ref, table_ref, octet_ref, send_ref, own_ref, z_ref
):
    _, _, ratio_ref, up_ref, down_ref, _ = factors(factor_ref)
    mine = lax.axis_index("gy")

    def take(i):
        return recv_ref[pl.ds(i, 8, stride=16), :]

    pieces = [[], []]
    for c in range(2):
        for i in range(2):
            pieces[c].append(take(c * 2 + i))
        for i in range(2):
            pieces[c].append(take(4 + c * 2 + i))
        column = take(8 + c)
        pieces[c].append(column + pltpu.roll(pltpu.roll(column, 1, 0), ROWS, 1))
    stacked = jnp.concatenate([jnp.concatenate(pieces[0], 1), jnp.concatenate(pieces[1], 1)], 0)
    mixed = dot(octet_ref[...], stacked)
    cos, sin = table_ref[0], table_ref[1]
    turned = [[], []]
    for line in range(2):
        re = mixed[:8, line * COLS : line * COLS + COLS]
        im = mixed[8:, line * COLS : line * COLS + COLS]
        turned[0].append(re * cos + im * sin)
        turned[1].append(im * cos - re * sin)
    both = dot(jnp.concatenate(turned[0] + turned[1], 0), dft_ref[...])
    columns = [mixed[c * 8 : c * 8 + 8, 2 * COLS :] for c in range(2)]
    lanes = lane_ids()
    state = [jnp.zeros((8, COLS), F32)] * 2
    for y in range(1, ROWS):
        ratio = ratio_ref[y]
        for c in range(2):
            source = wide(columns[c][:, y : y + 1])
            state[c] = (jnp.concatenate([source, source], 1) + state[c]) * ratio
            z_ref[y, c] = state[c]
    upper = [jnp.zeros((8, COLS), F32)] * 2
    total = [jnp.zeros((8, 128), F32)] * 2
    for y in range(ROWS - 1, 0, -1):
        ratio = ratio_ref[y]
        for c in range(2):
            upper[c] = z_ref[y, c] + ratio * upper[c]
            total[c] = jnp.where(lanes == y, row_sum(upper[c]), total[c])
    sides = []
    for line, extra in enumerate((upper, state)):
        re_cos = both[line * 8 : line * 8 + 8, :COLS]
        re_sin = both[line * 8 : line * 8 + 8, COLS:]
        im_cos = both[16 + line * 8 : 24 + line * 8, :COLS]
        im_sin = both[16 + line * 8 : 24 + line * 8, COLS:]
        sides.append((re_cos + im_sin + extra[0], im_cos - re_sin + extra[1]))
    for c in range(2):
        own_ref[c], own_ref[2 + c] = sides[0][c], sides[1][c]
        send_ref[mine, c] = jnp.zeros((8, COLS), F32)
    own_ref[4] = jnp.concatenate(total, 1)
    up, down = up_ref[mine], down_ref[mine]

    def above(band, carry):
        factor = up_ref[band]
        for c in range(2):
            send_ref[band, c] = carry[c]
        return tuple(value * factor for value in carry)

    def below(step, carry):
        band = mine - 1 - step
        factor = down_ref[band]
        for c in range(2):
            send_ref[band, c] = carry[c]
        return tuple(value * factor for value in carry)

    lax.fori_loop(mine + 1, BANDS, above, tuple(sides[1][c] + up * sides[0][c] for c in range(2)))
    lax.fori_loop(0, mine, below, tuple(sides[0][c] + down * sides[1][c] for c in range(2)))


def separator_kernel(
    recv_ref, own_ref, factor_ref, dft_ref, table_ref, octet_ref, send_ref
):
    over_ref, under_ref, _, _, _, final_ref = factors(factor_ref)
    mine = lax.axis_index("gy")
    from_below = [own_ref[c] for c in range(2)]
    from_above = [own_ref[2 + c] for c in range(2)]
    for band in range(BANDS):
        for c in range(2):
            value = recv_ref[band, c]
            from_below[c] = from_below[c] + jnp.where(band < mine, value, 0.0)
            from_above[c] = from_above[c] + jnp.where(band > mine, value, 0.0)
    down, inverse, pivot = final_ref[0], final_ref[1], final_ref[2]
    near = [(from_below[c] + down * from_above[c]) * pivot for c in range(2)]
    far = [from_above[c] * inverse + down * near[c] for c in range(2)]
    lanes = lane_ids()
    both = short_dot(jnp.concatenate([near[0], far[0], near[1], far[1]], 0), dft_ref[...])
    total = [own_ref[4, :, c * 128 : c * 128 + 128] for c in range(2)]
    gamma = final_ref[3]
    near = [value * gamma for value in near]
    far = [value * gamma for value in far]
    for y in range(1, ROWS):
        over, under = over_ref[y], under_ref[y]
        for c in range(2):
            extra = row_sum(over * near[c] + under * far[c])
            total[c] = total[c] + jnp.where(lanes == y, extra, 0.0)
    cos, sin = table_ref[0], table_ref[1]
    turned = [[], []]
    for line in range(2):
        re_cos = both[line * 8 : line * 8 + 8, :COLS]
        re_sin = both[line * 8 : line * 8 + 8, COLS:]
        im_cos = both[16 + line * 8 : 24 + line * 8, :COLS]
        im_sin = both[16 + line * 8 : 24 + line * 8, COLS:]
        re = re_cos - im_sin
        im = re_sin + im_cos
        turned[0].append(re * cos - im * sin)
        turned[1].append(re * sin + im * cos)
    stacked = [jnp.concatenate(turned[c] + [total[c]], 1) for c in range(2)]
    out = short_dot(octet_ref[...], jnp.concatenate(stacked, 0))
    for c in range(2):
        for i in range(4):
            row = (i // 2) * 4 + c * 2 + i % 2
            send_ref[pl.ds(row, 8, stride=16), :] = out[c * 8 : c * 8 + 8, i * 128 : i * 128 + 128]
        here = out[c * 8 : c * 8 + 8, 2 * COLS :]
        there = out[16 + c * 8 : 24 + c * 8, 2 * COLS :]
        send_ref[pl.ds(8 + c, 8, stride=16), :] = jnp.where(lanes < ROWS, here, pltpu.roll(there, ROWS, 1))
        for pad in range(3):
            send_ref[pl.ds(10 + c * 3 + pad, 8, stride=16), :] = jnp.zeros((8, 128), F32)


def finish_kernel(recv_ref, solved_ref, local_ref, metric_ref, sine_ref, edge_ref, out_hbm, z_ref, o_lo, o_hi, sems):
    band = lax.axis_index("gy")
    lanes = lane_ids()
    metric = jnp.broadcast_to(metric_ref[pl.ds(band // 2, 1), :], (8, 128))
    swapped = pltpu.roll(metric, ROWS, 1)
    metric = jnp.where((lanes < ROWS) == (band % 2 == 0), metric, swapped)
    def take(i):
        return recv_ref[pl.ds(i, 8, stride=16), :]

    sine = sine_ref[...]
    near = [jnp.concatenate([take(c * 2), take(c * 2 + 1)], 1) for c in range(2)]
    far = [jnp.concatenate([take(4 + c * 2), take(5 + c * 2)], 1) for c in range(2)]
    columns = [take(8 + c) for c in range(2)]
    edges = short_dot(jnp.concatenate(near + far, 0), sine)
    scaled = [value / metric for value in columns]
    left, flip = edge_ref[0], edge_ref[4]
    zero_lane = lax.broadcasted_iota(jnp.int32, (8, COLS), 1) == 0
    state = [edges[c * 8 : c * 8 + 8] for c in range(2)]
    for y in range(1, ROWS):
        ratio = local_ref[y]
        for c in range(2):
            here = wide(scaled[c][:, y : y + 1])
            there = wide(scaled[c][:, ROWS + y : ROWS + y + 1])
            here = jnp.concatenate([here, here], 1)
            there = jnp.concatenate([there, there], 1)
            state[c] = (state[c] + left * (here + flip * there)) * ratio
            z_ref[y, c] = state[c]
    upper = [edges[16 + c * 8 : 24 + c * 8] for c in range(2)]
    flat = [ref.reshape(16 * PITCH, 128) for ref in (o_lo, o_hi)]
    group, half = 8, ROWS // 2
    copies = []

    def store(base, product):
        for i in range(2 * group):
            rows = pl.ds(i % 2 * PITCH + base + group - 1 - i // 2, 8, stride=2 * PITCH)
            flat[0][rows, :] = product[i * 8 : i * 8 + 8, :128]
            flat[1][rows, :] = product[i * 8 : i * 8 + 8, 128:]
        if base % half == 0:
            for side, ref in enumerate((o_lo, o_hi)):
                copies.append(
                    pltpu.make_async_copy(
                        ref.at[:, pl.ds(base, half), :],
                        out_hbm.at[:, pl.ds(base, half), pl.ds(side * 128, 128)],
                        sems.at[len(copies)],
                    )
                )
                copies[-1].start()

    behind = None
    for base in range(ROWS - group, -1, -group):
        lines = []
        for y in range(base + group - 1, base - 1, -1):
            for c in range(2):
                if y:
                    upper[c] = z_ref[y, c] + local_ref[y] * upper[c]
                    here = wide(columns[c][:, y : y + 1])
                    here = jnp.concatenate([here, here], 1)
                    lines.append(jnp.where(zero_lane, here, upper[c] + solved_ref[y, c]))
                else:
                    lines.append(edges[c * 8 : c * 8 + 8])
        product = short_dot(jnp.concatenate(lines, 0), sine)
        if behind:
            store(*behind)
        behind = (base, product)
    store(*behind)
    for copy in copies:
        copy.wait()


def call(kernel, outs, scratch, *operands, scalars=(), far=(), manual=(), space=pltpu.VMEM):
    places = [pltpu.SMEM if i in scalars else space for i in range(len(operands))]
    if space == pltpu.HBM:
        operands = [pltpu.with_memory_space_constraint(a, space) for a in operands]
    return pl.pallas_call(
        kernel,
        out_shape=[(pltpu.HBM if i in far else pltpu.VMEM)(s, F32) for i, s in enumerate(outs)],
        in_specs=[pl.BlockSpec(memory_space=place) for place in places],
        out_specs=[pl.BlockSpec(memory_space=pltpu.HBM if i in manual else pltpu.VMEM) for i in range(len(outs))],
        scratch_shapes=[pltpu.VMEM(s, F32) if isinstance(s, tuple) else s for s in scratch],
        compiler_params=pltpu.CompilerParams(vmem_limit_bytes=VMEM_LIMIT),
    )(*operands)


def per_device(rhs, metric, wavenumber):
    sine, edge = jnp.asarray(sine_table()), jnp.asarray(edge_table())
    dft, table = jnp.asarray(dft_table()), jnp.asarray(wave_table())
    full, lines, side, bands = (ROWS, 8, COLS), (ROWS, 2, 8, COLS), (16, PITCH, 128), (BANDS, 8, COLS)
    solved, send, metrics, shift, ratio = call(
        local_kernel,
        [lines, (128, 128), (16, 128), (8, COLS), full],
        [
            (16, 128), (8, COLS), (128, 128), full, lines, side, side, (COLS, COLS), (5, 8, COLS), (8, 128),
            pltpu.SMEM((1024,), F32), pltpu.SMEM((8,), F32),
            pltpu.SemaphoreType.DMA((4,)), pltpu.SemaphoreType.DMA((5,)), pltpu.SemaphoreType.DMA((4,)),
        ],
        rhs.reshape(16, ROWS, COLS), metric, metric.reshape(8, 128), wavenumber, sine, edge,
        space=pltpu.HBM, far=range(5), manual=range(5),
    )
    recv = lax.all_to_all(send.reshape(8, 16, 128), "gx", 0, 0, tiled=True)
    (factor,) = call(
        factor_kernel,
        [(3 * ROWS + 2 * BANDS + 4, 8, COLS)],
        [bands] * 6 + [pltpu.SMEM((2048,), F32), (8, COLS), pltpu.SemaphoreType.DMA((2,))],
        metrics.reshape(2048), shift,
        space=pltpu.HBM,
    )
    send, own = call(
        spectrum_kernel,
        [(BANDS, 2, 8, COLS), (5, 8, COLS)],
        [lines],
        recv.reshape(128, 128), factor, dft, table, jnp.asarray(octet_forward()),
    )
    recv = lax.all_to_all(send, "gy", 0, 0, tiled=True)
    (send,) = call(
        separator_kernel,
        [(128, 128)],
        [],
        recv, own, factor, dft, table, jnp.asarray(octet_inverse()),
    )
    recv = lax.all_to_all(send.reshape(8, 16, 128), "gx", 0, 0, tiled=True)
    (out,) = call(
        finish_kernel,
        [(16, ROWS, COLS)],
        [lines, side, side, pltpu.SemaphoreType.DMA((4,))],
        recv.reshape(128, 128), solved, ratio, metric.reshape(8, 128), sine, edge,
        far=(0,), manual=(0,),
    )
    return out.reshape(8, 2, ROWS, COLS)


def solution(mesh):
    placed = (P(None, None, "gy", "gx"), P(), P())
    return jax.shard_map(
        per_device, mesh=mesh, in_specs=placed, out_specs=P(None, None, "gy", "gx"), check_vma=False
    )
```

```python
import functools
import math

import jax
import jax.numpy as jnp
import numpy as np
from jax import lax
from jax.experimental import pallas as pl
from jax.experimental.pallas import tpu as pltpu
from jax.sharding import PartitionSpec as P


ASPECT = 0.02
STRIPS = 8
COLS = 256
ROWS = 64
BANDS = 16
PITCH = ROWS + 8
NX = STRIPS * COLS
VMEM_LIMIT = 16 * 1024 * 1024
F32 = jnp.float32


def f32(values):
    return np.asarray(values, np.float32)


def sine_table():
    ramp = np.arange(COLS)
    table = np.sin(np.pi * (np.outer(ramp, ramp) % (2 * COLS)) / COLS) * math.sqrt(2.0 / COLS)
    table[0, :] = 0.0
    table[:, 0] = 0.0
    table[0, 0] = 1.0
    return f32(table)


def edge_table():
    ramp = np.arange(COLS)
    left = np.sin(np.pi * ramp / COLS) * math.sqrt(2.0 / COLS)
    left[0] = 0.0
    along = 4.0 * np.sin(np.pi * ramp / (2 * COLS)) ** 2
    flip = np.where(ramp % 2 == 1, 1.0, -1.0)
    rows = [ASPECT * left, ASPECT * left * flip, ASPECT * along]
    kappa = np.arange(STRIPS)[:, None]
    whole = ASPECT * (2.0 * np.sin(np.pi * (STRIPS * ramp[None, :] + kappa) / NX)) ** 2
    return f32(np.stack([np.broadcast_to(r, (8, COLS)) for r in rows] + [whole, np.broadcast_to(flip, (8, COLS))]))


def dft_table():
    ramp = np.arange(COLS)
    angle = 2.0 * np.pi * (np.outer(ramp, ramp) % COLS) / COLS
    return f32(np.concatenate([np.cos(angle), np.sin(angle)], 1))


def wave_table():
    kappa = np.arange(STRIPS)[:, None]
    j = np.arange(COLS)[None, :]
    angle = 2.0 * np.pi * j * kappa / NX
    return f32(np.stack([np.cos(angle), np.sin(angle)]))


def octet_forward():
    ramp = np.arange(STRIPS)
    angle = 2.0 * np.pi * np.outer(ramp, ramp) / STRIPS
    c, s = np.cos(angle), np.sin(angle)
    return f32(np.block([[c, s], [-s, c]]))


def octet_inverse():
    ramp = np.arange(STRIPS)
    parts = []
    for offset in (0, 1):
        angle = 2.0 * np.pi * np.outer(ramp + offset, ramp) / STRIPS
        c, s = np.cos(angle), np.sin(angle)
        parts.append(np.block([[c, -s], [s, c]]))
    return f32(np.concatenate(parts, 0) / NX)


def dot(a, b, precision=lax.Precision.HIGHEST):
    return jnp.dot(a, b, precision=precision, preferred_element_type=F32)


def short_dot(a, b):
    return dot(a, b, lax.Precision.HIGH)


def lane_ids():
    return lax.broadcasted_iota(jnp.int32, (8, 128), 1)


def wide(column):
    return jnp.broadcast_to(column, (8, 128))


def row_sum(values):
    return wide(jnp.sum(values[:, :128] + values[:, 128:], axis=1, keepdims=True))


def splat_inverse(metric_ref, row):
    return 1.0 / jnp.full((8, 128), metric_ref[row], F32)


def twice(values):
    return jnp.concatenate([values, values], 1)


def local_shift(wave_ref, edge_ref):
    sub = lax.broadcasted_iota(jnp.int32, (8, COLS), 0)
    shift = edge_ref[2]
    for mode in range(8):
        shift = shift + jnp.where(sub == mode, wave_ref[mode], 0.0)
    return shift


def local_kernel(
    rhs_hbm, metric_hbm, tiled_hbm, wave_hbm, sine_hbm, edge_hbm, solved_hbm, send_hbm, metrics_hbm, shift_hbm, ratio_hbm,
    metrics_ref, shift_ref, send_ref, inverse_ref, ratio_ref, z_ref, r_lo, r_hi, sine_ref, edge_ref, metric_vec, metric_ref, wave_ref, rhs_sem, sems, out_sem,
):
    first = lax.axis_index("gy") * ROWS
    pairs = (
        (metric_hbm, metric_ref), (wave_hbm, wave_ref), (edge_hbm, edge_ref), (tiled_hbm, metric_vec), (sine_hbm, sine_ref)
    )
    small = [pltpu.make_async_copy(a, b, sems.at[i]) for i, (a, b) in enumerate(pairs)]
    half = ROWS // 2
    large = [
        pltpu.make_async_copy(
            rhs_hbm.at[:, pl.ds(part * half, half), pl.ds(side * 128, 128)],
            ref.at[:, pl.ds(part * half, half), :],
            rhs_sem.at[part * 2 + side],
        )
        for part in range(2)
        for side, ref in enumerate((r_lo, r_hi))
    ]
    for copy in small + large:
        copy.start()
    for copy in small[:4]:
        copy.wait()
    metrics_ref[:8, :] = metric_vec[...]
    metrics_ref[8:, :] = 1.0 / metric_vec[...]
    shift = local_shift(wave_ref, edge_ref)
    shift_ref[...] = edge_ref[3] + wave_ref[lax.axis_index("gx")]
    done = [
        pltpu.make_async_copy(metrics_ref, metrics_hbm, sems.at[1]), pltpu.make_async_copy(shift_ref, shift_hbm, sems.at[2])
    ]
    for copy in done:
        copy.start()
    lanes = lane_ids()
    height = jnp.ones((8, COLS), F32)
    slope = jnp.ones((8, COLS), F32)
    for y in range(1, ROWS):
        inverse = splat_inverse(metric_ref, first + y)
        inverse_ref[y] = inverse
        slope = slope + shift * twice(inverse) * height
        taller = height + slope
        ratio_ref[y] = height / taller
        height = taller
    ratio_ref[0] = jnp.ones((8, COLS), F32)
    done.append(pltpu.make_async_copy(ratio_ref, ratio_hbm, sems.at[3]))
    done[-1].start()
    small[4].wait()
    sine = sine_ref[...]
    flat = [ref.reshape(16 * PITCH, 128) for ref in (r_lo, r_hi)]

    def line(y, c):
        rows = pl.ds(c * PITCH + y, 8, stride=2 * PITCH)
        return jnp.concatenate([ref[rows, :] for ref in flat], 1)

    state = [jnp.zeros((8, COLS), F32)] * 2
    group = 8
    for base in range(0, ROWS, group):
        if base % half == 0:
            for copy in large[base // half * 2 : base // half * 2 + 2]:
                copy.wait()
        lines = dot(jnp.concatenate([line(y, c) for y in range(base, base + group) for c in range(2)], 0), sine)
        for y in range(max(base, 1), base + group):
            ratio = ratio_ref[y]
            inverse = twice(inverse_ref[y])
            for c in range(2):
                at = ((y - base) * 2 + c) * 8
                state[c] = (lines[at : at + 8] * inverse + state[c]) * ratio
                z_ref[y, c] = state[c]
    left = edge_ref[0]
    right = edge_ref[1]
    columns = [[jnp.zeros((8, 128), F32)] * 2 for _ in range(2)]
    upper = [jnp.zeros((8, COLS), F32)] * 2
    for y in range(ROWS - 1, 0, -1):
        ratio = ratio_ref[y]
        inverse = inverse_ref[y]
        for c in range(2):
            upper[c] = z_ref[y, c] + ratio * upper[c]
            z_ref[y, c] = upper[c]
            a = upper[c] * left
            source = flat[0][pl.ds(c * PITCH + y, 8, stride=2 * PITCH), :]
            a = (a[:, :128] + a[:, 128:] + jnp.where(lanes == 0, source, 0.0)) * inverse
            b = upper[c] * right
            b = (b[:, :128] + b[:, 128:]) * inverse
            columns[0][c] = jnp.where(lanes == y, wide(jnp.sum(a, axis=1, keepdims=True)), columns[0][c])
            columns[1][c] = jnp.where(lanes == y + ROWS, wide(jnp.sum(b, axis=1, keepdims=True)), columns[1][c])
        if y % 16 == 0:
            done.append(pltpu.make_async_copy(z_ref.at[pl.ds(y, 16)], solved_hbm.at[pl.ds(y, 16)], out_sem.at[y // 16]))
            done[-1].start()
    z_ref[0] = jnp.zeros((2, 8, COLS), F32)
    done.append(pltpu.make_async_copy(z_ref.at[pl.ds(0, 16)], solved_hbm.at[pl.ds(0, 16)], out_sem.at[0]))
    done[-1].start()
    edges = jnp.concatenate([z_ref[y, c] for y in (1, ROWS - 1) for c in range(2)], 0)
    edges = dot(edges, sine)
    zero_lane = lax.broadcasted_iota(jnp.int32, (8, COLS), 1) == 0
    inverse = twice(splat_inverse(metric_ref, first))
    for c in range(2):
        near = jnp.where(zero_lane, 0.0, edges[c * 8 : c * 8 + 8]) + line(0, c) * inverse
        far = jnp.where(zero_lane, 0.0, edges[16 + c * 8 : 24 + c * 8])
        for i in range(2):
            part = slice(i * 128, i * 128 + 128)
            send_ref[pl.ds(c * 2 + i, 8, stride=16), :] = near[:, part]
            send_ref[pl.ds(4 + c * 2 + i, 8, stride=16), :] = far[:, part]
        send_ref[pl.ds(8 + c, 8, stride=16), :] = jnp.where(lanes < ROWS, columns[0][c], columns[1][c])
        for pad in range(3):
            send_ref[pl.ds(10 + c * 3 + pad, 8, stride=16), :] = jnp.zeros((8, 128), F32)
    done.append(pltpu.make_async_copy(send_ref, send_hbm, sems.at[0]))
    done[-1].start()
    for copy in done:
        copy.wait()


def factors(ref):
    sizes = (ROWS, ROWS, ROWS, BANDS, BANDS, 4)
    starts = np.cumsum((0,) + sizes)
    return [ref.at[pl.ds(int(a), n)] for a, n in zip(starts, sizes)]


def factor_kernel(
    metrics_hbm, shift_hbm, factor_ref,
    gamma_ref, base_ref, edge_ref, x_ref, above_ref, inverse_ref, metrics_ref, shift_ref, sems,
):
    copies = [
        pltpu.make_async_copy(metrics_hbm, metrics_ref, sems.at[0]), pltpu.make_async_copy(shift_hbm, shift_ref, sems.at[1])
    ]
    for copy in copies:
        copy.start()
    for copy in copies:
        copy.wait()
    over_ref, under_ref, ratio_ref, up_ref, down_ref, final_ref = factors(factor_ref)
    mine = lax.axis_index("gy")
    shift = shift_ref[...]

    def excess(row):
        double = 2.0 * metrics_ref[row]
        return ((double + shift) - double) * metrics_ref[1024 + row]

    one = jnp.ones((8, COLS), F32)
    zero = jnp.zeros((8, COLS), F32)
    together = 4

    def bands(outer, _):
        state = [(one, one, one, zero)] * together

        def rows(y, state):
            out = []
            for i in range(together):
                height, slope, rest, rise = state[i]
                t = excess((outer * together + i) * ROWS + y)
                slope = slope + t * height
                height = height + slope
                rise = rise + t * rest
                rest = rest + rise
                out.append((height, slope, rest, rise))
            return tuple(out)

        state = lax.fori_loop(1, ROWS, rows, tuple(state), unroll=21)
        for i in range(together):
            height, slope, rest, _ = state[i]
            band = outer * together + i
            gamma = 1.0 / height
            gamma_ref[band] = gamma
            base_ref[band] = excess(band * ROWS) + (rest - 1.0) * gamma
            edge_ref[band] = (slope - 1.0) * gamma
        return 0

    lax.fori_loop(0, BANDS // together, bands, 0)

    flow = one
    above, down, inverse = one, zero, zero
    height, slope = one, one
    rest, rise = one, one
    for y in range(1, ROWS + 1):
        if y < ROWS:
            under_ref[y] = height
            slope = slope + excess(mine * ROWS + y) * height
            taller = height + slope
            ratio_ref[y] = height / taller
            height = taller
            over_ref[ROWS - y] = rest
            rise = rise + excess(mine * ROWS + ROWS - y) * rest
            rest = rest + rise
        if y % 4 == 0:
            band = y // 4 - 1
            x = base_ref[band] + flow
            if band:
                x = x + edge_ref[band - 1]
            x_ref[band] = x
            gamma = gamma_ref[band]
            up = gamma / (gamma + x)
            up_ref[band] = up
            flow = up * x
            band = BANDS - 1 - band
            above_ref[band], down_ref[band], inverse_ref[band] = above, down, inverse
            if band:
                x = base_ref[band] + edge_ref[band - 1] + gamma_ref[band] * above
                below = gamma_ref[band - 1]
                inverse = 1.0 / (below + x)
                down = below * inverse
                above = x * inverse
    gamma = gamma_ref[mine]
    final_ref[0] = down_ref[mine]
    final_ref[1] = inverse_ref[mine]
    final_ref[2] = 1.0 / (x_ref[mine] + gamma * above_ref[mine])
    final_ref[3] = gamma


def spectrum_kernel(
    recv_ref, factor_ref, dft_ref, table_ref, octet_ref, send_ref, own_ref, z_ref
):
    _, _, ratio_ref, up_ref, down_ref, _ = factors(factor_ref)
    mine = lax.axis_index("gy")

    def take(i):
        return recv_ref[pl.ds(i, 8, stride=16), :]

    pieces = [[], []]
    for c in range(2):
        for i in range(2):
            pieces[c].append(take(c * 2 + i))
        for i in range(2):
            pieces[c].append(take(4 + c * 2 + i))
        column = take(8 + c)
        pieces[c].append(column + pltpu.roll(pltpu.roll(column, 1, 0), ROWS, 1))
    stacked = jnp.concatenate([jnp.concatenate(pieces[0], 1), jnp.concatenate(pieces[1], 1)], 0)
    mixed = dot(octet_ref[...], stacked)
    cos, sin = table_ref[0], table_ref[1]
    turned = [[], []]
    for line in range(2):
        re = mixed[:8, line * COLS : line * COLS + COLS]
        im = mixed[8:, line * COLS : line * COLS + COLS]
        turned[0].append(re * cos + im * sin)
        turned[1].append(im * cos - re * sin)
    both = dot(jnp.concatenate(turned[0] + turned[1], 0), dft_ref[...])
    columns = [mixed[c * 8 : c * 8 + 8, 2 * COLS :] for c in range(2)]
    lanes = lane_ids()
    state = [jnp.zeros((8, COLS), F32)] * 2
    for y in range(1, ROWS):
        ratio = ratio_ref[y]
        for c in range(2):
            source = wide(columns[c][:, y : y + 1])
            state[c] = (jnp.concatenate([source, source], 1) + state[c]) * ratio
            z_ref[y, c] = state[c]
    upper = [jnp.zeros((8, COLS), F32)] * 2
    total = [jnp.zeros((8, 128), F32)] * 2
    for y in range(ROWS - 1, 0, -1):
        ratio = ratio_ref[y]
        for c in range(2):
            upper[c] = z_ref[y, c] + ratio * upper[c]
            total[c] = jnp.where(lanes == y, row_sum(upper[c]), total[c])
    sides = []
    for line, extra in enumerate((upper, state)):
        re_cos = both[line * 8 : line * 8 + 8, :COLS]
        re_sin = both[line * 8 : line * 8 + 8, COLS:]
        im_cos = both[16 + line * 8 : 24 + line * 8, :COLS]
        im_sin = both[16 + line * 8 : 24 + line * 8, COLS:]
        sides.append((re_cos + im_sin + extra[0], im_cos - re_sin + extra[1]))
    for c in range(2):
        own_ref[c], own_ref[2 + c] = sides[0][c], sides[1][c]
        send_ref[mine, c] = jnp.zeros((8, COLS), F32)
    own_ref[4] = jnp.concatenate(total, 1)
    up, down = up_ref[mine], down_ref[mine]

    def above(band, carry):
        factor = up_ref[band]
        for c in range(2):
            send_ref[band, c] = carry[c]
        return tuple(value * factor for value in carry)

    def below(step, carry):
        band = mine - 1 - step
        factor = down_ref[band]
        for c in range(2):
            send_ref[band, c] = carry[c]
        return tuple(value * factor for value in carry)

    lax.fori_loop(mine + 1, BANDS, above, tuple(sides[1][c] + up * sides[0][c] for c in range(2)))
    lax.fori_loop(0, mine, below, tuple(sides[0][c] + down * sides[1][c] for c in range(2)))


def separator_kernel(
    recv_ref, own_ref, factor_ref, dft_ref, table_ref, octet_ref, send_ref
):
    over_ref, under_ref, _, _, _, final_ref = factors(factor_ref)
    mine = lax.axis_index("gy")
    from_below = [own_ref[c] for c in range(2)]
    from_above = [own_ref[2 + c] for c in range(2)]
    for band in range(BANDS):
        for c in range(2):
            value = recv_ref[band, c]
            from_below[c] = from_below[c] + jnp.where(band < mine, value, 0.0)
            from_above[c] = from_above[c] + jnp.where(band > mine, value, 0.0)
    down, inverse, pivot = final_ref[0], final_ref[1], final_ref[2]
    near = [(from_below[c] + down * from_above[c]) * pivot for c in range(2)]
    far = [from_above[c] * inverse + down * near[c] for c in range(2)]
    lanes = lane_ids()
    both = short_dot(jnp.concatenate([near[0], far[0], near[1], far[1]], 0), dft_ref[...])
    total = [own_ref[4, :, c * 128 : c * 128 + 128] for c in range(2)]
    gamma = final_ref[3]
    near = [value * gamma for value in near]
    far = [value * gamma for value in far]
    for y in range(1, ROWS):
        over, under = over_ref[y], under_ref[y]
        for c in range(2):
            extra = row_sum(over * near[c] + under * far[c])
            total[c] = total[c] + jnp.where(lanes == y, extra, 0.0)
    cos, sin = table_ref[0], table_ref[1]
    turned = [[], []]
    for line in range(2):
        re_cos = both[line * 8 : line * 8 + 8, :COLS]
        re_sin = both[line * 8 : line * 8 + 8, COLS:]
        im_cos = both[16 + line * 8 : 24 + line * 8, :COLS]
        im_sin = both[16 + line * 8 : 24 + line * 8, COLS:]
        re = re_cos - im_sin
        im = re_sin + im_cos
        turned[0].append(re * cos - im * sin)
        turned[1].append(re * sin + im * cos)
    stacked = [jnp.concatenate(turned[c] + [total[c]], 1) for c in range(2)]
    out = short_dot(octet_ref[...], jnp.concatenate(stacked, 0))
    for c in range(2):
        for i in range(4):
            row = (i // 2) * 4 + c * 2 + i % 2
            send_ref[pl.ds(row, 8, stride=16), :] = out[c * 8 : c * 8 + 8, i * 128 : i * 128 + 128]
        here = out[c * 8 : c * 8 + 8, 2 * COLS :]
        there = out[16 + c * 8 : 24 + c * 8, 2 * COLS :]
        send_ref[pl.ds(8 + c, 8, stride=16), :] = jnp.where(lanes < ROWS, here, pltpu.roll(there, ROWS, 1))
        for pad in range(3):
            send_ref[pl.ds(10 + c * 3 + pad, 8, stride=16), :] = jnp.zeros((8, 128), F32)


def finish_kernel(recv_ref, solved_ref, local_ref, metric_ref, sine_ref, edge_ref, out_hbm, z_ref, o_lo, o_hi, sems):
    band = lax.axis_index("gy")
    lanes = lane_ids()
    metric = jnp.broadcast_to(metric_ref[pl.ds(band // 2, 1), :], (8, 128))
    swapped = pltpu.roll(metric, ROWS, 1)
    metric = jnp.where((lanes < ROWS) == (band % 2 == 0), metric, swapped)
    def take(i):
        return recv_ref[pl.ds(i, 8, stride=16), :]

    sine = sine_ref[...]
    near = [jnp.concatenate([take(c * 2), take(c * 2 + 1)], 1) for c in range(2)]
    far = [jnp.concatenate([take(4 + c * 2), take(5 + c * 2)], 1) for c in range(2)]
    columns = [take(8 + c) for c in range(2)]
    edges = short_dot(jnp.concatenate(near + far, 0), sine)
    scaled = [value / metric for value in columns]
    left, flip = edge_ref[0], edge_ref[4]
    zero_lane = lax.broadcasted_iota(jnp.int32, (8, COLS), 1) == 0
    state = [edges[c * 8 : c * 8 + 8] for c in range(2)]
    for y in range(1, ROWS):
        ratio = local_ref[y]
        for c in range(2):
            here = wide(scaled[c][:, y : y + 1])
            there = wide(scaled[c][:, ROWS + y : ROWS + y + 1])
            here = jnp.concatenate([here, here], 1)
            there = jnp.concatenate([there, there], 1)
            state[c] = (state[c] + left * (here + flip * there)) * ratio
            z_ref[y, c] = state[c]
    upper = [edges[16 + c * 8 : 24 + c * 8] for c in range(2)]
    flat = [ref.reshape(16 * PITCH, 128) for ref in (o_lo, o_hi)]
    group, half = 8, ROWS // 2
    copies = []

    def store(base, product):
        for i in range(2 * group):
            rows = pl.ds(i % 2 * PITCH + base + group - 1 - i // 2, 8, stride=2 * PITCH)
            flat[0][rows, :] = product[i * 8 : i * 8 + 8, :128]
            flat[1][rows, :] = product[i * 8 : i * 8 + 8, 128:]
        if base % half == 0:
            for side, ref in enumerate((o_lo, o_hi)):
                copies.append(
                    pltpu.make_async_copy(
                        ref.at[:, pl.ds(base, half), :],
                        out_hbm.at[:, pl.ds(base, half), pl.ds(side * 128, 128)],
                        sems.at[len(copies)],
                    )
                )
                copies[-1].start()

    behind = None
    for base in range(ROWS - group, -1, -group):
        lines = []
        for y in range(base + group - 1, base - 1, -1):
            for c in range(2):
                if y:
                    upper[c] = z_ref[y, c] + local_ref[y] * upper[c]
                    here = wide(columns[c][:, y : y + 1])
                    here = jnp.concatenate([here, here], 1)
                    lines.append(jnp.where(zero_lane, here, upper[c] + solved_ref[y, c]))
                else:
                    lines.append(edges[c * 8 : c * 8 + 8])
        product = short_dot(jnp.concatenate(lines, 0), sine)
        if behind:
            store(*behind)
        behind = (base, product)
    store(*behind)
    for copy in copies:
        copy.wait()


def call(kernel, outs, scratch, *operands, scalars=(), far=(), manual=(), space=pltpu.VMEM):
    places = [pltpu.SMEM if i in scalars else space for i in range(len(operands))]
    if space == pltpu.HBM:
        operands = [pltpu.with_memory_space_constraint(a, space) for a in operands]
    return pl.pallas_call(
        kernel,
        out_shape=[(pltpu.HBM if i in far else pltpu.VMEM)(s, F32) for i, s in enumerate(outs)],
        in_specs=[pl.BlockSpec(memory_space=place) for place in places],
        out_specs=[pl.BlockSpec(memory_space=pltpu.HBM if i in manual else pltpu.VMEM) for i in range(len(outs))],
        scratch_shapes=[pltpu.VMEM(s, F32) if isinstance(s, tuple) else s for s in scratch],
        compiler_params=pltpu.CompilerParams(vmem_limit_bytes=VMEM_LIMIT),
    )(*operands)


def per_device(rhs, metric, wavenumber):
    sine, edge = jnp.asarray(sine_table()), jnp.asarray(edge_table())
    dft, table = jnp.asarray(dft_table()), jnp.asarray(wave_table())
    full, lines, side, bands = (ROWS, 8, COLS), (ROWS, 2, 8, COLS), (16, PITCH, 128), (BANDS, 8, COLS)
    solved, send, metrics, shift, ratio = call(
        local_kernel,
        [lines, (128, 128), (16, 128), (8, COLS), full],
        [
            (16, 128), (8, COLS), (128, 128), (ROWS, 8, 128), full, lines, side, side, (COLS, COLS), (5, 8, COLS), (8, 128),
            pltpu.SMEM((1024,), F32), pltpu.SMEM((8,), F32),
            pltpu.SemaphoreType.DMA((4,)), pltpu.SemaphoreType.DMA((5,)), pltpu.SemaphoreType.DMA((4,)),
        ],
        rhs.reshape(16, ROWS, COLS), metric, metric.reshape(8, 128), wavenumber, sine, edge,
        space=pltpu.HBM, far=range(5), manual=range(5),
    )
    recv = lax.all_to_all(send.reshape(8, 16, 128), "gx", 0, 0, tiled=True)
    (factor,) = call(
        factor_kernel,
        [(3 * ROWS + 2 * BANDS + 4, 8, COLS)],
        [bands] * 6 + [pltpu.SMEM((2048,), F32), (8, COLS), pltpu.SemaphoreType.DMA((2,))],
        metrics.reshape(2048), shift,
        space=pltpu.HBM,
    )
    send, own = call(
        spectrum_kernel,
        [(BANDS, 2, 8, COLS), (5, 8, COLS)],
        [lines],
        recv.reshape(128, 128), factor, dft, table, jnp.asarray(octet_forward()),
    )
    recv = lax.all_to_all(send, "gy", 0, 0, tiled=True)
    (send,) = call(
        separator_kernel,
        [(128, 128)],
        [],
        recv, own, factor, dft, table, jnp.asarray(octet_inverse()),
    )
    recv = lax.all_to_all(send.reshape(8, 16, 128), "gx", 0, 0, tiled=True)
    (out,) = call(
        finish_kernel,
        [(16, ROWS, COLS)],
        [lines, side, side, pltpu.SemaphoreType.DMA((4,))],
        recv.reshape(128, 128), solved, ratio, metric.reshape(8, 128), sine, edge,
        far=(0,), manual=(0,),
    )
    return out.reshape(8, 2, ROWS, COLS)


def solution(mesh):
    placed = (P(None, None, "gy", "gx"), P(), P())
    return jax.shard_map(
        per_device, mesh=mesh, in_specs=placed, out_specs=P(None, None, "gy", "gx"), check_vma=False
    )
```

```python
import functools
import math

import jax
import jax.numpy as jnp
import numpy as np
from jax import lax
from jax.experimental import pallas as pl
from jax.experimental.pallas import tpu as pltpu
from jax.sharding import PartitionSpec as P


ASPECT = 0.02
STRIPS = 8
COLS = 256
ROWS = 64
BANDS = 16
PITCH = ROWS + 8
NX = STRIPS * COLS
VMEM_LIMIT = 16 * 1024 * 1024
F32 = jnp.float32


def f32(values):
    return np.asarray(values, np.float32)


def sine_table():
    ramp = np.arange(COLS)
    table = np.sin(np.pi * (np.outer(ramp, ramp) % (2 * COLS)) / COLS) * math.sqrt(2.0 / COLS)
    table[0, :] = 0.0
    table[:, 0] = 0.0
    table[0, 0] = 1.0
    return f32(table)


def edge_table():
    ramp = np.arange(COLS)
    left = np.sin(np.pi * ramp / COLS) * math.sqrt(2.0 / COLS)
    left[0] = 0.0
    along = 4.0 * np.sin(np.pi * ramp / (2 * COLS)) ** 2
    flip = np.where(ramp % 2 == 1, 1.0, -1.0)
    rows = [ASPECT * left, ASPECT * left * flip, ASPECT * along]
    kappa = np.arange(STRIPS)[:, None]
    whole = ASPECT * (2.0 * np.sin(np.pi * (STRIPS * ramp[None, :] + kappa) / NX)) ** 2
    return f32(np.stack([np.broadcast_to(r, (8, COLS)) for r in rows] + [whole, np.broadcast_to(flip, (8, COLS))]))


def dft_table():
    ramp = np.arange(COLS)
    angle = 2.0 * np.pi * (np.outer(ramp, ramp) % COLS) / COLS
    return f32(np.concatenate([np.cos(angle), np.sin(angle)], 1))


def wave_table():
    kappa = np.arange(STRIPS)[:, None]
    j = np.arange(COLS)[None, :]
    angle = 2.0 * np.pi * j * kappa / NX
    return f32(np.stack([np.cos(angle), np.sin(angle)]))


def octet_forward():
    ramp = np.arange(STRIPS)
    angle = 2.0 * np.pi * np.outer(ramp, ramp) / STRIPS
    c, s = np.cos(angle), np.sin(angle)
    return f32(np.block([[c, s], [-s, c]]))


def octet_inverse():
    ramp = np.arange(STRIPS)
    parts = []
    for offset in (0, 1):
        angle = 2.0 * np.pi * np.outer(ramp + offset, ramp) / STRIPS
        c, s = np.cos(angle), np.sin(angle)
        parts.append(np.block([[c, -s], [s, c]]))
    return f32(np.concatenate(parts, 0) / NX)


def dot(a, b, precision=lax.Precision.HIGHEST):
    return jnp.dot(a, b, precision=precision, preferred_element_type=F32)


def short_dot(a, b):
    return dot(a, b, lax.Precision.HIGH)


def lane_ids():
    return lax.broadcasted_iota(jnp.int32, (8, 128), 1)


def wide(column):
    return jnp.broadcast_to(column, (8, 128))


def row_sum(values):
    return wide(jnp.sum(values[:, :128] + values[:, 128:], axis=1, keepdims=True))


def splat_inverse(metric_ref, row):
    return 1.0 / jnp.full((8, 128), metric_ref[row], F32)


def twice(values):
    return jnp.concatenate([values, values], 1)


def local_shift(wave_ref, edge_ref):
    sub = lax.broadcasted_iota(jnp.int32, (8, COLS), 0)
    shift = edge_ref[2]
    for mode in range(8):
        shift = shift + jnp.where(sub == mode, wave_ref[mode], 0.0)
    return shift


def local_kernel(
    rhs_hbm, metric_hbm, tiled_hbm, wave_hbm, sine_hbm, edge_hbm, solved_hbm, send_hbm, metrics_hbm, shift_hbm, ratio_hbm,
    metrics_ref, shift_ref, send_ref, inverse_ref, ratio_ref, z_ref, r_lo, r_hi, sine_ref, edge_ref, metric_vec, metric_ref, wave_ref, rhs_sem, sems, out_sem,
):
    first = lax.axis_index("gy") * ROWS
    pairs = (
        (metric_hbm, metric_ref), (wave_hbm, wave_ref), (edge_hbm, edge_ref), (tiled_hbm, metric_vec), (sine_hbm, sine_ref)
    )
    small = [pltpu.make_async_copy(a, b, sems.at[i]) for i, (a, b) in enumerate(pairs)]
    half = ROWS // 2
    large = [
        pltpu.make_async_copy(
            rhs_hbm.at[:, pl.ds(part * half, half), pl.ds(side * 128, 128)],
            ref.at[:, pl.ds(part * half, half), :],
            rhs_sem.at[part * 2 + side],
        )
        for part in range(2)
        for side, ref in enumerate((r_lo, r_hi))
    ]
    for copy in small + large:
        copy.start()
    for copy in small[:4]:
        copy.wait()
    metrics_ref[:8, :] = metric_vec[...]
    metrics_ref[8:, :] = 1.0 / metric_vec[...]
    shift = local_shift(wave_ref, edge_ref)
    shift_ref[...] = edge_ref[3] + wave_ref[lax.axis_index("gx")]
    done = [
        pltpu.make_async_copy(metrics_ref, metrics_hbm, sems.at[1]), pltpu.make_async_copy(shift_ref, shift_hbm, sems.at[2])
    ]
    for copy in done:
        copy.start()
    lanes = lane_ids()
    height = jnp.ones((8, COLS), F32)
    slope = jnp.ones((8, COLS), F32)
    for y in range(1, ROWS):
        inverse = splat_inverse(metric_ref, first + y)
        inverse_ref[y] = inverse
        slope = slope + shift * twice(inverse) * height
        taller = height + slope
        ratio_ref[y] = height / taller
        height = taller
    ratio_ref[0] = jnp.ones((8, COLS), F32)
    done.append(pltpu.make_async_copy(ratio_ref, ratio_hbm, sems.at[3]))
    done[-1].start()
    small[4].wait()
    sine = sine_ref[...]
    flat = [ref.reshape(16 * PITCH, 128) for ref in (r_lo, r_hi)]

    def line(y, c):
        rows = pl.ds(c * PITCH + y, 8, stride=2 * PITCH)
        return jnp.concatenate([ref[rows, :] for ref in flat], 1)

    state = [jnp.zeros((8, COLS), F32)] * 2
    group = 8
    for base in range(0, ROWS, group):
        if base % half == 0:
            for copy in large[base // half * 2 : base // half * 2 + 2]:
                copy.wait()
        lines = dot(jnp.concatenate([line(y, c) for y in range(base, base + group) for c in range(2)], 0), sine)
        for y in range(max(base, 1), base + group):
            ratio = ratio_ref[y]
            inverse = twice(inverse_ref[y])
            for c in range(2):
                at = ((y - base) * 2 + c) * 8
                state[c] = (lines[at : at + 8] * inverse + state[c]) * ratio
                z_ref[y, c] = state[c]
    left = edge_ref[0]
    right = edge_ref[1]
    columns = [[jnp.zeros((8, 128), F32)] * 2 for _ in range(2)]
    upper = [jnp.zeros((8, COLS), F32)] * 2
    for y in range(ROWS - 1, 0, -1):
        ratio = ratio_ref[y]
        inverse = inverse_ref[y]
        for c in range(2):
            upper[c] = z_ref[y, c] + ratio * upper[c]
            z_ref[y, c] = upper[c]
            a = upper[c] * left
            source = flat[0][pl.ds(c * PITCH + y, 8, stride=2 * PITCH), :]
            a = (a[:, :128] + a[:, 128:] + jnp.where(lanes == 0, source, 0.0)) * inverse
            b = upper[c] * right
            b = (b[:, :128] + b[:, 128:]) * inverse
            columns[0][c] = jnp.where(lanes == y, wide(jnp.sum(a, axis=1, keepdims=True)), columns[0][c])
            columns[1][c] = jnp.where(lanes == y + ROWS, wide(jnp.sum(b, axis=1, keepdims=True)), columns[1][c])
        if y % 16 == 0:
            done.append(pltpu.make_async_copy(z_ref.at[pl.ds(y, 16)], solved_hbm.at[pl.ds(y, 16)], out_sem.at[y // 16]))
            done[-1].start()
    z_ref[0] = jnp.zeros((2, 8, COLS), F32)
    done.append(pltpu.make_async_copy(z_ref.at[pl.ds(0, 16)], solved_hbm.at[pl.ds(0, 16)], out_sem.at[0]))
    done[-1].start()
    edges = jnp.concatenate([z_ref[y, c] for y in (1, ROWS - 1) for c in range(2)], 0)
    edges = dot(edges, sine)
    zero_lane = lax.broadcasted_iota(jnp.int32, (8, COLS), 1) == 0
    inverse = twice(splat_inverse(metric_ref, first))
    for c in range(2):
        near = jnp.where(zero_lane, 0.0, edges[c * 8 : c * 8 + 8]) + line(0, c) * inverse
        far = jnp.where(zero_lane, 0.0, edges[16 + c * 8 : 24 + c * 8])
        for i in range(2):
            part = slice(i * 128, i * 128 + 128)
            send_ref[pl.ds(c * 2 + i, 8, stride=16), :] = near[:, part]
            send_ref[pl.ds(4 + c * 2 + i, 8, stride=16), :] = far[:, part]
        send_ref[pl.ds(8 + c, 8, stride=16), :] = jnp.where(lanes < ROWS, columns[0][c], columns[1][c])
        for pad in range(3):
            send_ref[pl.ds(10 + c * 3 + pad, 8, stride=16), :] = jnp.zeros((8, 128), F32)
    done.append(pltpu.make_async_copy(send_ref, send_hbm, sems.at[0]))
    done[-1].start()
    for copy in done:
        copy.wait()


def factors(ref):
    sizes = (ROWS, ROWS, ROWS, BANDS, BANDS, 4)
    starts = np.cumsum((0,) + sizes)
    return [ref.at[pl.ds(int(a), n)] for a, n in zip(starts, sizes)]


def factor_kernel(
    metrics_hbm, shift_hbm, factor_ref,
    gamma_ref, base_ref, edge_ref, x_ref, above_ref, inverse_ref, metrics_ref, shift_ref, sems,
):
    copies = [
        pltpu.make_async_copy(metrics_hbm, metrics_ref, sems.at[0]), pltpu.make_async_copy(shift_hbm, shift_ref, sems.at[1])
    ]
    for copy in copies:
        copy.start()
    for copy in copies:
        copy.wait()
    over_ref, under_ref, ratio_ref, up_ref, down_ref, final_ref = factors(factor_ref)
    mine = lax.axis_index("gy")
    shift = shift_ref[...]

    def excess(row):
        double = 2.0 * metrics_ref[row]
        return ((double + shift) - double) * metrics_ref[1024 + row]

    one = jnp.ones((8, COLS), F32)
    zero = jnp.zeros((8, COLS), F32)
    together = 4

    def bands(outer, _):
        state = [(one, one, one, zero)] * together

        def rows(y, state):
            out = []
            for i in range(together):
                height, slope, rest, rise = state[i]
                t = excess((outer * together + i) * ROWS + y)
                slope = slope + t * height
                height = height + slope
                rise = rise + t * rest
                rest = rest + rise
                out.append((height, slope, rest, rise))
            return tuple(out)

        state = lax.fori_loop(1, ROWS, rows, tuple(state), unroll=21)
        for i in range(together):
            height, slope, rest, _ = state[i]
            band = outer * together + i
            gamma = 1.0 / height
            gamma_ref[band] = gamma
            base_ref[band] = excess(band * ROWS) + (rest - 1.0) * gamma
            edge_ref[band] = (slope - 1.0) * gamma
        return 0

    lax.fori_loop(0, BANDS // together, bands, 0)

    flow = one
    above, down, inverse = one, zero, zero
    height, slope = one, one
    rest, rise = one, one
    for y in range(1, ROWS + 1):
        if y < ROWS:
            under_ref[y] = height
            slope = slope + excess(mine * ROWS + y) * height
            taller = height + slope
            ratio_ref[y] = height / taller
            height = taller
            over_ref[ROWS - y] = rest
            rise = rise + excess(mine * ROWS + ROWS - y) * rest
            rest = rest + rise
        if y % 4 == 0:
            band = y // 4 - 1
            x = base_ref[band] + flow
            if band:
                x = x + edge_ref[band - 1]
            x_ref[band] = x
            gamma = gamma_ref[band]
            up = gamma / (gamma + x)
            up_ref[band] = up
            flow = up * x
            band = BANDS - 1 - band
            above_ref[band], down_ref[band], inverse_ref[band] = above, down, inverse
            if band:
                x = base_ref[band] + edge_ref[band - 1] + gamma_ref[band] * above
                below = gamma_ref[band - 1]
                inverse = 1.0 / (below + x)
                down = below * inverse
                above = x * inverse
    gamma = gamma_ref[mine]
    final_ref[0] = down_ref[mine]
    final_ref[1] = inverse_ref[mine]
    final_ref[2] = 1.0 / (x_ref[mine] + gamma * above_ref[mine])
    final_ref[3] = gamma


def spectrum_kernel(
    recv_ref, factor_ref, dft_ref, table_ref, octet_ref, send_ref, own_ref, z_ref
):
    _, _, ratio_ref, up_ref, down_ref, _ = factors(factor_ref)
    mine = lax.axis_index("gy")

    def take(i):
        return recv_ref[pl.ds(i, 8, stride=16), :]

    pieces = [[], []]
    for c in range(2):
        for i in range(2):
            pieces[c].append(take(c * 2 + i))
        for i in range(2):
            pieces[c].append(take(4 + c * 2 + i))
        column = take(8 + c)
        pieces[c].append(column + pltpu.roll(pltpu.roll(column, 1, 0), ROWS, 1))
    stacked = jnp.concatenate([jnp.concatenate(pieces[0], 1), jnp.concatenate(pieces[1], 1)], 0)
    mixed = dot(octet_ref[...], stacked)
    cos, sin = table_ref[0], table_ref[1]
    turned = [[], []]
    for line in range(2):
        re = mixed[:8, line * COLS : line * COLS + COLS]
        im = mixed[8:, line * COLS : line * COLS + COLS]
        turned[0].append(re * cos + im * sin)
        turned[1].append(im * cos - re * sin)
    both = dot(jnp.concatenate(turned[0] + turned[1], 0), dft_ref[...])
    columns = [mixed[c * 8 : c * 8 + 8, 2 * COLS :] for c in range(2)]
    lanes = lane_ids()
    state = [jnp.zeros((8, COLS), F32)] * 2
    for y in range(1, ROWS):
        ratio = ratio_ref[y]
        for c in range(2):
            source = wide(columns[c][:, y : y + 1])
            state[c] = (jnp.concatenate([source, source], 1) + state[c]) * ratio
            z_ref[y, c] = state[c]
    upper = [jnp.zeros((8, COLS), F32)] * 2
    total = [jnp.zeros((8, 128), F32)] * 2
    for y in range(ROWS - 1, 0, -1):
        ratio = ratio_ref[y]
        for c in range(2):
            upper[c] = z_ref[y, c] + ratio * upper[c]
            total[c] = jnp.where(lanes == y, row_sum(upper[c]), total[c])
    sides = []
    for line, extra in enumerate((upper, state)):
        re_cos = both[line * 8 : line * 8 + 8, :COLS]
        re_sin = both[line * 8 : line * 8 + 8, COLS:]
        im_cos = both[16 + line * 8 : 24 + line * 8, :COLS]
        im_sin = both[16 + line * 8 : 24 + line * 8, COLS:]
        sides.append((re_cos + im_sin + extra[0], im_cos - re_sin + extra[1]))
    for c in range(2):
        own_ref[c], own_ref[2 + c] = sides[0][c], sides[1][c]
    own_ref[4] = jnp.concatenate(total, 1)
    up, down = up_ref[mine], down_ref[mine]
    zero = jnp.zeros((8, COLS), F32)
    first = [sides[1][c] + up * sides[0][c] for c in range(2)]
    last = [sides[0][c] + down * sides[1][c] for c in range(2)]
    above = [zero] * 2
    rows = []
    for band in range(BANDS):
        rows.append(above)
        factor = up_ref[band]
        above = [jnp.where(band == mine, first[c], above[c] * factor) for c in range(2)]
    below = [zero] * 2
    for band in range(BANDS - 1, -1, -1):
        factor = down_ref[band]
        for c in range(2):
            send_ref[band, c] = rows[band][c] + below[c]
        below = [jnp.where(band == mine, last[c], below[c] * factor) for c in range(2)]


def separator_kernel(
    recv_ref, own_ref, factor_ref, dft_ref, table_ref, octet_ref, send_ref
):
    over_ref, under_ref, _, _, _, final_ref = factors(factor_ref)
    mine = lax.axis_index("gy")
    from_below = [own_ref[c] for c in range(2)]
    from_above = [own_ref[2 + c] for c in range(2)]
    for band in range(BANDS):
        for c in range(2):
            value = recv_ref[band, c]
            from_below[c] = from_below[c] + jnp.where(band < mine, value, 0.0)
            from_above[c] = from_above[c] + jnp.where(band > mine, value, 0.0)
    down, inverse, pivot = final_ref[0], final_ref[1], final_ref[2]
    near = [(from_below[c] + down * from_above[c]) * pivot for c in range(2)]
    far = [from_above[c] * inverse + down * near[c] for c in range(2)]
    lanes = lane_ids()
    both = short_dot(jnp.concatenate([near[0], far[0], near[1], far[1]], 0), dft_ref[...])
    total = [own_ref[4, :, c * 128 : c * 128 + 128] for c in range(2)]
    gamma = final_ref[3]
    near = [value * gamma for value in near]
    far = [value * gamma for value in far]
    for y in range(1, ROWS):
        over, under = over_ref[y], under_ref[y]
        for c in range(2):
            extra = row_sum(over * near[c] + under * far[c])
            total[c] = total[c] + jnp.where(lanes == y, extra, 0.0)
    cos, sin = table_ref[0], table_ref[1]
    turned = [[], []]
    for line in range(2):
        re_cos = both[line * 8 : line * 8 + 8, :COLS]
        re_sin = both[line * 8 : line * 8 + 8, COLS:]
        im_cos = both[16 + line * 8 : 24 + line * 8, :COLS]
        im_sin = both[16 + line * 8 : 24 + line * 8, COLS:]
        re = re_cos - im_sin
        im = re_sin + im_cos
        turned[0].append(re * cos - im * sin)
        turned[1].append(re * sin + im * cos)
    stacked = [jnp.concatenate(turned[c] + [total[c]], 1) for c in range(2)]
    out = short_dot(octet_ref[...], jnp.concatenate(stacked, 0))
    for c in range(2):
        for i in range(4):
            row = (i // 2) * 4 + c * 2 + i % 2
            send_ref[pl.ds(row, 8, stride=16), :] = out[c * 8 : c * 8 + 8, i * 128 : i * 128 + 128]
        here = out[c * 8 : c * 8 + 8, 2 * COLS :]
        there = out[16 + c * 8 : 24 + c * 8, 2 * COLS :]
        send_ref[pl.ds(8 + c, 8, stride=16), :] = jnp.where(lanes < ROWS, here, pltpu.roll(there, ROWS, 1))
        for pad in range(3):
            send_ref[pl.ds(10 + c * 3 + pad, 8, stride=16), :] = jnp.zeros((8, 128), F32)


def finish_kernel(recv_ref, solved_ref, local_ref, metric_ref, sine_ref, edge_ref, out_hbm, z_ref, o_lo, o_hi, sems):
    band = lax.axis_index("gy")
    lanes = lane_ids()
    metric = jnp.broadcast_to(metric_ref[pl.ds(band // 2, 1), :], (8, 128))
    swapped = pltpu.roll(metric, ROWS, 1)
    metric = jnp.where((lanes < ROWS) == (band % 2 == 0), metric, swapped)
    def take(i):
        return recv_ref[pl.ds(i, 8, stride=16), :]

    sine = sine_ref[...]
    near = [jnp.concatenate([take(c * 2), take(c * 2 + 1)], 1) for c in range(2)]
    far = [jnp.concatenate([take(4 + c * 2), take(5 + c * 2)], 1) for c in range(2)]
    columns = [take(8 + c) for c in range(2)]
    edges = short_dot(jnp.concatenate(near + far, 0), sine)
    scaled = [value / metric for value in columns]
    left, flip = edge_ref[0], edge_ref[4]
    zero_lane = lax.broadcasted_iota(jnp.int32, (8, COLS), 1) == 0
    state = [edges[c * 8 : c * 8 + 8] for c in range(2)]
    for y in range(1, ROWS):
        ratio = local_ref[y]
        for c in range(2):
            here = wide(scaled[c][:, y : y + 1])
            there = wide(scaled[c][:, ROWS + y : ROWS + y + 1])
            here = jnp.concatenate([here, here], 1)
            there = jnp.concatenate([there, there], 1)
            state[c] = (state[c] + left * (here + flip * there)) * ratio
            z_ref[y, c] = state[c]
    upper = [edges[16 + c * 8 : 24 + c * 8] for c in range(2)]
    flat = [ref.reshape(16 * PITCH, 128) for ref in (o_lo, o_hi)]
    group, half = 8, ROWS // 2
    copies = []

    def store(base, product):
        for i in range(2 * group):
            rows = pl.ds(i % 2 * PITCH + base + group - 1 - i // 2, 8, stride=2 * PITCH)
            flat[0][rows, :] = product[i * 8 : i * 8 + 8, :128]
            flat[1][rows, :] = product[i * 8 : i * 8 + 8, 128:]
        if base % half == 0:
            for side, ref in enumerate((o_lo, o_hi)):
                copies.append(
                    pltpu.make_async_copy(
                        ref.at[:, pl.ds(base, half), :],
                        out_hbm.at[:, pl.ds(base, half), pl.ds(side * 128, 128)],
                        sems.at[len(copies)],
                    )
                )
                copies[-1].start()

    behind = None
    for base in range(ROWS - group, -1, -group):
        lines = []
        for y in range(base + group - 1, base - 1, -1):
            for c in range(2):
                if y:
                    upper[c] = z_ref[y, c] + local_ref[y] * upper[c]
                    here = wide(columns[c][:, y : y + 1])
                    here = jnp.concatenate([here, here], 1)
                    lines.append(jnp.where(zero_lane, here, upper[c] + solved_ref[y, c]))
                else:
                    lines.append(edges[c * 8 : c * 8 + 8])
        product = short_dot(jnp.concatenate(lines, 0), sine)
        if behind:
            store(*behind)
        behind = (base, product)
    store(*behind)
    for copy in copies:
        copy.wait()


def call(kernel, outs, scratch, *operands, scalars=(), far=(), manual=(), space=pltpu.VMEM):
    places = [pltpu.SMEM if i in scalars else space for i in range(len(operands))]
    if space == pltpu.HBM:
        operands = [pltpu.with_memory_space_constraint(a, space) for a in operands]
    return pl.pallas_call(
        kernel,
        out_shape=[(pltpu.HBM if i in far else pltpu.VMEM)(s, F32) for i, s in enumerate(outs)],
        in_specs=[pl.BlockSpec(memory_space=place) for place in places],
        out_specs=[pl.BlockSpec(memory_space=pltpu.HBM if i in manual else pltpu.VMEM) for i in range(len(outs))],
        scratch_shapes=[pltpu.VMEM(s, F32) if isinstance(s, tuple) else s for s in scratch],
        compiler_params=pltpu.CompilerParams(vmem_limit_bytes=VMEM_LIMIT),
    )(*operands)


def per_device(rhs, metric, wavenumber):
    sine, edge = jnp.asarray(sine_table()), jnp.asarray(edge_table())
    dft, table = jnp.asarray(dft_table()), jnp.asarray(wave_table())
    full, lines, side, bands = (ROWS, 8, COLS), (ROWS, 2, 8, COLS), (16, PITCH, 128), (BANDS, 8, COLS)
    solved, send, metrics, shift, ratio = call(
        local_kernel,
        [lines, (128, 128), (16, 128), (8, COLS), full],
        [
            (16, 128), (8, COLS), (128, 128), (ROWS, 8, 128), full, lines, side, side, (COLS, COLS), (5, 8, COLS), (8, 128),
            pltpu.SMEM((1024,), F32), pltpu.SMEM((8,), F32),
            pltpu.SemaphoreType.DMA((4,)), pltpu.SemaphoreType.DMA((5,)), pltpu.SemaphoreType.DMA((4,)),
        ],
        rhs.reshape(16, ROWS, COLS), metric, metric.reshape(8, 128), wavenumber, sine, edge,
        space=pltpu.HBM, far=range(5), manual=range(5),
    )
    recv = lax.all_to_all(send.reshape(8, 16, 128), "gx", 0, 0, tiled=True)
    (factor,) = call(
        factor_kernel,
        [(3 * ROWS + 2 * BANDS + 4, 8, COLS)],
        [bands] * 6 + [pltpu.SMEM((2048,), F32), (8, COLS), pltpu.SemaphoreType.DMA((2,))],
        metrics.reshape(2048), shift,
        space=pltpu.HBM,
    )
    send, own = call(
        spectrum_kernel,
        [(BANDS, 2, 8, COLS), (5, 8, COLS)],
        [lines],
        recv.reshape(128, 128), factor, dft, table, jnp.asarray(octet_forward()),
    )
    recv = lax.all_to_all(send, "gy", 0, 0, tiled=True)
    (send,) = call(
        separator_kernel,
        [(128, 128)],
        [],
        recv, own, factor, dft, table, jnp.asarray(octet_inverse()),
    )
    recv = lax.all_to_all(send.reshape(8, 16, 128), "gx", 0, 0, tiled=True)
    (out,) = call(
        finish_kernel,
        [(16, ROWS, COLS)],
        [lines, side, side, pltpu.SemaphoreType.DMA((4,))],
        recv.reshape(128, 128), solved, ratio, metric.reshape(8, 128), sine, edge,
        far=(0,), manual=(0,),
    )
    return out.reshape(8, 2, ROWS, COLS)


def solution(mesh):
    placed = (P(None, None, "gy", "gx"), P(), P())
    return jax.shard_map(
        per_device, mesh=mesh, in_specs=placed, out_specs=P(None, None, "gy", "gx"), check_vma=False
    )
```

```python
import functools
import math

import jax
import jax.numpy as jnp
import numpy as np
from jax import lax
from jax.experimental import pallas as pl
from jax.experimental.pallas import tpu as pltpu
from jax.sharding import PartitionSpec as P


ASPECT = 0.02
STRIPS = 8
COLS = 256
ROWS = 64
BANDS = 16
PITCH = ROWS + 8
NX = STRIPS * COLS
VMEM_LIMIT = 16 * 1024 * 1024
F32 = jnp.float32


def f32(values):
    return np.asarray(values, np.float32)


def sine_table():
    ramp = np.arange(COLS)
    table = np.sin(np.pi * (np.outer(ramp, ramp) % (2 * COLS)) / COLS) * math.sqrt(2.0 / COLS)
    table[0, :] = 0.0
    table[:, 0] = 0.0
    table[0, 0] = 1.0
    return f32(table)


def edge_table():
    ramp = np.arange(COLS)
    left = np.sin(np.pi * ramp / COLS) * math.sqrt(2.0 / COLS)
    left[0] = 0.0
    along = 4.0 * np.sin(np.pi * ramp / (2 * COLS)) ** 2
    flip = np.where(ramp % 2 == 1, 1.0, -1.0)
    rows = [ASPECT * left, ASPECT * left * flip, ASPECT * along]
    kappa = np.arange(STRIPS)[:, None]
    whole = ASPECT * (2.0 * np.sin(np.pi * (STRIPS * ramp[None, :] + kappa) / NX)) ** 2
    return f32(np.stack([np.broadcast_to(r, (8, COLS)) for r in rows] + [whole, np.broadcast_to(flip, (8, COLS))]))


def dft_table():
    ramp = np.arange(COLS)
    angle = 2.0 * np.pi * (np.outer(ramp, ramp) % COLS) / COLS
    return f32(np.concatenate([np.cos(angle), np.sin(angle)], 1))


def wave_table():
    kappa = np.arange(STRIPS)[:, None]
    j = np.arange(COLS)[None, :]
    angle = 2.0 * np.pi * j * kappa / NX
    return f32(np.stack([np.cos(angle), np.sin(angle)]))


def octet_forward():
    ramp = np.arange(STRIPS)
    angle = 2.0 * np.pi * np.outer(ramp, ramp) / STRIPS
    c, s = np.cos(angle), np.sin(angle)
    return f32(np.block([[c, s], [-s, c]]))


def octet_inverse():
    ramp = np.arange(STRIPS)
    parts = []
    for offset in (0, 1):
        angle = 2.0 * np.pi * np.outer(ramp + offset, ramp) / STRIPS
        c, s = np.cos(angle), np.sin(angle)
        parts.append(np.block([[c, -s], [s, c]]))
    return f32(np.concatenate(parts, 0) / NX)


def dot(a, b, precision=lax.Precision.HIGHEST):
    return jnp.dot(a, b, precision=precision, preferred_element_type=F32)


def short_dot(a, b):
    return dot(a, b, lax.Precision.HIGH)


def lane_ids():
    return lax.broadcasted_iota(jnp.int32, (8, 128), 1)


def wide(column):
    return jnp.broadcast_to(column, (8, 128))


def row_sum(values):
    return wide(jnp.sum(values[:, :128] + values[:, 128:], axis=1, keepdims=True))


def splat_inverse(metric_ref, row):
    return 1.0 / jnp.full((8, 128), metric_ref[row], F32)


def twice(values):
    return jnp.concatenate([values, values], 1)


def local_shift(wave_ref, edge_ref):
    sub = lax.broadcasted_iota(jnp.int32, (8, COLS), 0)
    shift = edge_ref[2]
    for mode in range(8):
        shift = shift + jnp.where(sub == mode, wave_ref[mode], 0.0)
    return shift


def local_kernel(
    rhs_hbm, metric_hbm, tiled_hbm, wave_hbm, sine_hbm, edge_hbm, solved_hbm, send_hbm, metrics_hbm, shift_hbm, ratio_hbm,
    metrics_ref, shift_ref, send_ref, inverse_ref, ratio_ref, z_ref, r_lo, r_hi, sine_ref, edge_ref, metric_vec, metric_ref, wave_ref, rhs_sem, sems, out_sem,
):
    first = lax.axis_index("gy") * ROWS
    pairs = (
        (metric_hbm, metric_ref), (wave_hbm, wave_ref), (edge_hbm, edge_ref), (tiled_hbm, metric_vec), (sine_hbm, sine_ref)
    )
    small = [pltpu.make_async_copy(a, b, sems.at[i]) for i, (a, b) in enumerate(pairs)]
    half = ROWS // 2
    large = [
        pltpu.make_async_copy(
            rhs_hbm.at[:, pl.ds(part * half, half), pl.ds(side * 128, 128)],
            ref.at[:, pl.ds(part * half, half), :],
            rhs_sem.at[part * 2 + side],
        )
        for part in range(2)
        for side, ref in enumerate((r_lo, r_hi))
    ]
    for copy in small + large:
        copy.start()
    for copy in small[:4]:
        copy.wait()
    metrics_ref[:8, :] = metric_vec[...]
    metrics_ref[8:, :] = 1.0 / metric_vec[...]
    shift = local_shift(wave_ref, edge_ref)
    shift_ref[...] = edge_ref[3] + wave_ref[lax.axis_index("gx")]
    done = [
        pltpu.make_async_copy(metrics_ref, metrics_hbm, sems.at[1]), pltpu.make_async_copy(shift_ref, shift_hbm, sems.at[2])
    ]
    for copy in done:
        copy.start()
    lanes = lane_ids()
    height = jnp.ones((8, COLS), F32)
    slope = jnp.ones((8, COLS), F32)
    for y in range(1, ROWS):
        inverse = splat_inverse(metric_ref, first + y)
        inverse_ref[y] = inverse
        slope = slope + shift * twice(inverse) * height
        taller = height + slope
        ratio_ref[y] = height / taller
        height = taller
    ratio_ref[0] = jnp.ones((8, COLS), F32)
    done.append(pltpu.make_async_copy(ratio_ref, ratio_hbm, sems.at[3]))
    done[-1].start()
    small[4].wait()
    sine = sine_ref[...]
    flat = [ref.reshape(16 * PITCH, 128) for ref in (r_lo, r_hi)]

    def line(y, c):
        rows = pl.ds(c * PITCH + y, 8, stride=2 * PITCH)
        return jnp.concatenate([ref[rows, :] for ref in flat], 1)

    state = [jnp.zeros((8, COLS), F32)] * 2
    group = 8
    for base in range(0, ROWS, group):
        if base % half == 0:
            for copy in large[base // half * 2 : base // half * 2 + 2]:
                copy.wait()
        lines = dot(jnp.concatenate([line(y, c) for y in range(base, base + group) for c in range(2)], 0), sine)
        for y in range(max(base, 1), base + group):
            ratio = ratio_ref[y]
            inverse = twice(inverse_ref[y])
            for c in range(2):
                at = ((y - base) * 2 + c) * 8
                state[c] = (lines[at : at + 8] * inverse + state[c]) * ratio
                z_ref[y, c] = state[c]
    left = edge_ref[0]
    right = edge_ref[1]
    columns = [[jnp.zeros((8, 128), F32)] * 2 for _ in range(2)]
    upper = [jnp.zeros((8, COLS), F32)] * 2
    for y in range(ROWS - 1, 0, -1):
        ratio = ratio_ref[y]
        inverse = inverse_ref[y]
        for c in range(2):
            upper[c] = z_ref[y, c] + ratio * upper[c]
            z_ref[y, c] = upper[c]
            a = upper[c] * left
            source = flat[0][pl.ds(c * PITCH + y, 8, stride=2 * PITCH), :]
            a = (a[:, :128] + a[:, 128:] + jnp.where(lanes == 0, source, 0.0)) * inverse
            b = upper[c] * right
            b = (b[:, :128] + b[:, 128:]) * inverse
            columns[0][c] = jnp.where(lanes == y, wide(jnp.sum(a, axis=1, keepdims=True)), columns[0][c])
            columns[1][c] = jnp.where(lanes == y + ROWS, wide(jnp.sum(b, axis=1, keepdims=True)), columns[1][c])
        if y % 16 == 0:
            done.append(pltpu.make_async_copy(z_ref.at[pl.ds(y, 16)], solved_hbm.at[pl.ds(y, 16)], out_sem.at[y // 16]))
            done[-1].start()
    z_ref[0] = jnp.zeros((2, 8, COLS), F32)
    done.append(pltpu.make_async_copy(z_ref.at[pl.ds(0, 16)], solved_hbm.at[pl.ds(0, 16)], out_sem.at[0]))
    done[-1].start()
    edges = jnp.concatenate([z_ref[y, c] for y in (1, ROWS - 1) for c in range(2)], 0)
    edges = dot(edges, sine)
    zero_lane = lax.broadcasted_iota(jnp.int32, (8, COLS), 1) == 0
    inverse = twice(splat_inverse(metric_ref, first))
    for c in range(2):
        near = jnp.where(zero_lane, 0.0, edges[c * 8 : c * 8 + 8]) + line(0, c) * inverse
        far = jnp.where(zero_lane, 0.0, edges[16 + c * 8 : 24 + c * 8])
        for i in range(2):
            part = slice(i * 128, i * 128 + 128)
            send_ref[pl.ds(c * 2 + i, 8, stride=16), :] = near[:, part]
            send_ref[pl.ds(4 + c * 2 + i, 8, stride=16), :] = far[:, part]
        send_ref[pl.ds(8 + c, 8, stride=16), :] = jnp.where(lanes < ROWS, columns[0][c], columns[1][c])
        for pad in range(3):
            send_ref[pl.ds(10 + c * 3 + pad, 8, stride=16), :] = jnp.zeros((8, 128), F32)
    done.append(pltpu.make_async_copy(send_ref, send_hbm, sems.at[0]))
    done[-1].start()
    for copy in done:
        copy.wait()


def factors(ref):
    sizes = (ROWS, ROWS, ROWS, BANDS, BANDS, 4)
    starts = np.cumsum((0,) + sizes)
    return [ref.at[pl.ds(int(a), n)] for a, n in zip(starts, sizes)]


def factor_kernel(
    metrics_hbm, shift_hbm, factor_ref,
    gamma_ref, base_ref, edge_ref, x_ref, above_ref, inverse_ref, metrics_ref, shift_ref, sems,
):
    copies = [
        pltpu.make_async_copy(metrics_hbm, metrics_ref, sems.at[0]), pltpu.make_async_copy(shift_hbm, shift_ref, sems.at[1])
    ]
    for copy in copies:
        copy.start()
    for copy in copies:
        copy.wait()
    over_ref, under_ref, ratio_ref, up_ref, down_ref, final_ref = factors(factor_ref)
    mine = lax.axis_index("gy")
    shift = shift_ref[...]

    def excess(row):
        double = 2.0 * metrics_ref[row]
        return ((double + shift) - double) * metrics_ref[1024 + row]

    one = jnp.ones((8, COLS), F32)
    zero = jnp.zeros((8, COLS), F32)
    together = 4

    def bands(outer, _):
        state = [(one, one, one, zero)] * together

        def rows(y, state):
            out = []
            for i in range(together):
                height, slope, rest, rise = state[i]
                t = excess((outer * together + i) * ROWS + y)
                slope = slope + t * height
                height = height + slope
                rise = rise + t * rest
                rest = rest + rise
                out.append((height, slope, rest, rise))
            return tuple(out)

        state = lax.fori_loop(1, ROWS, rows, tuple(state), unroll=21)
        for i in range(together):
            height, slope, rest, _ = state[i]
            band = outer * together + i
            gamma = 1.0 / height
            gamma_ref[band] = gamma
            base_ref[band] = excess(band * ROWS) + (rest - 1.0) * gamma
            edge_ref[band] = (slope - 1.0) * gamma
        return 0

    lax.fori_loop(0, BANDS // together, bands, 0)

    flow = one
    above, down, inverse = one, zero, zero
    height, slope = one, one
    rest, rise = one, one
    for y in range(1, ROWS + 1):
        if y < ROWS:
            under_ref[y] = height
            slope = slope + excess(mine * ROWS + y) * height
            taller = height + slope
            ratio_ref[y] = height / taller
            height = taller
            over_ref[ROWS - y] = rest
            rise = rise + excess(mine * ROWS + ROWS - y) * rest
            rest = rest + rise
        if y % 4 == 0:
            band = y // 4 - 1
            x = base_ref[band] + flow
            if band:
                x = x + edge_ref[band - 1]
            x_ref[band] = x
            gamma = gamma_ref[band]
            up = gamma / (gamma + x)
            up_ref[band] = up
            flow = up * x
            band = BANDS - 1 - band
            above_ref[band], down_ref[band], inverse_ref[band] = above, down, inverse
            if band:
                x = base_ref[band] + edge_ref[band - 1] + gamma_ref[band] * above
                below = gamma_ref[band - 1]
                inverse = 1.0 / (below + x)
                down = below * inverse
                above = x * inverse
    gamma = gamma_ref[mine]
    final_ref[0] = down_ref[mine]
    final_ref[1] = inverse_ref[mine]
    final_ref[2] = 1.0 / (x_ref[mine] + gamma * above_ref[mine])
    final_ref[3] = gamma


def spectrum_kernel(
    recv_ref, factor_ref, dft_ref, table_ref, octet_ref, send_ref, own_ref, z_ref
):
    _, _, ratio_ref, up_ref, down_ref, _ = factors(factor_ref)
    mine = lax.axis_index("gy")

    def take(i):
        return recv_ref[pl.ds(i, 8, stride=16), :]

    pieces = [[], []]
    for c in range(2):
        for i in range(2):
            pieces[c].append(take(c * 2 + i))
        for i in range(2):
            pieces[c].append(take(4 + c * 2 + i))
        column = take(8 + c)
        pieces[c].append(column + pltpu.roll(pltpu.roll(column, 1, 0), ROWS, 1))
    stacked = jnp.concatenate([jnp.concatenate(pieces[0], 1), jnp.concatenate(pieces[1], 1)], 0)
    mixed = dot(octet_ref[...], stacked)
    cos, sin = table_ref[0], table_ref[1]
    turned = [[], []]
    for line in range(2):
        re = mixed[:8, line * COLS : line * COLS + COLS]
        im = mixed[8:, line * COLS : line * COLS + COLS]
        turned[0].append(re * cos + im * sin)
        turned[1].append(im * cos - re * sin)
    both = dot(jnp.concatenate(turned[0] + turned[1], 0), dft_ref[...])
    columns = [mixed[c * 8 : c * 8 + 8, 2 * COLS :] for c in range(2)]
    lanes = lane_ids()
    state = [jnp.zeros((8, COLS), F32)] * 2
    for y in range(1, ROWS):
        ratio = ratio_ref[y]
        for c in range(2):
            source = wide(columns[c][:, y : y + 1])
            state[c] = (jnp.concatenate([source, source], 1) + state[c]) * ratio
            z_ref[y, c] = state[c]
    upper = [jnp.zeros((8, COLS), F32)] * 2
    total = [jnp.zeros((8, 128), F32)] * 2
    for y in range(ROWS - 1, 0, -1):
        ratio = ratio_ref[y]
        for c in range(2):
            upper[c] = z_ref[y, c] + ratio * upper[c]
            total[c] = jnp.where(lanes == y, row_sum(upper[c]), total[c])
    sides = []
    for line, extra in enumerate((upper, state)):
        re_cos = both[line * 8 : line * 8 + 8, :COLS]
        re_sin = both[line * 8 : line * 8 + 8, COLS:]
        im_cos = both[16 + line * 8 : 24 + line * 8, :COLS]
        im_sin = both[16 + line * 8 : 24 + line * 8, COLS:]
        sides.append((re_cos + im_sin + extra[0], im_cos - re_sin + extra[1]))
    for c in range(2):
        own_ref[c], own_ref[2 + c] = sides[0][c], sides[1][c]
    own_ref[4] = jnp.concatenate(total, 1)
    up, down = up_ref[mine], down_ref[mine]
    zero = jnp.zeros((8, COLS), F32)
    first = [sides[1][c] + up * sides[0][c] for c in range(2)]
    last = [sides[0][c] + down * sides[1][c] for c in range(2)]
    above = [zero] * 2
    rows = []
    for band in range(BANDS):
        rows.append(above)
        factor = up_ref[band]
        above = [jnp.where(band == mine, first[c], above[c] * factor) for c in range(2)]
    below = [zero] * 2
    for band in range(BANDS - 1, -1, -1):
        factor = down_ref[band]
        for c in range(2):
            send_ref[band, c] = rows[band][c] + below[c]
        below = [jnp.where(band == mine, last[c], below[c] * factor) for c in range(2)]


def separator_kernel(
    recv_ref, own_ref, factor_ref, dft_ref, table_ref, octet_ref, send_ref
):
    over_ref, under_ref, _, _, _, final_ref = factors(factor_ref)
    mine = lax.axis_index("gy")
    from_below = [own_ref[c] for c in range(2)]
    from_above = [own_ref[2 + c] for c in range(2)]
    for band in range(BANDS):
        for c in range(2):
            value = recv_ref[band, c]
            from_below[c] = from_below[c] + jnp.where(band < mine, value, 0.0)
            from_above[c] = from_above[c] + jnp.where(band > mine, value, 0.0)
    down, inverse, pivot = final_ref[0], final_ref[1], final_ref[2]
    near = [(from_below[c] + down * from_above[c]) * pivot for c in range(2)]
    far = [from_above[c] * inverse + down * near[c] for c in range(2)]
    lanes = lane_ids()
    both = short_dot(jnp.concatenate([near[0], far[0], near[1], far[1]], 0), dft_ref[...])
    total = [own_ref[4, :, c * 128 : c * 128 + 128] for c in range(2)]
    gamma = final_ref[3]
    near = [value * gamma for value in near]
    far = [value * gamma for value in far]
    for y in range(1, ROWS):
        over, under = over_ref[y], under_ref[y]
        for c in range(2):
            extra = row_sum(over * near[c] + under * far[c])
            total[c] = total[c] + jnp.where(lanes == y, extra, 0.0)
    cos, sin = table_ref[0], table_ref[1]
    turned = [[], []]
    for line in range(2):
        re_cos = both[line * 8 : line * 8 + 8, :COLS]
        re_sin = both[line * 8 : line * 8 + 8, COLS:]
        im_cos = both[16 + line * 8 : 24 + line * 8, :COLS]
        im_sin = both[16 + line * 8 : 24 + line * 8, COLS:]
        re = re_cos - im_sin
        im = re_sin + im_cos
        turned[0].append(re * cos - im * sin)
        turned[1].append(re * sin + im * cos)
    stacked = [jnp.concatenate(turned[c] + [total[c]], 1) for c in range(2)]
    out = short_dot(octet_ref[...], jnp.concatenate(stacked, 0))
    for c in range(2):
        for i in range(4):
            row = (i // 2) * 4 + c * 2 + i % 2
            send_ref[pl.ds(row, 8, stride=16), :] = out[c * 8 : c * 8 + 8, i * 128 : i * 128 + 128]
        here = out[c * 8 : c * 8 + 8, 2 * COLS :]
        there = out[16 + c * 8 : 24 + c * 8, 2 * COLS :]
        send_ref[pl.ds(8 + c, 8, stride=16), :] = jnp.where(lanes < ROWS, here, pltpu.roll(there, ROWS, 1))
        for pad in range(3):
            send_ref[pl.ds(10 + c * 3 + pad, 8, stride=16), :] = jnp.zeros((8, 128), F32)


def finish_kernel(recv_ref, solved_ref, local_ref, metric_ref, sine_ref, edge_ref, out_hbm, z_ref, o_lo, o_hi, sems):
    band = lax.axis_index("gy")
    lanes = lane_ids()
    metric = jnp.broadcast_to(metric_ref[pl.ds(band // 2, 1), :], (8, 128))
    swapped = pltpu.roll(metric, ROWS, 1)
    metric = jnp.where((lanes < ROWS) == (band % 2 == 0), metric, swapped)
    def take(i):
        return recv_ref[pl.ds(i, 8, stride=16), :]

    sine = sine_ref[...]
    near = [jnp.concatenate([take(c * 2), take(c * 2 + 1)], 1) for c in range(2)]
    far = [jnp.concatenate([take(4 + c * 2), take(5 + c * 2)], 1) for c in range(2)]
    columns = [take(8 + c) for c in range(2)]
    edges = short_dot(jnp.concatenate(near + far, 0), sine)
    scaled = [value / metric for value in columns]
    left, flip = edge_ref[0], edge_ref[4]
    zero_lane = lax.broadcasted_iota(jnp.int32, (8, COLS), 1) == 0
    state = [edges[c * 8 : c * 8 + 8] for c in range(2)]
    for y in range(1, ROWS):
        ratio = local_ref[y]
        for c in range(2):
            here = wide(scaled[c][:, y : y + 1])
            there = wide(scaled[c][:, ROWS + y : ROWS + y + 1])
            here = jnp.concatenate([here, here], 1)
            there = jnp.concatenate([there, there], 1)
            state[c] = (state[c] + left * (here + flip * there)) * ratio
            z_ref[y, c] = state[c]
    upper = [edges[16 + c * 8 : 24 + c * 8] for c in range(2)]
    flat = [ref.reshape(16 * PITCH, 128) for ref in (o_lo, o_hi)]
    group, half = 16, ROWS // 2
    copies = []

    def store(base, product):
        for i in range(2 * group):
            rows = pl.ds(i % 2 * PITCH + base + group - 1 - i // 2, 8, stride=2 * PITCH)
            flat[0][rows, :] = product[i * 8 : i * 8 + 8, :128]
            flat[1][rows, :] = product[i * 8 : i * 8 + 8, 128:]
        if base % half == 0:
            for side, ref in enumerate((o_lo, o_hi)):
                copies.append(
                    pltpu.make_async_copy(
                        ref.at[:, pl.ds(base, half), :],
                        out_hbm.at[:, pl.ds(base, half), pl.ds(side * 128, 128)],
                        sems.at[len(copies)],
                    )
                )
                copies[-1].start()

    behind = None
    for base in range(ROWS - group, -1, -group):
        lines = []
        for y in range(base + group - 1, base - 1, -1):
            for c in range(2):
                if y:
                    upper[c] = z_ref[y, c] + local_ref[y] * upper[c]
                    here = wide(columns[c][:, y : y + 1])
                    here = jnp.concatenate([here, here], 1)
                    lines.append(jnp.where(zero_lane, here, upper[c] + solved_ref[y, c]))
                else:
                    lines.append(edges[c * 8 : c * 8 + 8])
        product = short_dot(jnp.concatenate(lines, 0), sine)
        if behind:
            store(*behind)
        behind = (base, product)
    store(*behind)
    for copy in copies:
        copy.wait()


def call(kernel, outs, scratch, *operands, scalars=(), far=(), manual=(), space=pltpu.VMEM):
    places = [pltpu.SMEM if i in scalars else space for i in range(len(operands))]
    if space == pltpu.HBM:
        operands = [pltpu.with_memory_space_constraint(a, space) for a in operands]
    return pl.pallas_call(
        kernel,
        out_shape=[(pltpu.HBM if i in far else pltpu.VMEM)(s, F32) for i, s in enumerate(outs)],
        in_specs=[pl.BlockSpec(memory_space=place) for place in places],
        out_specs=[pl.BlockSpec(memory_space=pltpu.HBM if i in manual else pltpu.VMEM) for i in range(len(outs))],
        scratch_shapes=[pltpu.VMEM(s, F32) if isinstance(s, tuple) else s for s in scratch],
        compiler_params=pltpu.CompilerParams(vmem_limit_bytes=VMEM_LIMIT),
    )(*operands)


def per_device(rhs, metric, wavenumber):
    sine, edge = jnp.asarray(sine_table()), jnp.asarray(edge_table())
    dft, table = jnp.asarray(dft_table()), jnp.asarray(wave_table())
    full, lines, side, bands = (ROWS, 8, COLS), (ROWS, 2, 8, COLS), (16, PITCH, 128), (BANDS, 8, COLS)
    solved, send, metrics, shift, ratio = call(
        local_kernel,
        [lines, (128, 128), (16, 128), (8, COLS), full],
        [
            (16, 128), (8, COLS), (128, 128), (ROWS, 8, 128), full, lines, side, side, (COLS, COLS), (5, 8, COLS), (8, 128),
            pltpu.SMEM((1024,), F32), pltpu.SMEM((8,), F32),
            pltpu.SemaphoreType.DMA((4,)), pltpu.SemaphoreType.DMA((5,)), pltpu.SemaphoreType.DMA((4,)),
        ],
        rhs.reshape(16, ROWS, COLS), metric, metric.reshape(8, 128), wavenumber, sine, edge,
        space=pltpu.HBM, far=range(5), manual=range(5),
    )
    recv = lax.all_to_all(send.reshape(8, 16, 128), "gx", 0, 0, tiled=True)
    (factor,) = call(
        factor_kernel,
        [(3 * ROWS + 2 * BANDS + 4, 8, COLS)],
        [bands] * 6 + [pltpu.SMEM((2048,), F32), (8, COLS), pltpu.SemaphoreType.DMA((2,))],
        metrics.reshape(2048), shift,
        space=pltpu.HBM,
    )
    send, own = call(
        spectrum_kernel,
        [(BANDS, 2, 8, COLS), (5, 8, COLS)],
        [lines],
        recv.reshape(128, 128), factor, dft, table, jnp.asarray(octet_forward()),
    )
    recv = lax.all_to_all(send, "gy", 0, 0, tiled=True)
    (send,) = call(
        separator_kernel,
        [(128, 128)],
        [],
        recv, own, factor, dft, table, jnp.asarray(octet_inverse()),
    )
    recv = lax.all_to_all(send.reshape(8, 16, 128), "gx", 0, 0, tiled=True)
    (out,) = call(
        finish_kernel,
        [(16, ROWS, COLS)],
        [lines, side, side, pltpu.SemaphoreType.DMA((4,))],
        recv.reshape(128, 128), solved, ratio, metric.reshape(8, 128), sine, edge,
        far=(0,), manual=(0,),
    )
    return out.reshape(8, 2, ROWS, COLS)


def solution(mesh):
    placed = (P(None, None, "gy", "gx"), P(), P())
    return jax.shard_map(
        per_device, mesh=mesh, in_specs=placed, out_specs=P(None, None, "gy", "gx"), check_vma=False
    )
```
